32 devices in a mesh: ctx: 8 (over y, x, core), exp: 4 (over z).
Axes of the slice: x: 2, y: 2, z: 4, core: 2. Of those that a mesh axis runs over, the one named last changes fastest.
Arguments:
- tokens: bfloat16 [4, 1024, 2048], P('exp', 'ctx'), may hold values from -6 to 6
- expert_ids: int32 [4, 1024, 8], P('exp', 'ctx'), may hold values from 0 to 31, all different within a row; in each aligned block of 128 rows (0 to 127, 128 to 255, ..., all dimensions but the last counted through in order) at most 48 rows name the same one
- cotangent: bfloat16 [4, 1024, 2048], P('exp', 'ctx'), may hold values from -6 to 6
- attn_gain: bfloat16 [2048], P(('ctx', 'exp')), may hold values from 0.5 to 1.5
- ffn_gain: bfloat16 [2048], P(('ctx', 'exp')), may hold values from 0.5 to 1.5
- query_gain: bfloat16 [128], P(('ctx', 'exp')), may hold values from 0.099609375 to 1.8984375
- key_gain: bfloat16 [128], P(('ctx', 'exp')), may hold values from 0.099609375 to 1.8984375
- query_weight: bfloat16 [2048, 4096], P(('ctx', 'exp')), may hold values from -0.125 to 0.125
- key_weight: bfloat16 [2048, 512], P(('ctx', 'exp')), may hold values from -0.125 to 0.125
- value_weight: bfloat16 [2048, 512], P(('ctx', 'exp')), may hold values from -0.125 to 0.125
- output_weight: bfloat16 [4096, 2048], P(('ctx', 'exp')), may hold values from -1.5 to 1.5
- router_weight: bfloat16 [2048, 32], P(('ctx', 'exp')), may hold values from -0.0625 to 0.0625
- gate_weight: bfloat16 [32, 2048, 768], P(('ctx', 'exp')), may hold values from -0.125 to 0.125
- up_weight: bfloat16 [32, 2048, 768], P(('ctx', 'exp')), may hold values from -0.125 to 0.125
- down_weight: bfloat16 [32, 768, 2048], P(('ctx', 'exp')), may hold values from -0.875 to 0.875
Outputs:
- layer_out: bfloat16 [4, 1024, 2048], P('exp', 'ctx')
- grad_tokens: float32 [4, 1024, 2048], P('exp', 'ctx')
- grad_attn_gain: float32 [2048], P(('ctx', 'exp'))
- grad_ffn_gain: float32 [2048], P(('ctx', 'exp'))
- grad_query_gain: float32 [128], P(('ctx', 'exp'))
- grad_key_gain: float32 [128], P(('ctx', 'exp'))
- grad_query: float32 [2048, 4096], P(('ctx', 'exp'))
- grad_key: float32 [2048, 512], P(('ctx', 'exp'))
- grad_value: float32 [2048, 512], P(('ctx', 'exp'))
- grad_output: float32 [4096, 2048], P(('ctx', 'exp'))
- grad_router: float32 [2048, 32], P(('ctx', 'exp'))
- grad_gate: float32 [32, 2048, 768], P(('ctx', 'exp'))
- grad_up: float32 [32, 2048, 768], P(('ctx', 'exp'))
- grad_down: float32 [32, 768, 2048], P(('ctx', 'exp'))
The draws below stay inside these ranges and needn't reach their ends.
Inputs may be any that keep to these rules, and one draw needn't show every extreme that they name: `expert_ids`: each row names 8 different experts. Among the 128 rows of one device no expert is named more than 48 times, and in every draw some expert is named exactly 48 times in some device's rows.
All inputs are finite; a program needn't handle non-finite values.
Results may differ from the reference program's by a relative error of at most 0.03.
Values may be sent and summed in bfloat16 or wider, within the bound.
No kernel may reach another device: no remote copies, remote signals or barrier semaphores. Data moves between devices by JAX's collectives and lax.ppermute only.
A program may use at most 256 MiB of HBM per device.

```python
import math
import jax
import jax.numpy as jnp
import numpy as np
from jax import lax

D = 2048
H = 32
KVH = 4
HD = 128
FF = 768
TOP = 8
BLK = 256
TOK_DEV = 128
EXPERTS = 32
CAP = 48
BATCH = 4
SEQ = 1024


def steps_of(rng, extent, cuts, smallest, largest):
    factor_of = 1.0
    for axis_at, shards_of in cuts:
        heights = jax.random.uniform(jax.random.fold_in(jax.random.fold_in(rng, 6), axis_at), (shards_of,), jnp.float32, smallest / len(cuts), largest / len(cuts))
        factor_of = factor_of * jnp.repeat(jnp.exp(heights), extent[axis_at] // shards_of).reshape((-1,) + (1,) * (len(extent) - 1 - axis_at))
    return factor_of


def routed_block(stream_key, own, number, rows, count, top, bound, skew):
    order = jax.random.permutation(stream_key, count)
    heavy_load, common = portions_of(count, rows * top, bound, skew, True), portions_of(count, rows * top, bound, skew, False)
    places = jnp.arange(count)

    def named(tallies, rotation):
        used = int((tallies > 0).sum())
        fixed = max(1, used // 4)
        passed = fixed + (places - fixed + rotation * (used - fixed)) % max(1, count - fixed)
        return jnp.zeros((count,), jnp.int32).at[order[jnp.where(places < fixed, places, passed)]].set(jnp.asarray(tallies, jnp.int32))

    tallies = jnp.where(number % 4 == 0, named(heavy_load, number // 4), named(common, number - number // 4 - 1))
    mixed = jax.random.permutation(jax.random.fold_in(own, 3), count)
    giver, taker = mixed[0:count // 2 * 2:2], mixed[1:count // 2 * 2:2]
    margin = jnp.minimum(tallies[giver] - 1, bound - tallies[taker]) // 2
    margin = jnp.where((giver == order[0]) | (taker == order[0]) | (tallies[taker] == 0), 0, jnp.maximum(margin, 0))
    passed = jax.random.randint(jax.random.fold_in(own, 4), (count // 2,), 0, 1 << 20) % (margin + 1)
    tallies = tallies.at[giver].add(-passed).at[taker].add(passed)
    items = jnp.searchsorted(jnp.cumsum(tallies), jnp.arange(rows * top), side="right").astype(jnp.int32)
    listing = items.reshape(top, rows).T
    listing = listing[jax.random.permutation(jax.random.fold_in(own, 1), rows)]
    rotation = jax.random.randint(jax.random.fold_in(own, 2), (rows, 1), 0, top)
    return jnp.take_along_axis(listing, (jnp.arange(top)[None, :] + rotation) % top, axis=1)


def portions_of(count, total, limit, slope, full):
    loads = [(1 << 20) // math.isqrt(standing ** slope) + 1 for standing in range(1, count + 1)]
    largest = limit if full else min(limit, max(-(-total // count), total * loads[0] // sum(loads)))
    least = 1 if total - largest >= count - 1 else 0
    holding, spare = [largest] + [least] * (count - 1), total - largest - least * (count - 1)
    while spare > 0:
        candidates = [i for i in range(1, count) if holding[i] < largest] or [i for i in range(1, count) if holding[i] < limit]
        whole, budget = sum([loads[i] for i in candidates]), spare
        for i in candidates:
            extra = min(limit - holding[i], max(1, budget * loads[i] // whole), spare)
            holding[i] = holding[i] + extra
            spare = spare - extra
    return np.array(holding)


def normal_values(key, extent, width, most, split=(), kind=jnp.bfloat16):
    gain = steps_of(key, extent, split, -0.22, 0.18) if split else 1.0
    entries = jax.random.normal(key, extent, jnp.float32) * width * gain
    return jnp.minimum(jnp.maximum(entries, -most), most).astype(kind)


def setup_inputs(seed: int = 0) -> dict:
    key_of = jax.random.split(jax.random.key(seed), 16)
    tokens = normal_values(key_of[0], (BATCH, SEQ, D), 1.0, 6.0, ((0, 4), (1, 8)))
    expert_ids_keys = jax.random.split(jax.random.fold_in(key_of[1], 1), BATCH * SEQ // TOK_DEV)
    expert_ids_turns = jax.random.permutation(jax.random.fold_in(key_of[1], 3), BATCH * SEQ // TOK_DEV)
    expert_ids = jax.vmap(lambda own, number: routed_block(jax.random.fold_in(key_of[1], 2), own, number, TOK_DEV, EXPERTS, TOP, CAP, 1))(expert_ids_keys, expert_ids_turns).reshape((BATCH, SEQ, TOP))
    cotangent = normal_values(key_of[2], (BATCH, SEQ, D), 1.0, 6.0, ((0, 4), (1, 8)))
    attn_gain = jnp.clip(1.0 + 0.1 * jax.random.normal(key_of[3], (D,), jnp.float32), 0.5, 1.5).astype(jnp.bfloat16)
    ffn_gain = jnp.clip(1.0 + 0.1 * jax.random.normal(key_of[4], (D,), jnp.float32), 0.5, 1.5).astype(jnp.bfloat16)
    query_gain = jnp.clip(1.0 + 0.18 * jax.random.normal(key_of[5], (HD,), jnp.float32), 0.099609375, 1.8984375).astype(jnp.bfloat16)
    key_gain = jnp.clip(1.0 + 0.18 * jax.random.normal(key_of[6], (HD,), jnp.float32), 0.099609375, 1.8984375).astype(jnp.bfloat16)
    query_weight = normal_values(key_of[7], (D, H * HD), D ** -0.5, 0.125, ((0, 32),))
    key_weight = normal_values(key_of[8], (D, KVH * HD), D ** -0.5, 0.125, ((0, 32),))
    value_weight = normal_values(key_of[9], (D, KVH * HD), D ** -0.5, 0.125, ((0, 32),))
    output_weight = normal_values(key_of[10], (H * HD, D), (max(1, 4 * H * HD // SEQ)) ** -0.5, 1.5, ((0, 32),))
    router_weight = normal_values(key_of[11], (D, EXPERTS), (4 * D) ** -0.5, 0.0625, ((0, 32),))
    gate_weight = normal_values(key_of[12], (EXPERTS, D, FF), D ** -0.5, 0.125, ((0, 32),))
    up_weight = normal_values(key_of[13], (EXPERTS, D, FF), D ** -0.5, 0.125, ((0, 32),))
    down_weight = normal_values(key_of[14], (EXPERTS, FF, D), (FF // 16) ** -0.5, 0.875, ((0, 32),))
    return dict(tokens=tokens, expert_ids=expert_ids, cotangent=cotangent, attn_gain=attn_gain, ffn_gain=ffn_gain, query_gain=query_gain, key_gain=key_gain, query_weight=query_weight, key_weight=key_weight, value_weight=value_weight, output_weight=output_weight, router_weight=router_weight, gate_weight=gate_weight, up_weight=up_weight, down_weight=down_weight)


@jax.custom_vjp
def low(v):
    return lax.optimization_barrier(v.astype(jnp.bfloat16)).astype(jnp.float32)

@jax.custom_vjp
def low_back(v):
    return v

def low_keep(v):
    return (low(v), None)

def low_pass(kept, grad):
    return (grad,)

def back_keep(v):
    return (v, None)

def back_low(kept, grad):
    return (low(grad),)
low.defvjp(low_keep, low_pass)
low_back.defvjp(back_keep, back_low)
EPSILON = 1e-06
ROPE_BASE = 1000000.0
HIGHEST = lax.Precision.HIGHEST

def norm_gain(values, gain_vec):
    inverse = lax.rsqrt(lax.optimization_barrier(jnp.mean(values * values, axis=-1, keepdims=True)) + EPSILON)
    return values * inverse * gain_vec

def rotary(values, positions):
    half_dim = values.shape[-1] // 2
    exponent = jnp.arange(half_dim).astype(jnp.float32) * (-2.0 / values.shape[-1])
    frequency = jnp.power(ROPE_BASE, exponent)
    angles = positions.astype(jnp.float32)[:, None] * frequency[None, :]
    cosine = jnp.cos(angles)[:, None, :]
    sine_vals = jnp.sin(angles)[:, None, :]
    first_half = values[..., :half_dim]
    second_half = values[..., half_dim:]
    return jnp.concatenate([first_half * cosine - second_half * sine_vals, second_half * cosine + first_half * sine_vals], axis=-1)

def silu_product(gate_act, up_act):
    return gate_act * jax.nn.sigmoid(gate_act) * up_act

def attend_block(query_block, query_pos, keys_seq, values_seq):
    block_rows = query_block.shape[0]
    groups = H // KVH
    grouped = query_block.reshape(block_rows, KVH, groups, HD)
    scores = jnp.einsum('rkgd,skd->kgrs', grouped, keys_seq, precision=HIGHEST) * HD ** (-0.5)
    scores = low_back(scores)
    key_pos = jnp.arange(keys_seq.shape[0]).astype(jnp.int32)
    allowed = (key_pos // BLK)[None, :] <= (query_pos // BLK)[:, None]
    scores = jnp.where(allowed[None, None], scores, -1e+30)
    highest = lax.optimization_barrier(jnp.max(scores, axis=-1, keepdims=True))
    raised = jnp.exp(scores - highest)
    probs = low(raised / lax.optimization_barrier(jnp.sum(raised, axis=-1, keepdims=True)))
    mixed = jnp.einsum('kgrs,skd->rkgd', probs, values_seq, precision=HIGHEST)
    return mixed.reshape(block_rows, H * HD)

def reference(tokens, expert_ids, cotangent, attn_gain, ffn_gain, query_gain, key_gain, query_weight, key_weight, value_weight, output_weight, router_weight, gate_weight, up_weight, down_weight):
    tokens_count = BATCH * SEQ
    blocks_count = tokens_count // TOK_DEV
    slots_per = blocks_count * CAP
    flat_ids = expert_ids.reshape(tokens_count, TOP).astype(jnp.int32)
    selector_int = (flat_ids[:, :, None] == jnp.arange(EXPERTS).astype(jnp.int32)[None, None, :]).astype(jnp.int32)
    per_block = selector_int.reshape(blocks_count, TOK_DEV * TOP, EXPERTS)
    earlier = jnp.cumsum(per_block, axis=1) - per_block
    rank_rows = lax.optimization_barrier(jnp.sum(earlier * per_block, axis=-1)).reshape(-1).astype(jnp.int32)
    block_of = (jnp.arange(tokens_count * TOP) // (TOK_DEV * TOP)).astype(jnp.int32)
    slot_index = (flat_ids.reshape(-1) * slots_per + block_of * CAP + rank_rows).astype(jnp.int32)
    selector = selector_int.astype(jnp.float32)
    positions = jnp.arange(SEQ).astype(jnp.int32)
    block_rows = math.gcd(SEQ, 512)
    blocks_per = SEQ // block_rows
    seq_of_block = (jnp.arange(BATCH * blocks_per) // blocks_per).astype(jnp.int32)
    start_of_block = (jnp.arange(BATCH * blocks_per) % blocks_per * block_rows).astype(jnp.int32)

    def layer(tokens_in, gain_attn, gain_ffn, gain_query, gain_key, w_query, w_key, w_value, w_output, w_router, w_gate, w_up, w_down):
        normed = low(norm_gain(tokens_in, gain_attn))
        query_raw = low_back(jnp.einsum('bsd,df->bsf', normed, w_query, precision=HIGHEST))
        key_raw = low_back(jnp.einsum('bsd,df->bsf', normed, w_key, precision=HIGHEST))
        value_all = low_back(low(jnp.einsum('bsd,df->bsf', normed, w_value, precision=HIGHEST))).reshape(BATCH, SEQ, KVH, HD)
        query_all = low(rotary(norm_gain(query_raw.reshape(BATCH, SEQ, H, HD), gain_query), positions))
        key_all = low(rotary(norm_gain(key_raw.reshape(BATCH, SEQ, KVH, HD), gain_key), positions))
        query_blocks = query_all.reshape(BATCH * blocks_per, block_rows, H, HD)

        def one_block(items):
            query_block, seq_id, start_row = items
            keys_seq = lax.dynamic_index_in_dim(key_all, seq_id, 0, keepdims=False)
            values_seq = lax.dynamic_index_in_dim(value_all, seq_id, 0, keepdims=False)
            query_pos = start_row + jnp.arange(block_rows).astype(jnp.int32)
            return attend_block(query_block, query_pos, keys_seq, values_seq)
        mixed = lax.map(jax.checkpoint(one_block), (query_blocks, seq_of_block, start_of_block))
        attn_out = low_back(low(mixed.reshape(BATCH, SEQ, H * HD)))
        residual = tokens_in + low_back(jnp.einsum('bsf,fd->bsd', attn_out, w_output, precision=HIGHEST))
        ffn_in = low(norm_gain(residual, gain_ffn)).reshape(tokens_count, D)
        logits = low_back(jnp.dot(ffn_in, w_router, precision=HIGHEST))
        picked_logits = lax.optimization_barrier(jnp.sum(selector * logits[:, None, :], axis=-1))
        highest = lax.optimization_barrier(jnp.max(picked_logits, axis=-1, keepdims=True))
        raised = jnp.exp(picked_logits - highest)
        gate_probs = raised / lax.optimization_barrier(jnp.sum(raised, axis=-1, keepdims=True))
        copies = low_back(jnp.repeat(ffn_in, TOP, axis=0))
        buffer = jnp.zeros((EXPERTS * slots_per, D), jnp.float32).at[slot_index].set(copies)

        def expert_rows(items):
            rows_in, gate_one, up_one, down_one = items
            gate_act = low_back(jnp.dot(rows_in, gate_one, precision=HIGHEST))
            up_act = low_back(jnp.dot(rows_in, up_one, precision=HIGHEST))
            hidden = low(silu_product(gate_act, up_act))
            return low_back(low(jnp.dot(hidden, down_one, precision=HIGHEST)))
        expert_out = lax.map(jax.checkpoint(expert_rows), (buffer.reshape(EXPERTS, slots_per, D), w_gate, w_up, w_down))
        expert_out = expert_out.reshape(EXPERTS * slots_per, D)
        picked = expert_out[slot_index].reshape(tokens_count, TOP, D)
        mixture = lax.optimization_barrier(jnp.sum(gate_probs[..., None] * picked, axis=1))
        return residual + mixture.reshape(BATCH, SEQ, D)
    params = tuple((member.astype(jnp.float32) for member in (tokens, attn_gain, ffn_gain, query_gain, key_gain, query_weight, key_weight, value_weight, output_weight, router_weight, gate_weight, up_weight, down_weight)))
    result, pullback = jax.vjp(layer, *params)
    grads = pullback(cotangent.astype(jnp.float32))
    return (result.astype(jnp.bfloat16), grads[0], grads[1], grads[2], grads[3], grads[4], grads[5], grads[6], grads[7], grads[8], grads[9], grads[10], grads[11], grads[12])
```

```python
import jax
import jax.numpy as jnp
import numpy as np
from jax import lax
from jax.experimental import pallas as pl
from jax.experimental.pallas import tpu as pltpu
from jax.sharding import PartitionSpec as P

D = 2048
H = 32
KVH = 4
HD = 128
TOP = 8
BLK = 256

EPSILON = 1e-06
ROPE_BASE = 1000000.0
SCALE = HD**-0.5
BF = jnp.bfloat16
F32 = jnp.float32
VMEM_LIMIT = 48 * 1024 * 1024


def rope_tables(rows):
    half = HD // 2
    freq = np.power(ROPE_BASE, np.arange(half) * (-2.0 / HD))
    angles = np.arange(rows)[:, None] * freq[None, :]
    cos, sin = np.cos(angles), np.sin(angles)
    return (
        np.concatenate([cos, cos], axis=1).astype(np.float32),
        np.concatenate([-sin, sin], axis=1).astype(np.float32),
    )


def inv_rms(values):
    return lax.rsqrt(jnp.mean(values * values, axis=-1, keepdims=True) + EPSILON)


def nt_dot(a, b):
    return lax.dot_general(a, b, (((1,), (1,)), ((), ())), preferred_element_type=F32)


def tn_dot(a, b):
    return lax.dot_general(a, b, (((0,), (0,)), ((), ())), preferred_element_type=F32)


def mm(a, b):
    return jnp.dot(a, b, preferred_element_type=F32)


def spin(values, cos, sin):
    return values * cos + pltpu.roll(values, HD // 2, 1) * sin


def unspin(values, cos, sin):
    return values * cos - pltpu.roll(values, HD // 2, 1) * sin


def attn_forward_kernel(blocks, raw, kraw, vraw, cos_all, sin_all, cos, sin, qgain, kgain, out, keys, vals):
    head, block = pl.program_id(0), pl.program_id(1)

    @pl.when((head == 0) & (block == 0))
    def _():
        rows = kraw[...]
        keys[...] = spin(rows * inv_rms(rows) * kgain[...], cos_all[...], sin_all[...]).astype(BF)
        vals[...] = vraw[...].astype(BF)

    rows = raw[...]
    query = spin(rows * inv_rms(rows) * qgain[...], cos[...], sin[...]).astype(BF)
    for n in range(blocks):

        @pl.when(block == n)
        def _(n=n):
            span = (n + 1) * BLK
            weights = jnp.exp(nt_dot(query, keys[:span, :]) * SCALE)
            total = jnp.sum(weights, axis=-1, keepdims=True)
            probs = (weights * (1.0 / total)).astype(BF)
            out[...] = mm(probs, vals[:span, :]).astype(BF)


def attn_backward_kernel(
    blocks, raw, kraw, vraw, cos_all, sin_all, cos, sin, qgain, kgain, gout,
    gq, gk, gv, gqgain, keys, vals,
):
    head, block = pl.program_id(0), pl.program_id(1)

    @pl.when((head == 0) & (block == 0))
    def _():
        rows = kraw[...]
        keys[...] = spin(rows * inv_rms(rows) * kgain[...], cos_all[...], sin_all[...]).astype(BF)
        vals[...] = vraw[...].astype(BF)
        gk[...] = jnp.zeros_like(gk)
        gv[...] = jnp.zeros_like(gv)
        gqgain[...] = jnp.zeros_like(gqgain)

    rows = raw[...]
    inverse = inv_rms(rows)
    normed = rows * inverse
    query = spin(normed * qgain[...], cos[...], sin[...]).astype(BF)
    grad_out = gout[...]

    def finish(grad_query):
        turned = unspin(grad_query, cos[...], sin[...])
        gqgain[...] += jnp.sum(turned * normed, axis=0, keepdims=True)
        scaled = turned * qgain[...]
        mean = jnp.mean(scaled * normed, axis=-1, keepdims=True)
        gq[...] = (inverse * (scaled - normed * mean)).astype(BF)

    for n in range(blocks):

        @pl.when(block == n)
        def _(n=n):
            span = (n + 1) * BLK
            seen, values = keys[:span, :], vals[:span, :]
            weights = jnp.exp(nt_dot(query, seen) * SCALE)
            total = jnp.sum(weights, axis=-1, keepdims=True)
            probs = weights * (1.0 / total)
            grad_probs = nt_dot(grad_out, values)
            delta = jnp.sum(probs * grad_probs, axis=-1, keepdims=True)
            grad_scores = (probs * (grad_probs - delta)).astype(BF)
            gv[:span, :] += tn_dot(probs.astype(BF), grad_out)
            gk[:span, :] += tn_dot(grad_scores, query) * SCALE
            finish(mm(grad_scores, seen) * SCALE)


def key_backward_kernel(count, kraw, cos, sin, kgain, *rest):
    gks, gvs, (gk_low, gv_low, gkgain) = rest[:count], rest[count : 2 * count], rest[2 * count :]
    grad_keys, grad_vals = gks[0][...], gvs[0][...]
    for n in range(1, count):
        grad_keys = grad_keys + gks[n][...]
        grad_vals = grad_vals + gvs[n][...]
    rows = kraw[...]
    inverse = inv_rms(rows)
    normed = rows * inverse
    turned = unspin(grad_keys, cos[...], sin[...])
    gkgain[...] = jnp.sum(turned * normed, axis=0, keepdims=True)
    scaled = turned * kgain[...]
    mean = jnp.mean(scaled * normed, axis=-1, keepdims=True)
    gk_low[...] = (inverse * (scaled - normed * mean)).astype(BF)
    gv_low[...] = grad_vals.astype(BF)


def attn_specs(rows, heads):
    return [
        pl.BlockSpec((BLK, HD), lambda h, i: (i, h)),
        pl.BlockSpec((rows, HD), lambda h, i: (0, 0)),
        pl.BlockSpec((rows, HD), lambda h, i: (0, 0)),
        pl.BlockSpec((rows, HD), lambda h, i: (0, 0)),
        pl.BlockSpec((rows, HD), lambda h, i: (0, 0)),
        pl.BlockSpec((BLK, HD), lambda h, i: (i, 0)),
        pl.BlockSpec((BLK, HD), lambda h, i: (i, 0)),
        pl.BlockSpec((1, HD), lambda h, i: (0, 0)),
        pl.BlockSpec((1, HD), lambda h, i: (0, 0)),
    ]


def attn_forward(raw, kraw, vraw, cos, sin, qgain, kgain, heads):
    rows = raw.shape[0]
    blocks = rows // BLK
    return pl.pallas_call(
        lambda *refs: attn_forward_kernel(blocks, *refs),
        grid=(heads, blocks),
        in_specs=attn_specs(rows, heads),
        out_specs=pl.BlockSpec((BLK, HD), lambda h, i: (i, h)),
        out_shape=jax.ShapeDtypeStruct((rows, heads * HD), BF),
        scratch_shapes=[pltpu.VMEM((rows, HD), BF), pltpu.VMEM((rows, HD), BF)],
        compiler_params=pltpu.CompilerParams(vmem_limit_bytes=VMEM_LIMIT),
        name="attn_fw",
    )(raw, kraw, vraw, cos, sin, cos, sin, qgain, kgain)


def attn_backward(raw, kraw, vraw, cos, sin, qgain, kgain, gout, heads):
    rows = raw.shape[0]
    blocks = rows // BLK
    return pl.pallas_call(
        lambda *refs: attn_backward_kernel(blocks, *refs),
        grid=(heads, blocks),
        in_specs=attn_specs(rows, heads) + [pl.BlockSpec((BLK, HD), lambda h, i: (i, h))],
        out_specs=[
            pl.BlockSpec((BLK, HD), lambda h, i: (i, h)),
            pl.BlockSpec((rows, HD), lambda h, i: (0, 0)),
            pl.BlockSpec((rows, HD), lambda h, i: (0, 0)),
            pl.BlockSpec((1, HD), lambda h, i: (0, 0)),
        ],
        out_shape=[
            jax.ShapeDtypeStruct((rows, heads * HD), BF),
            jax.ShapeDtypeStruct((rows, HD), F32),
            jax.ShapeDtypeStruct((rows, HD), F32),
            jax.ShapeDtypeStruct((1, HD), F32),
        ],
        scratch_shapes=[pltpu.VMEM((rows, HD), BF), pltpu.VMEM((rows, HD), BF)],
        compiler_params=pltpu.CompilerParams(vmem_limit_bytes=VMEM_LIMIT),
        name="attn_bw",
    )(raw, kraw, vraw, cos, sin, cos, sin, qgain, kgain, gout)


def key_backward(kraw, cos, sin, kgain, gks, gvs):
    rows = kraw.shape[0]
    return pl.pallas_call(
        lambda *refs: key_backward_kernel(len(gks), *refs),
        out_shape=[
            jax.ShapeDtypeStruct((rows, HD), BF),
            jax.ShapeDtypeStruct((rows, HD), BF),
            jax.ShapeDtypeStruct((1, HD), F32),
        ],
        compiler_params=pltpu.CompilerParams(vmem_limit_bytes=VMEM_LIMIT),
        name="key_bw",
    )(kraw, cos, sin, kgain, *gks, *gvs)


def on_device(
    tokens,
    expert_ids,
    cotangent,
    attn_gain,
    ffn_gain,
    query_gain,
    key_gain,
    query_weight,
    key_weight,
    value_weight,
    output_weight,
    router_weight,
    gate_weight,
    up_weight,
    down_weight,
):
    both = ("ctx", "exp")
    nc, ne = lax.axis_size("ctx"), lax.axis_size("exp")
    ci, ei = lax.axis_index("ctx"), lax.axis_index("exp")
    count = nc * ne
    rows = tokens.shape[1]
    seq = rows * nc
    heads = H // nc
    width = heads * HD
    share = nc // KVH
    piece = 2 * HD // share
    member = ci % share
    experts = router_weight.shape[1]
    cap = max(2, rows * TOP * 3 // (2 * experts))
    slots = nc * cap
    wrows = query_weight.shape[0]
    gain_rows, head_rows = attn_gain.shape[0], query_gain.shape[0]

    def mate(values, bit):
        return lax.ppermute(values, "ctx", [(i, i ^ bit) for i in range(nc)])

    def along(values):
        return lax.ppermute(values, "exp", [(i, (i + 1) % ne) for i in range(ne)])

    def spread(values):
        return lax.all_to_all(values, "ctx", split_axis=0, concat_axis=0, tiled=True)

    packed = jnp.concatenate(
        [
            attn_gain,
            ffn_gain,
            query_gain,
            key_gain,
            router_weight.reshape(-1),
            expert_ids.astype(BF).reshape(-1),
        ]
    )
    table = lax.all_gather(packed, both, axis=0, tiled=False)
    cuts = np.cumsum([gain_rows, gain_rows, head_rows, head_rows, wrows * experts]).tolist()
    gain_attn = table[:, : cuts[0]].reshape(1, D).astype(F32)
    gain_ffn = table[:, cuts[0] : cuts[1]].reshape(1, D).astype(F32)
    gain_query = table[:, cuts[1] : cuts[2]].reshape(1, HD).astype(F32)
    gain_key = table[:, cuts[2] : cuts[3]].reshape(1, HD).astype(F32)
    router = table[:, cuts[3] : cuts[4]].reshape(D, experts)
    ids_ctx = lax.dynamic_slice_in_dim(
        table[:, cuts[4] :].reshape(nc, ne, rows, TOP), ci, 1, 0
    )[0].astype(jnp.int32)

    own_tokens = tokens[0]
    x_all = lax.all_gather(own_tokens, "ctx", axis=0, tiled=True)
    kv = jnp.concatenate(
        [key_weight.reshape(wrows, KVH, HD), value_weight.reshape(wrows, KVH, HD)], axis=2
    ).reshape(wrows, nc, piece)
    part = jnp.concatenate([query_weight.reshape(wrows, nc, width), kv], axis=2)
    part = spread(part.transpose(1, 0, 2))
    w_in = (
        lax.all_gather(part, "exp", axis=0, tiled=False)
        .transpose(1, 0, 2, 3)
        .reshape(D, width + piece)
    )
    w_out = lax.all_gather(output_weight, "exp", axis=0, tiled=True)

    plane_ids = lax.iota(jnp.int32, nc) * ne + ei
    lower = (
        lax.broadcasted_iota(jnp.int32, (rows, rows), 0)
        > lax.broadcasted_iota(jnp.int32, (rows, rows), 1)
    ).astype(BF)
    picks = []
    for step in range(ne):
        ids = lax.dynamic_index_in_dim(ids_ctx, (ei - step) % ne, 0, keepdims=False)
        named = jnp.any(ids[:, :, None] == plane_ids[None, None, :], axis=1)
        rank = mm(lower, named.astype(BF)).astype(jnp.int32)
        place = jnp.where(named, rank, -1).T
        picks.append(
            (place[:, None, :] == lax.iota(jnp.int32, cap)[None, :, None])
            .astype(BF)
            .reshape(slots, rows)
        )

    def ring(values):
        chain = [values]
        for _ in range(1, ne):
            chain.append(along(chain[-1]))
        return chain

    def dispatch(step, values):
        return spread(mm(picks[step], values).astype(BF).reshape(nc, cap, D)).reshape(slots, D)

    cot_rows = [dispatch(step, values) for step, values in enumerate(ring(cotangent[0]))]

    cos, sin = (jnp.asarray(v) for v in rope_tables(seq))
    x_f32 = x_all.astype(F32)
    xa = (x_f32 * inv_rms(x_f32) * gain_attn).astype(BF)
    raw = mm(xa, w_in)
    q_raw = raw[:, :width]
    kv_own = raw[:, width:]
    kv_parts = [kv_own] + [mate(kv_own, bit) for bit in range(1, share)]
    ordered = []
    for spot in range(share):
        chosen = kv_parts[spot]
        for m in range(1, share):
            chosen = jnp.where(member == m, kv_parts[spot ^ m], chosen)
        ordered.append(chosen)
    kv_raw = jnp.concatenate(ordered, axis=1) if share > 1 else ordered[0]
    k_raw, v_raw = kv_raw[:, :HD], kv_raw[:, HD:]
    attn = attn_forward(q_raw, k_raw, v_raw, cos, sin, gain_query, gain_key, heads)
    branch = mm(attn, w_out).astype(BF)
    inputs = own_tokens.astype(F32)
    residual = inputs + lax.psum_scatter(
        branch, "ctx", scatter_dimension=0, tiled=True
    ).astype(F32)
    inv_res = inv_rms(residual)
    normed_res = residual * inv_res
    ffn_in = (normed_res * gain_ffn).astype(BF)

    def gates_of(values, ids):
        logits = mm(values, router)
        chosen = jnp.any(ids[:, :, None] == lax.iota(jnp.int32, experts)[None, None, :], axis=1)
        top = jnp.max(jnp.where(chosen, logits, -jnp.inf), axis=-1, keepdims=True)
        raised = jnp.where(chosen, jnp.exp(jnp.where(chosen, logits - top, 0.0)), 0.0)
        return raised / jnp.sum(raised, axis=-1, keepdims=True)

    w_gate, w_up, w_down = gate_weight[0], up_weight[0], down_weight[0]
    ffn_chain = ring(ffn_in)
    gates_home = None
    gate_sends = []
    for step, values in enumerate(ffn_chain):
        ids = lax.dynamic_index_in_dim(ids_ctx, (ei - step) % ne, 0, keepdims=False)
        gates = gates_of(values, ids)
        if step == 0:
            gates_home = gates
        plane = lax.dynamic_index_in_dim(gates.reshape(rows, nc, ne), ei, 2, keepdims=False)
        gate_sends.append(
            jnp.sum(
                picks[step].reshape(nc, cap, rows).astype(F32) * plane.T[:, None, :], axis=-1
            )
        )
    ffn_rows = [dispatch(step, values) for step, values in enumerate(ffn_chain)]
    gate_rows = spread(jnp.stack(gate_sends, axis=1))

    hidden_g, act_gate, act_up, back_rows, mix_rows, score_rows = [], [], [], [], [], []
    for step in range(ne):
        gate_vec = gate_rows[:, step].reshape(slots, 1)
        gate_act = mm(ffn_rows[step], w_gate)
        up_act = mm(ffn_rows[step], w_up)
        sig = jax.nn.sigmoid(gate_act)
        silu = gate_act * sig
        hidden = silu * up_act
        hidden_low = hidden.astype(BF)
        upstream = nt_dot(cot_rows[step], w_down)
        score_rows.append(jnp.sum(upstream * hidden_low.astype(F32), axis=-1).reshape(nc, cap))
        grad_hidden = upstream * gate_vec
        grad_gate_low = (grad_hidden * up_act * sig * (1.0 + gate_act * (1.0 - sig))).astype(BF)
        grad_up_low = (grad_hidden * silu).astype(BF)
        back_rows.append((nt_dot(grad_gate_low, w_gate) + nt_dot(grad_up_low, w_up)).astype(BF))
        mix_rows.append((mm(hidden_low, w_down) * gate_vec).astype(BF))
        hidden_g.append((hidden_low.astype(F32) * gate_vec).astype(BF))
        act_gate.append(grad_gate_low)
        act_up.append(grad_up_low)

    score_back = spread(jnp.stack(score_rows, axis=1))
    order = list(range(1, ne)) + [0]

    def collect(chunks):
        total = None
        for step in order:
            home = spread(chunks[step].reshape(nc, cap, D)).reshape(slots, D)
            part_sum = tn_dot(picks[step], home)
            total = part_sum if total is None else part_sum + along(total.astype(BF)).astype(F32)
        return total

    grad_ffn_experts = collect(back_rows)
    mixture = collect(mix_rows)
    layer_out = (residual + mixture).astype(BF)[None]

    def tokens_of(step):
        return jnp.sum(
            picks[step].reshape(nc, cap, rows).astype(F32)
            * score_back[:, step].reshape(nc, cap, 1),
            axis=1,
        )

    scores = [tokens_of(step) for step in range(ne)]
    planes = [scores[0]]
    for step in range(1, ne):
        planes.append(
            lax.ppermute(scores[step], "exp", [(i, (i - step) % ne) for i in range(ne)])
        )
    grad_gates = jnp.zeros((ne, nc, rows), F32)
    for step in range(ne):
        grad_gates = lax.dynamic_update_slice_in_dim(
            grad_gates, planes[step][None], (ei + step) % ne, 0
        )
    grad_gates = grad_gates.transpose(2, 1, 0).reshape(rows, experts)
    grad_logits = gates_home * (
        grad_gates - jnp.sum(gates_home * grad_gates, axis=-1, keepdims=True)
    )
    grad_logits_low = grad_logits.astype(BF)
    grad_router = tn_dot(ffn_in, grad_logits_low)
    grad_ffn_in = grad_ffn_experts + nt_dot(grad_logits_low, router)
    grad_gain_ffn = jnp.sum(grad_ffn_in * normed_res, axis=0)
    scaled = grad_ffn_in * gain_ffn
    grad_residual = cotangent[0].astype(F32) + inv_res * (
        scaled - normed_res * jnp.mean(scaled * normed_res, axis=-1, keepdims=True)
    )

    grad_branch = lax.all_gather(grad_residual.astype(BF), "ctx", axis=0, tiled=True)
    grad_attn = nt_dot(grad_branch, w_out).astype(BF)
    grad_q_low, grad_k, grad_v, grad_gain_query = attn_backward(
        q_raw, k_raw, v_raw, cos, sin, gain_query, gain_key, grad_attn, heads
    )
    gks = [grad_k] + [mate(grad_k, bit) for bit in range(1, share)]
    gvs = [grad_v] + [mate(grad_v, bit) for bit in range(1, share)]
    grad_k_low, grad_v_low, grad_gain_key = key_backward(k_raw, cos, sin, gain_key, gks, gvs)
    grad_gain_key = jnp.where(member == 0, grad_gain_key, 0.0)
    grad_kv = jnp.concatenate([grad_k_low, grad_v_low], axis=1)
    if share > 1:
        grad_kv = lax.dynamic_slice_in_dim(grad_kv, member * piece, piece, 1)
    grad_in = jnp.concatenate([grad_q_low, grad_kv], axis=1)
    grad_xa = lax.psum_scatter(
        nt_dot(grad_in, w_in).astype(BF), "ctx", scatter_dimension=0, tiled=True
    ).astype(F32)
    inv_in = inv_rms(inputs)
    normed_in = inputs * inv_in
    scaled_in = grad_xa * gain_attn
    grad_tokens = (
        grad_residual
        + inv_in
        * (scaled_in - normed_in * jnp.mean(scaled_in * normed_in, axis=-1, keepdims=True))
    )[None]

    all_rows = jnp.concatenate(ffn_rows)
    grad_gate = tn_dot(all_rows, jnp.concatenate(act_gate))
    grad_up = tn_dot(all_rows, jnp.concatenate(act_up))
    grad_down = tn_dot(jnp.concatenate(hidden_g), jnp.concatenate(cot_rows))

    grad_output = lax.psum_scatter(
        tn_dot(attn, grad_branch).astype(BF), "exp", scatter_dimension=0, tiled=True
    ).astype(F32)
    grad_w = tn_dot(xa, grad_in).astype(BF).reshape(nc, ne, wrows, width + piece)
    grad_w = lax.psum_scatter(
        grad_w.transpose(1, 0, 2, 3), "exp", scatter_dimension=0, tiled=True
    )[0]
    grad_w = spread(grad_w).astype(F32)
    sum_query = grad_w[:, :, :width].transpose(1, 0, 2).reshape(wrows, H * HD)
    sum_kv = grad_w[:, :, width:].transpose(1, 0, 2).reshape(wrows, KVH, 2 * HD)
    sum_key = sum_kv[:, :, :HD].reshape(wrows, KVH * HD)
    sum_value = sum_kv[:, :, HD:].reshape(wrows, KVH * HD)
    sum_attn_gain = (
        jnp.sum(sum_query * query_weight.astype(F32), axis=1)
        + jnp.sum(sum_key * key_weight.astype(F32), axis=1)
        + jnp.sum(sum_value * value_weight.astype(F32), axis=1)
    ) / attn_gain.astype(F32)

    small = jnp.concatenate(
        [
            grad_router.reshape(count, wrows * experts),
            grad_gain_ffn.reshape(count, gain_rows),
            grad_gain_query.reshape(count, head_rows),
            grad_gain_key.reshape(count, head_rows),
        ],
        axis=1,
    )
    small = jnp.sum(
        lax.all_to_all(small, both, split_axis=0, concat_axis=0, tiled=True), axis=0
    )
    ends = np.cumsum([wrows * experts, gain_rows, head_rows, head_rows]).tolist()
    return (
        layer_out,
        grad_tokens,
        sum_attn_gain,
        small[ends[0] : ends[1]],
        small[ends[1] : ends[2]],
        small[ends[2] : ends[3]],
        sum_query,
        sum_key,
        sum_value,
        grad_output,
        small[: ends[0]].reshape(wrows, experts),
        grad_gate[None],
        grad_up[None],
        grad_down[None],
    )


def solution(mesh):
    shard = ("ctx", "exp")
    rows = P("exp", "ctx", None)
    vector, matrix, stack = P(shard), P(shard, None), P(shard, None, None)
    return jax.shard_map(
        on_device,
        mesh=mesh,
        in_specs=(rows,) * 3 + (vector,) * 4 + (matrix,) * 5 + (stack,) * 3,
        out_specs=(rows,) * 2 + (vector,) * 4 + (matrix,) * 5 + (stack,) * 3,
        check_vma=False,
    )
```

```python
import jax
import jax.numpy as jnp
import numpy as np
from jax import lax
from jax.experimental import pallas as pl
from jax.experimental.pallas import tpu as pltpu
from jax.sharding import PartitionSpec as P

D = 2048
H = 32
KVH = 4
HD = 128
TOP = 8
BLK = 256

EPSILON = 1e-06
ROPE_BASE = 1000000.0
SCALE = HD**-0.5
BF = jnp.bfloat16
F32 = jnp.float32
MASKED = -1e30
VMEM_LIMIT = 48 * 1024 * 1024
ATTN_LIMIT = 24 * 1024 * 1024
SMALL = pl.CostEstimate(flops=1000, bytes_accessed=1000, transcendentals=0)
TILE = 512


def cost(micros):
    return pl.CostEstimate(flops=int(1.1e9 * micros), bytes_accessed=1000, transcendentals=0)


def rope_tables(rows):
    half = HD // 2
    freq = np.power(ROPE_BASE, np.arange(half) * (-2.0 / HD))
    angles = np.arange(rows)[:, None] * freq[None, :]
    cos, sin = np.cos(angles), np.sin(angles)
    return (
        np.concatenate([cos, cos], axis=1).astype(np.float32),
        np.concatenate([-sin, sin], axis=1).astype(np.float32),
    )


def inv_rms(values):
    return lax.rsqrt(jnp.mean(values * values, axis=-1, keepdims=True) + EPSILON)


def nt_dot(a, b):
    return lax.dot_general(a, b, (((1,), (1,)), ((), ())), preferred_element_type=F32)


def tn_dot(a, b):
    return lax.dot_general(a, b, (((0,), (0,)), ((), ())), preferred_element_type=F32)


def mm(a, b):
    return jnp.dot(a, b, preferred_element_type=F32)


def spin(values, cos, sin):
    return values * cos + pltpu.roll(values, HD // 2, 1) * sin


def unspin(values, cos, sin):
    return values * cos - pltpu.roll(values, HD // 2, 1) * sin


def attn_forward_kernel(blocks, raw, kraw, vraw, cos_all, sin_all, cos, sin, qgain, kgain, out, keys, vals):
    head, block = pl.program_id(0), pl.program_id(1)

    @pl.when((head == 0) & (block == 0))
    def _():
        rows = kraw[...]
        keys[...] = spin(rows * inv_rms(rows) * kgain[...], cos_all[...], sin_all[...]).astype(BF)
        vals[...] = vraw[...].astype(BF)

    rows = raw[...]
    query = spin(rows * inv_rms(rows) * qgain[...], cos[...], sin[...]).astype(BF)
    for n in range(blocks):

        @pl.when(block == n)
        def _(n=n):
            span = (n + 1) * BLK
            weights = jnp.exp(nt_dot(query, keys[:span, :]) * SCALE)
            total = jnp.sum(weights, axis=-1, keepdims=True)
            probs = (weights * (1.0 / total)).astype(BF)
            out[...] = mm(probs, vals[:span, :]).astype(BF)


def attn_backward_kernel(
    blocks, raw, kraw, vraw, cos_all, sin_all, cos, sin, qgain, kgain, gout, *rest
):
    *start, gq, gk, gv, gqgain, keys, vals = rest
    head, block = pl.program_id(0), pl.program_id(1)

    @pl.when((head == 0) & (block == 0))
    def _():
        rows = kraw[...]
        keys[...] = spin(rows * inv_rms(rows) * kgain[...], cos_all[...], sin_all[...]).astype(BF)
        vals[...] = vraw[...].astype(BF)
        for ref, first in zip((gk, gv, gqgain), start or (None,) * 3):
            ref[...] = jnp.zeros_like(ref) if first is None else first[...]

    rows = raw[...]
    inverse = inv_rms(rows)
    normed = rows * inverse
    query = spin(normed * qgain[...], cos[...], sin[...]).astype(BF)
    grad_out = gout[...]

    def finish(grad_query):
        turned = unspin(grad_query, cos[...], sin[...])
        gqgain[...] += jnp.sum(turned * normed, axis=0, keepdims=True)
        scaled = turned * qgain[...]
        mean = jnp.mean(scaled * normed, axis=-1, keepdims=True)
        gq[...] = (inverse * (scaled - normed * mean)).astype(BF)

    for n in range(blocks):

        @pl.when(block == n)
        def _(n=n):
            span = (n + 1) * BLK
            seen, values = keys[:span, :], vals[:span, :]
            weights = jnp.exp(nt_dot(query, seen) * SCALE)
            total = jnp.sum(weights, axis=-1, keepdims=True)
            probs = weights * (1.0 / total)
            grad_probs = nt_dot(grad_out, values)
            delta = jnp.sum(probs * grad_probs, axis=-1, keepdims=True)
            grad_scores = (probs * (grad_probs - delta)).astype(BF)
            gv[:span, :] += tn_dot(probs.astype(BF), grad_out)
            gk[:span, :] += tn_dot(grad_scores, query) * SCALE
            finish(mm(grad_scores, seen) * SCALE)


def key_backward_kernel(count, kraw, cos, sin, kgain, *rest):
    gks, gvs, (gk_low, gv_low, gkgain) = rest[:count], rest[count : 2 * count], rest[2 * count :]
    grad_keys, grad_vals = gks[0][...], gvs[0][...]
    for n in range(1, count):
        grad_keys = grad_keys + gks[n][...]
        grad_vals = grad_vals + gvs[n][...]
    rows = kraw[...]
    inverse = inv_rms(rows)
    normed = rows * inverse
    turned = unspin(grad_keys, cos[...], sin[...])
    gkgain[...] = jnp.sum(turned * normed, axis=0, keepdims=True)
    scaled = turned * kgain[...]
    mean = jnp.mean(scaled * normed, axis=-1, keepdims=True)
    gk_low[...] = (inverse * (scaled - normed * mean)).astype(BF)
    gv_low[...] = grad_vals.astype(BF)


def attn_specs(rows, first=0):
    return [
        pl.BlockSpec((BLK, HD), lambda h, i: (i, h + first)),
        pl.BlockSpec((rows, HD), lambda h, i: (0, 0)),
        pl.BlockSpec((rows, HD), lambda h, i: (0, 0)),
        pl.BlockSpec((rows, HD), lambda h, i: (0, 0)),
        pl.BlockSpec((rows, HD), lambda h, i: (0, 0)),
        pl.BlockSpec((BLK, HD), lambda h, i: (i, 0)),
        pl.BlockSpec((BLK, HD), lambda h, i: (i, 0)),
        pl.BlockSpec((1, HD), lambda h, i: (0, 0)),
        pl.BlockSpec((1, HD), lambda h, i: (0, 0)),
    ]


def attn_forward(raw, kraw, vraw, cos, sin, qgain, kgain, first, heads):
    rows = raw.shape[0]
    blocks = rows // BLK
    return pl.pallas_call(
        lambda *refs: attn_forward_kernel(blocks, *refs),
        grid=(heads, blocks),
        in_specs=attn_specs(rows, first),
        out_specs=pl.BlockSpec((BLK, HD), lambda h, i: (i, h)),
        out_shape=jax.ShapeDtypeStruct((rows, heads * HD), BF),
        scratch_shapes=[pltpu.VMEM((rows, HD), BF), pltpu.VMEM((rows, HD), BF)],
        compiler_params=pltpu.CompilerParams(vmem_limit_bytes=ATTN_LIMIT),
        cost_estimate=cost(7),
        name="attn_fw",
    )(raw, kraw, vraw, cos, sin, cos, sin, qgain, kgain)


def attn_backward(raw, kraw, vraw, cos, sin, qgain, kgain, gout, first, heads, start):
    rows = raw.shape[0]
    blocks = rows // BLK
    return pl.pallas_call(
        lambda *refs: attn_backward_kernel(blocks, *refs),
        grid=(heads, blocks),
        in_specs=attn_specs(rows, first)
        + [pl.BlockSpec((BLK, HD), lambda h, i: (i, h + first))]
        + [pl.BlockSpec(v.shape, lambda h, i: (0, 0)) for v in start],
        out_specs=[
            pl.BlockSpec((BLK, HD), lambda h, i: (i, h)),
            pl.BlockSpec((rows, HD), lambda h, i: (0, 0)),
            pl.BlockSpec((rows, HD), lambda h, i: (0, 0)),
            pl.BlockSpec((1, HD), lambda h, i: (0, 0)),
        ],
        out_shape=[
            jax.ShapeDtypeStruct((rows, heads * HD), BF),
            jax.ShapeDtypeStruct((rows, HD), F32),
            jax.ShapeDtypeStruct((rows, HD), F32),
            jax.ShapeDtypeStruct((1, HD), F32),
        ],
        scratch_shapes=[pltpu.VMEM((rows, HD), BF), pltpu.VMEM((rows, HD), BF)],
        compiler_params=pltpu.CompilerParams(vmem_limit_bytes=ATTN_LIMIT),
        cost_estimate=cost(12),
        name="attn_bw",
    )(raw, kraw, vraw, cos, sin, cos, sin, qgain, kgain, gout, *start)


def key_backward(kraw, cos, sin, kgain, gks, gvs):
    rows = kraw.shape[0]
    return pl.pallas_call(
        lambda *refs: key_backward_kernel(len(gks), *refs),
        out_shape=[
            jax.ShapeDtypeStruct((rows, HD), BF),
            jax.ShapeDtypeStruct((rows, HD), BF),
            jax.ShapeDtypeStruct((1, HD), F32),
        ],
        compiler_params=pltpu.CompilerParams(vmem_limit_bytes=ATTN_LIMIT),
        cost_estimate=cost(2),
        name="key_bw",
    )(kraw, cos, sin, kgain, *gks, *gvs)


def call(kernel, name, out_shape, micros=0, **kw):
    return pl.pallas_call(
        kernel,
        out_shape=out_shape,
        compiler_params=pltpu.CompilerParams(vmem_limit_bytes=VMEM_LIMIT),
        cost_estimate=cost(micros) if micros else SMALL,
        name=name,
        **kw,
    )


def whole(values):
    return pl.BlockSpec(values.shape, lambda *_: (0,) * values.ndim)


def column_tile(height):
    return pl.BlockSpec((height, TILE), lambda j: (0, j))


def routing(ids, place, ne, experts, cap):
    nc, _, rows = ids.shape
    nchip = nc // 2
    block = 2 * cap

    def kernel(at, ids_ref, send, direct, chosen, spots, named):
        chip, core, ci, ei = at[0], at[1], at[2], at[3]
        number = lax.broadcasted_iota(jnp.int32, (experts, rows), 0)
        slot = lax.broadcasted_iota(jnp.int32, (cap, rows), 0).astype(F32)
        lower = (
            lax.broadcasted_iota(jnp.int32, (rows, rows), 0)
            < lax.broadcasted_iota(jnp.int32, (rows, rows), 1)
        ).astype(BF)
        for dev in range(nc):
            got = ids_ref[dev]
            hits = jnp.zeros((experts, rows), F32)
            for k in range(TOP):
                hits = hits + (got[k : k + 1, :] == number).astype(F32)
            named[dev] = hits.astype(BF)
            spots[dev] = jnp.where(hits > 0.5, mm(hits.astype(BF), lower), -1.0)

        def slots_of(dev, expert):
            line = jnp.sum(jnp.where(number == expert, spots[dev], 0.0), axis=0, keepdims=True)
            return (line == slot).astype(BF)

        for m in range(nchip):
            expert = ((chip ^ m) * 2 + core) * ne + ei
            send[m] = jnp.zeros((block, 2 * rows), BF)
            send[m, :cap, :rows] = slots_of(ci, expert)
            send[m, cap:, rows:] = slots_of(ci ^ 1, expert)
            for src in range(2):
                dev = (chip ^ m) * 2 + (core ^ src)
                taken = slots_of(dev, ci * ne + ei)
                first = (m * 2 + src) * cap
                chosen[first : first + cap, :] = nt_dot(taken, named[dev])
        for dev in range(nc):
            direct[dev] = slots_of(ci, dev * ne + ei)

    return pl.pallas_call(
        kernel,
        out_shape=[
            jax.ShapeDtypeStruct((nchip, block, 2 * rows), BF),
            jax.ShapeDtypeStruct((nc, cap, rows), BF),
            jax.ShapeDtypeStruct((nc * cap, experts), F32),
        ],
        in_specs=[pl.BlockSpec(memory_space=pltpu.SMEM), pl.BlockSpec(memory_space=pltpu.VMEM)],
        scratch_shapes=[
            pltpu.VMEM((nc, experts, rows), F32),
            pltpu.VMEM((nc, experts, rows), BF),
        ],
        compiler_params=pltpu.CompilerParams(vmem_limit_bytes=ATTN_LIMIT),
        cost_estimate=SMALL,
        name="routing",
    )(place, ids)


def select_direct(direct, planes, values):
    steps, (nc, cap, rows) = len(direct), direct[0].shape

    def kernel(at, *refs):
        tokens, out = refs[steps], refs[steps + 1]
        for n in range(steps):
            part = tokens[at[n]]
            for dev in range(nc):
                out[dev, n * cap : (n + 1) * cap, :] = mm(refs[n][dev], part).astype(BF)

    return call(
        kernel,
        "select_direct",
        micros=3,
        out_shape=jax.ShapeDtypeStruct((nc, steps * cap, D), BF),
        grid=(D // TILE,),
        in_specs=[pl.BlockSpec(memory_space=pltpu.SMEM)]
        + [whole(v) for v in direct]
        + [pl.BlockSpec((values.shape[0], rows, TILE), lambda j: (0, 0, j))],
        out_specs=pl.BlockSpec((nc, steps * cap, TILE), lambda j: (0, 0, j)),
    )(planes, *direct, values)


def select_rows(send, values, mates):
    nchip, block, _ = send.shape
    rows, count = values[0].shape[0], len(values)

    def kernel(picks, *refs):
        outs = refs[2 * count :]
        for n in range(count):
            pair = jnp.concatenate([refs[n][...], refs[count + n][...]], axis=0)
            for m in range(nchip):
                outs[m][n] = mm(picks[m], pair).astype(BF)

    return call(
        kernel,
        "select_rows",
        micros=3,
        out_shape=[jax.ShapeDtypeStruct((count, block, D), BF)] * nchip,
        grid=(D // TILE,),
        in_specs=[whole(send)] + [column_tile(rows)] * (2 * count),
        out_specs=[pl.BlockSpec((count, block, TILE), lambda j: (0, 0, j))] * nchip,
    )(send, *values, *mates)


def combine_rows(send, home):
    nchip, block, _ = send.shape
    rows, wide = send.shape[2] // 2, home[0].shape[1]

    def kernel(picks, *refs):
        blocks, mine, theirs = refs[:nchip], refs[nchip], refs[nchip + 1]
        got = jnp.concatenate([b[...] for b in blocks], axis=0)
        chosen = jnp.concatenate([picks[m] for m in range(nchip)], axis=0)
        both = tn_dot(chosen, got)
        mine[...] = both[:rows]
        theirs[...] = both[rows:].astype(BF)

    return call(
        kernel,
        "combine_rows",
        micros=3,
        out_shape=[jax.ShapeDtypeStruct((rows, wide), F32), jax.ShapeDtypeStruct((rows, wide), BF)],
    )(send, *home)


def combine_all(send, planes, home):
    ne, (nchip, block, wide) = len(send), send[0].shape
    rows = wide // 2

    def kernel(at, *refs):
        mine, theirs = refs[-2:]
        for step in range(ne):
            blocks = refs[ne + step * nchip : ne + (step + 1) * nchip]
            got = jnp.concatenate([b[...] for b in blocks], axis=0)
            chosen = jnp.concatenate([refs[step][m] for m in range(nchip)], axis=0)
            both = tn_dot(chosen, got).astype(BF)
            mine[at[step]] = both[:rows]
            theirs[at[step]] = both[rows:]

    return call(
        kernel,
        "combine_all",
        micros=6,
        out_shape=[jax.ShapeDtypeStruct((ne, rows, D), BF)] * 2,
        grid=(D // TILE,),
        in_specs=[pl.BlockSpec(memory_space=pltpu.SMEM)]
        + [whole(v) for v in send]
        + [column_tile(block)] * (ne * nchip),
        out_specs=[pl.BlockSpec((ne, rows, TILE), lambda j: (0, 0, j))] * 2,
    )(planes, *send, *(v for blocks in home for v in blocks))


def expert_rows(rows_in, cot_in, devices, row_chosen, router, column, lane, weights):
    nchip, (both, block, _) = len(rows_in), rows_in[0].shape
    nc, cap = 2 * nchip, block // 2
    cots = 0 if both > 1 else nc
    slots, lanes, hidden_size = nchip * block, lane.shape[1], weights[0].shape[1]

    def kernel(_, *refs):
        ffn_in, cot_refs = refs[:nchip], refs[nchip : nchip + cots]
        chosen_ref, router_ref, column_ref, lane_ref, w_gate, w_up, w_down = refs[
            nchip + cots : nchip + cots + 7
        ]
        outs = refs[nchip + cots + 7 :]
        backs, mixes, kept = outs[:nchip], outs[nchip : 2 * nchip], outs[2 * nchip :]
        all_out, hidden_out, gate_out, up_out = kept
        rows = jnp.concatenate([r[0] for r in ffn_in], axis=0)
        cot = jnp.concatenate([r[0] for r in cot_refs] or [r[1] for r in ffn_in], axis=0)
        all_out[...] = rows
        gates = gates_of(mm(rows, router_ref[...]), chosen_ref[...] > 0.5, True)
        gate_vec = jnp.sum(gates * column_ref[...], axis=-1, keepdims=True)
        gate_act = mm(rows, w_gate[...])
        up_act = mm(rows, w_up[...])
        upstream = nt_dot(cot, w_down[...])
        sig = 1.0 / (1.0 + jnp.exp(-gate_act))
        silu = gate_act * sig
        hidden = (silu * up_act).astype(BF).astype(F32)
        score = jnp.sum(upstream * hidden, axis=-1, keepdims=True)
        gated = (hidden * gate_vec).astype(BF)
        hidden_out[...] = gated
        grad_hidden = upstream * gate_vec
        grad_gate = (grad_hidden * up_act * sig * (1.0 + gate_act * (1.0 - sig))).astype(BF)
        grad_up = (grad_hidden * silu).astype(BF)
        gate_out[...] = grad_gate
        up_out[...] = grad_up
        back = (nt_dot(grad_gate, w_gate[...]) + nt_dot(grad_up, w_up[...])).astype(BF)
        scores = (score * lane_ref[...]).astype(BF)
        for m in range(nchip):
            part = slice(m * block, (m + 1) * block)
            backs[m][:, :D] = back[part]
            backs[m][:, D:] = scores[part]
            mixes[m][...] = mm(gated[part], w_down[...]).astype(BF)

    narrow = jax.ShapeDtypeStruct((slots, hidden_size), BF)
    out_shape = [jax.ShapeDtypeStruct((block, D + lanes), BF)] * nchip
    out_shape += [jax.ShapeDtypeStruct((block, D), BF)] * nchip + [
        jax.ShapeDtypeStruct((slots, D), BF),
        narrow,
        narrow,
        narrow,
    ]
    fixed = [row_chosen, router, column, lane, *weights]
    outs = call(
        kernel,
        "expert_rows",
        micros=14,
        out_shape=out_shape,
        grid_spec=pltpu.PrefetchScalarGridSpec(
            num_scalar_prefetch=1,
            grid=(1,),
            in_specs=[whole(r) for r in rows_in]
            + [
                pl.BlockSpec((1, cap, D), lambda i, at, n=n: (at[n], 0, 0))
                for n in range(cots)
            ]
            + [whole(v) for v in fixed],
            out_specs=[whole(v) for v in out_shape],
        ),
    )(devices, *rows_in, *([cot_in] * cots), *fixed)
    return outs[:nchip], outs[nchip : 2 * nchip], outs[2 * nchip :]


def grad_in_weight(rows, grads):
    chunks, slots, size = len(rows), rows[0].shape[0], grads[0].shape[1]

    def kernel(*refs):
        total = tn_dot(refs[0][...], refs[chunks][...])
        for n in range(1, chunks):
            total += tn_dot(refs[n][...], refs[chunks + n][...])
        refs[2 * chunks][...] = total

    return call(
        kernel,
        "grad_in_weight",
        micros=10,
        out_shape=jax.ShapeDtypeStruct((D, size), F32),
        grid=(D // TILE,),
        in_specs=[column_tile(slots)] * chunks + [whole(v) for v in grads],
        out_specs=pl.BlockSpec((TILE, size), lambda i: (i, 0)),
    )(*rows, *grads)


def grad_down_weight(hidden, devices, cot_first, later):
    chunks = len(hidden)
    (nc, cap, _), size = cot_first.shape, hidden[0].shape[1]
    nchip = nc // 2

    def kernel(at, *refs):
        hid, early, late, out = refs[:chunks], refs[chunks], refs[chunks + 1 : -1], refs[-1]
        total = None
        for n in range(chunks):
            if n:
                rows = [r[0] for r in late[(n - 1) * nchip : n * nchip]]
            else:
                rows = [early[at[i]] for i in range(nc)]
            part = tn_dot(hid[n][...], jnp.concatenate(rows, axis=0))
            total = part if total is None else total + part
        out[...] = total

    late = [v for blocks in later for v in blocks]
    return call(
        kernel,
        "grad_down_weight",
        micros=10,
        out_shape=jax.ShapeDtypeStruct((size, D), F32),
        grid=(D // TILE,),
        in_specs=[pl.BlockSpec(memory_space=pltpu.SMEM)]
        + [whole(v) for v in hidden]
        + [pl.BlockSpec((nc, cap, TILE), lambda j: (0, 0, j))]
        + [pl.BlockSpec((1, 2 * cap, TILE), lambda j: (1, 0, j))] * len(late),
        out_specs=column_tile(size),
    )(devices, *hidden, cot_first, *late)


def project(x_all, gain, weight, wrows):
    rows, size = x_all.shape[0], weight.shape[3]

    def kernel(x, gain_ref, w, normed, raw):
        values = x[...].astype(F32)
        low = (values * inv_rms(values) * gain_ref[...]).astype(BF)
        normed[...] = low
        raw[...] = mm(low, w[:, :, :wrows, :].reshape(D, size))

    band = pl.BlockSpec((BLK, D), lambda i: (i, 0))
    return call(
        kernel,
        "project",
        micros=6,
        out_shape=[jax.ShapeDtypeStruct((rows, D), BF), jax.ShapeDtypeStruct((rows, size), F32)],
        grid=(rows // BLK,),
        in_specs=[band, whole(gain), whole(weight)],
        out_specs=[band, pl.BlockSpec((BLK, size), lambda i: (i, 0))],
    )(x_all, gain, weight)


def part_product(values, index, rows, weight, wrows, theirs, dtype):
    size = values.shape[1]
    extra = [] if theirs is None else [theirs]

    def kernel(_, part, w, *refs):
        if wrows:
            out = nt_dot(part[...], w[:, :, :wrows, :].reshape(TILE, size))
        else:
            out = mm(part[...], w[...])
        if theirs is not None:
            out = out + refs[0][...].astype(F32)
        refs[-1][...] = out.astype(dtype)

    if wrows:
        shape = (TILE // (weight.shape[1] * wrows),) + weight.shape[1:]
        weight_spec = pl.BlockSpec(shape, lambda j, at: (j, 0, 0, 0))
    else:
        weight_spec = pl.BlockSpec((size, TILE), lambda j, at: (0, j))
    column = pl.BlockSpec((rows, TILE), lambda j, at: (0, j))
    return call(
        kernel,
        "part_product",
        micros=2,
        out_shape=jax.ShapeDtypeStruct((rows, D), dtype),
        grid_spec=pltpu.PrefetchScalarGridSpec(
            num_scalar_prefetch=1,
            grid=(D // TILE,),
            in_specs=[pl.BlockSpec((rows, size), lambda j, at: (at[0], 0)), weight_spec]
            + [column] * len(extra),
            out_specs=column,
        ),
    )(index.reshape(1), values, weight, *extra)


def output_grads(attn, grad_branch):
    rows, size = attn.shape

    def kernel(a, g, out):
        out[...] = tn_dot(a[...], g[...]).astype(BF)

    return call(
        kernel,
        "output_grads",
        micros=5,
        out_shape=jax.ShapeDtypeStruct((size, D), BF),
        grid=(D // TILE,),
        in_specs=[whole(attn), column_tile(rows)],
        out_specs=column_tile(size),
    )(attn, grad_branch)


def attn_grads(grad_branch, weight):
    rows, size = grad_branch.shape[0], weight.shape[0]

    def kernel(g, w, out):
        out[...] = nt_dot(g[...], w[...]).astype(BF)

    return call(
        kernel,
        "attn_grads",
        micros=5,
        out_shape=jax.ShapeDtypeStruct((rows, size), BF),
        grid=(rows // BLK,),
        in_specs=[pl.BlockSpec((BLK, D), lambda i: (i, 0)), whole(weight)],
        out_specs=pl.BlockSpec((BLK, size), lambda i: (i, 0)),
    )(grad_branch, weight)


def projection_grads(xa, grads, nc, ne, small=None):
    rows, wrows, size = xa.shape[0], D // (nc * ne), grads.shape[1]
    more = [] if small is None else list(small)
    high = wrows + sum(v.shape[2] for v in more)

    def kernel(x, g, *refs):
        out = refs[-1]
        out[:, :, :wrows, :] = tn_dot(x[...], g[...]).astype(BF).reshape(ne, 1, wrows, size)
        if small is not None:
            out[:, :, wrows:, :] = jnp.concatenate([refs[0][...], refs[1][...]], axis=2)

    return call(
        kernel,
        "projection_grads",
        micros=3,
        out_shape=jax.ShapeDtypeStruct((ne, nc, high, size), BF),
        grid=(nc,),
        in_specs=[pl.BlockSpec((rows, ne * wrows), lambda i: (0, i)), whole(grads)]
        + [pl.BlockSpec((ne, 1) + v.shape[2:], lambda i: (0, i, 0, 0)) for v in more],
        out_specs=pl.BlockSpec((ne, 1, high, size), lambda i: (0, i, 0, 0)),
    )(xa, grads, *more)


def gates_of(logits, chosen, empty):
    top = jnp.max(jnp.where(chosen, logits, MASKED), axis=-1, keepdims=True)
    raised = jnp.where(chosen, jnp.exp(jnp.where(chosen, logits - top, 0.0)), 0.0)
    total = jnp.sum(raised, axis=-1, keepdims=True)
    return raised / (jnp.where(total > 0.0, total, 1.0) if empty else total)


def on_device(
    tokens,
    expert_ids,
    cotangent,
    attn_gain,
    ffn_gain,
    query_gain,
    key_gain,
    query_weight,
    key_weight,
    value_weight,
    output_weight,
    router_weight,
    gate_weight,
    up_weight,
    down_weight,
):
    both = ("ctx", "exp")
    nc, ne = lax.axis_size("ctx"), lax.axis_size("exp")
    ci, ei = lax.axis_index("ctx"), lax.axis_index("exp")
    chip, core = ci // 2, ci % 2
    nchip = nc // 2
    count = nc * ne
    rows = tokens.shape[1]
    seq = rows * nc
    heads = H // nc
    width = heads * HD
    share = nc // KVH
    piece = 2 * HD // share
    member = ci % share
    experts = router_weight.shape[1]
    lanes = -(-experts // 128) * 128
    cap = -(-max(2, rows * TOP * 3 // (2 * experts)) // 8) * 8
    block = 2 * cap
    slots = nchip * block
    wrows = query_weight.shape[0]
    gain_rows, head_rows = attn_gain.shape[0], query_gain.shape[0]

    def mate(values, bit=1):
        return lax.ppermute(values, "ctx", [(i, i ^ bit) for i in range(nc)])

    def peer(values, step):
        return mate(values, 2 * step) if step else values

    def along(values):
        return lax.ppermute(values, "exp", [(i, (i + 1) % ne) for i in range(ne)])

    def after(values, *others):
        return lax.optimization_barrier((values,) + others)[0]

    def place(step, other):
        return (chip ^ step) * 2 + (1 - core if other else core)

    def gather_ctx(values, out):
        got = [values] + [None] * (nchip - 1)
        for step in range(nchip - 1, 0, -1):
            got[step] = peer(values, step)
        for step in range(nchip):
            out = lax.dynamic_update_slice_in_dim(out, got[step], place(step, False) * rows, 0)
            out = lax.dynamic_update_slice_in_dim(
                out, mate(got[step]), place(step, True) * rows, 0
            )
        return out

    def scatter_ctx(values, weight, height):
        def part(step, other, theirs, dtype):
            return part_product(values, place(step, other), rows, weight, height, theirs, dtype)

        arrived, sent = [], []
        for step in list(range(nchip - 1, 0, -1)) + [0]:
            theirs = mate(part(step, True, None, BF))
            mine = part(step, False, theirs, BF if step else F32)
            sent.append(mine)
            if step:
                arrived.append(peer(mine, step))
        total = mine
        for values in arrived:
            total = total + values.astype(F32)
        return total, sent

    own_tokens = tokens[0]
    x_all = lax.all_gather(own_tokens, "ctx", axis=0, tiled=True)
    w_out = lax.all_gather(after(output_weight, x_all), "exp", axis=0, tiled=True)
    total_width = width + piece
    packed = jnp.concatenate(
        [
            expert_ids[0].T.astype(BF).reshape(-1),
            attn_gain,
            ffn_gain,
            query_gain,
            key_gain,
            router_weight.reshape(-1),
        ]
    )
    more = -(-packed.shape[0] // (8 * total_width)) * 8
    packed = jnp.pad(packed, (0, more * total_width - packed.shape[0]))
    kv = jnp.concatenate(
        [key_weight.reshape(wrows, KVH, HD), value_weight.reshape(wrows, KVH, HD)], axis=2
    ).reshape(wrows, nc, piece)
    part = jnp.concatenate([query_weight.reshape(wrows, nc, width), kv], axis=2)
    part = jnp.concatenate(
        [
            part.transpose(1, 0, 2),
            jnp.broadcast_to(packed.reshape(1, more, total_width), (nc, more, total_width)),
        ],
        axis=1,
    )
    part = lax.all_to_all(part, "ctx", split_axis=0, concat_axis=0, tiled=True)

    spot = jnp.stack([chip, core, ci, ei]).astype(jnp.int32)
    index = lax.iota(jnp.int32, nc)
    devices = (chip ^ (index // 2)) * 2 + (core ^ (index % 2))
    planes = (ei - lax.iota(jnp.int32, ne)) % ne
    moving, send, direct, row_chosen = part, [], [], []
    w_in = jnp.zeros((nc, ne, wrows + more, total_width), BF)
    for step in range(ne):
        if step:
            moving = along(moving)
        w_in = lax.dynamic_update_slice(w_in, moving[:, None], (0, (ei - step) % ne, 0, 0))
        ids = moving[:, wrows:].reshape(nc, more * total_width)[:, : TOP * rows]
        ids = ids.reshape(nc, TOP, rows).astype(jnp.int32)
        if step:
            ids = after(ids, row_chosen[-1])
        else:
            own_ids = ids
        for into, values in zip(
            (send, direct, row_chosen), routing(ids, spot, ne, experts, cap)
        ):
            into.append(values)
        if step == 0:
            cot_first = select_direct(direct, jnp.zeros((1,), jnp.int32), cotangent)
            cot_first = lax.all_to_all(
                cot_first, "ctx", split_axis=0, concat_axis=0, tiled=True
            )
    table = w_in[:, :, wrows:].reshape(count, more * total_width)
    cuts = np.cumsum(
        [TOP * rows, gain_rows, gain_rows, head_rows, head_rows, wrows * experts]
    ).tolist()
    gain_attn = table[:, cuts[0] : cuts[1]].reshape(1, D).astype(F32)
    gain_ffn = table[:, cuts[1] : cuts[2]].reshape(1, D).astype(F32)
    gain_query = table[:, cuts[2] : cuts[3]].reshape(1, HD).astype(F32)
    gain_key = table[:, cuts[3] : cuts[4]].reshape(1, HD).astype(F32)
    router = table[:, cuts[4] : cuts[5]].reshape(D, experts)
    own_ids = lax.dynamic_index_in_dim(own_ids, ci, 0, keepdims=False)
    chosen_home = jnp.any(
        own_ids.T[:, :, None] == lax.iota(jnp.int32, experts)[None, None, :], axis=1
    )
    cot_all = lax.all_gather(
        after(cotangent[0], moving, w_out), "exp", axis=0, tiled=False
    )

    def to_experts(picked):
        return [peer(picked[m], m) for m in range(nchip - 1, -1, -1)][::-1]

    cos, sin = (jnp.asarray(v) for v in rope_tables(seq))
    x_all = after(x_all, cot_first)
    xa, raw = project(x_all, gain_attn, w_in, wrows)
    q_raw = raw[:, :width]
    kv_own = raw[:, width:]
    kv_parts = [kv_own] + [mate(kv_own, bit) for bit in range(1, share)]
    ordered = []
    for spot in range(share):
        chosen = kv_parts[spot]
        for m in range(1, share):
            chosen = jnp.where(member == m, kv_parts[spot ^ m], chosen)
        ordered.append(chosen)
    kv_raw = jnp.concatenate(ordered, axis=1) if share > 1 else ordered[0]
    k_raw, v_raw = kv_raw[:, :HD], kv_raw[:, HD:]
    near = heads // 2
    attn_near = attn_forward(q_raw, k_raw, v_raw, cos, sin, gain_query, gain_key, 0, near)
    k_far = after(k_raw, attn_near, w_out)
    attn_far = attn_forward(
        q_raw, k_far, v_raw, cos, sin, gain_query, gain_key, near, heads - near
    )
    attn = jnp.concatenate([attn_near, attn_far], axis=1)
    w_gate, w_up, w_down = gate_weight[0], up_weight[0], down_weight[0]
    cot_all = after(cot_all, attn_far)
    cot_moving = [
        lax.dynamic_index_in_dim(cot_all, (ei - step) % ne, 0, keepdims=False)
        for step in range(ne)
    ]
    cot_mates = [mate(v) for v in cot_moving]
    inputs = own_tokens.astype(F32)
    residual = inputs + scatter_ctx(attn, w_out, 0)[0]
    inv_res = inv_rms(residual)
    normed_res = residual * inv_res
    ffn_in = (normed_res * gain_ffn).astype(BF)

    lane = (lax.iota(jnp.int32, lanes)[None, :] == ci * ne + ei).astype(F32)
    column = lane[:, :experts]
    ffn_moving = [ffn_in]
    for _ in range(1, ne):
        ffn_moving.append(along(ffn_moving[-1]))
    arrived, done, mixed, back_home = [None] * ne, [], [], {}

    def send_chunk(step, *others):
        values = [after(ffn_moving[step], *others)]
        mates = [mate(values[0])]
        if step:
            values.append(cot_moving[step])
            mates.append(cot_mates[step])
        picked = select_rows(send[step], values, mates)
        arrived[step] = to_experts(picked)
        return picked[0]

    def run_chunk(step, *others):
        rows_in = [after(v, *others) for v in arrived[step]]
        backs, mixes, kept = expert_rows(
            rows_in, cot_first, devices, row_chosen[step], router, column, lane,
            (w_gate, w_up, w_down),
        )
        done.append((backs, kept))
        mixed.append(mixes)
        return kept[0]

    def give_back(step, *others):
        backs = [after(v, *others) for v in done[step][0]] if others else done[step][0]
        back_home[step] = to_experts(backs)

    order = list(range(1, ne)) + [0]
    tick = send_chunk(0)
    for step in range(ne):
        if step + 1 < ne:
            tick = send_chunk(step + 1, tick, *arrived[step])
        tick = run_chunk(step, tick)
    waits = arrived[-1]
    for step in order:
        give_back(step, *waits)
        waits = back_home[step]

    all_rows, hidden_g, act_gate, act_up = ([d[1][n] for d in done] for n in range(4))
    work = [
        lambda t: grad_in_weight(all_rows, [after(v, t) for v in act_gate]),
        lambda t: grad_in_weight(all_rows, [after(v, t) for v in act_up]),
        lambda t: grad_down_weight(
            [after(v, t) for v in hidden_g], devices, cot_first, arrived[1:]
        ),
    ]
    grads, travelling = [], None
    for at, step in enumerate(order):
        waits = (tick,) if travelling is None else (tick, travelling)
        mine, theirs = combine_rows(send[step], [after(v, *waits) for v in back_home[step]])
        back_total = mine + mate(theirs).astype(F32)
        if travelling is not None:
            back_total = back_total + travelling.astype(F32)
        if at < ne - 1:
            tick = back_total.astype(BF)
            travelling = along(tick)
            if work:
                tick = work.pop(0)(tick)
                grads.append(tick)
    grad_gate, grad_up, grad_down = grads

    gates_home = gates_of(mm(ffn_in, router), chosen_home, False)
    grad_gates = back_total[:, D : D + experts]
    grad_logits = gates_home * (
        grad_gates - jnp.sum(gates_home * grad_gates, axis=-1, keepdims=True)
    )
    grad_logits_low = grad_logits.astype(BF)
    grad_ffn_in = back_total[:, :D] + nt_dot(grad_logits_low, router)
    scaled = grad_ffn_in * gain_ffn
    grad_residual = cotangent[0].astype(F32) + inv_res * (
        scaled - normed_res * jnp.mean(scaled * normed_res, axis=-1, keepdims=True)
    )
    grad_router = tn_dot(ffn_in, grad_logits_low)
    grad_gain_ffn = jnp.sum(grad_ffn_in * normed_res, axis=0)

    grad_branch = gather_ctx(grad_residual.astype(BF), x_all)
    far_width = (heads - heads // 2) * HD + piece
    small = jnp.concatenate(
        [grad_router.reshape(nc, ne, wrows * experts), grad_gain_ffn.reshape(nc, ne, gain_rows)],
        axis=2,
    )
    ends = small.shape[2]
    extra = -(-(-(-ends // far_width) + 1) // 8) * 8
    small = jnp.pad(small, ((0, 0), (0, 0), (0, (extra - 1) * far_width - ends)))
    small = small.transpose(1, 0, 2).astype(BF).reshape(ne, nc, extra - 1, far_width)
    grad_branch = after(grad_branch, small)
    grad_output = output_grads(attn, grad_branch)
    grad_branch_late = after(grad_branch, grad_output)
    orows = output_weight.shape[0]

    def output_part(step):
        return lax.dynamic_slice_in_dim(grad_output, ((ei - step) % ne) * orows, orows, 0)

    output_ring = [output_part(1 % ne)]
    for step in range(2, ne):
        output_ring.append(output_part(step) + along(output_ring[-1]))
    output_sum = output_part(0).astype(F32)
    if ne > 1:
        output_sum = output_sum + along(output_ring[-1]).astype(F32)
    grad_attn = attn_grads(grad_branch_late, w_out)

    mix_home, waits = [], (grad_branch,)
    for blocks in mixed:
        waits = to_experts([after(v, *waits) for v in blocks])
        mix_home.append(waits)
    grad_attn = after(grad_attn, *mix_home[0], output_ring[1 % len(output_ring)])

    def weight_grad(earlier, grads, *small):
        local = projection_grads(xa, grads, nc, ne, *small)
        late = after(local, earlier)
        return local, lax.psum_scatter(late, "exp", scatter_dimension=0, tiled=True)[0]

    grad_q_near, *start = attn_backward(
        q_raw, k_raw, v_raw, cos, sin, gain_query, gain_key, grad_attn, 0, near, ()
    )
    local_near, grad_w_near = weight_grad(grad_output, grad_q_near)
    grad_attn = after(grad_attn, local_near, *mix_home[1], output_ring[-1])
    grad_q_far, grad_k, grad_v, grad_gain_query = attn_backward(
        q_raw, k_raw, v_raw, cos, sin, gain_query, gain_key, grad_attn, near, heads - near, start
    )
    grad_k = after(grad_k, *mix_home[2], output_sum)
    gks = [grad_k] + [mate(grad_k, bit) for bit in range(1, share)]
    gvs = [grad_v] + [mate(grad_v, bit) for bit in range(1, share)]
    grad_k_low, grad_v_low, grad_gain_key = key_backward(k_raw, cos, sin, gain_key, gks, gvs)
    grad_gain_key = jnp.where(member == 0, grad_gain_key, 0.0)
    grad_kv = jnp.concatenate([grad_k_low, grad_v_low], axis=1)
    if share > 1:
        grad_kv = lax.dynamic_slice_in_dim(grad_kv, member * piece, piece, 1)
    grad_far = jnp.concatenate([grad_q_far, grad_kv], axis=1)
    grad_in = jnp.concatenate([grad_q_near, grad_far], axis=1)
    gains = jnp.concatenate(
        [
            grad_gain_query.reshape(nc, ne, head_rows),
            grad_gain_key.reshape(nc, ne, head_rows),
        ],
        axis=2,
    )
    gains = jnp.pad(gains, ((0, 0), (0, 0), (0, far_width - 2 * head_rows)))
    gains = gains.transpose(1, 0, 2).astype(BF).reshape(ne, nc, 1, far_width)
    local_far, grad_w_far = weight_grad(grad_w_near, grad_far, (small, gains))
    grad_in = after(grad_in, local_far, *(v for blocks in mix_home[3:] for v in blocks))
    grad_w_near = jnp.pad(grad_w_near, ((0, 0), (0, extra), (0, 0)))
    grad_w = lax.all_to_all(
        jnp.concatenate([grad_w_near, grad_w_far], axis=2),
        "ctx",
        split_axis=0,
        concat_axis=0,
        tiled=True,
    ).astype(F32)
    small = jnp.sum(grad_w[:, wrows:, near * HD :], axis=0)
    gains, small = small[-1], small[:-1].reshape(-1)
    grad_w = grad_w[:, :wrows]
    sum_query = grad_w[:, :, :width].transpose(1, 0, 2).reshape(wrows, H * HD)
    sum_kv = grad_w[:, :, width:].transpose(1, 0, 2).reshape(wrows, KVH, 2 * HD)
    sum_key = sum_kv[:, :, :HD].reshape(wrows, KVH * HD)
    sum_value = sum_kv[:, :, HD:].reshape(wrows, KVH * HD)
    sum_attn_gain = (
        jnp.sum(sum_query * query_weight.astype(F32), axis=1)
        + jnp.sum(sum_key * key_weight.astype(F32), axis=1)
        + jnp.sum(sum_value * value_weight.astype(F32), axis=1)
    ) / attn_gain.astype(F32)

    grad_xa, sent = scatter_ctx(grad_in, w_in, wrows)
    mix_home[0][0] = after(mix_home[0][0], *sent)
    mine, theirs = combine_all(send, planes, mix_home)
    mixture = (mine.astype(F32) + mate(theirs).astype(F32)).astype(BF)
    mixture = after(mixture, grad_w_far)
    mixture = lax.psum_scatter(mixture, "exp", scatter_dimension=0, tiled=True)[0].astype(F32)
    inv_in = inv_rms(inputs)
    normed_in = inputs * inv_in
    scaled_in = grad_xa * gain_attn
    grad_tokens = (
        grad_residual
        + inv_in
        * (scaled_in - normed_in * jnp.mean(scaled_in * normed_in, axis=-1, keepdims=True))
    )[None]

    layer_out = (residual + mixture).astype(BF)[None]

    router_size = wrows * experts
    return (
        layer_out,
        grad_tokens,
        sum_attn_gain,
        small[router_size : router_size + gain_rows],
        gains[:head_rows],
        gains[head_rows : 2 * head_rows],
        sum_query,
        sum_key,
        sum_value,
        output_sum,
        small[:router_size].reshape(wrows, experts),
        grad_gate[None],
        grad_up[None],
        grad_down[None],
    )


def solution(mesh):
    shard = ("ctx", "exp")
    rows = P("exp", "ctx", None)
    vector, matrix, stack = P(shard), P(shard, None), P(shard, None, None)
    return jax.shard_map(
        on_device,
        mesh=mesh,
        in_specs=(rows,) * 3 + (vector,) * 4 + (matrix,) * 5 + (stack,) * 3,
        out_specs=(rows,) * 2 + (vector,) * 4 + (matrix,) * 5 + (stack,) * 3,
        check_vma=False,
    )
```

```python
import jax
import jax.numpy as jnp
import numpy as np
from jax import lax
from jax.experimental import pallas as pl
from jax.experimental.pallas import tpu as pltpu
from jax.sharding import PartitionSpec as P

D = 2048
H = 32
KVH = 4
HD = 128
TOP = 8
BLK = 256

EPSILON = 1e-06
ROPE_BASE = 1000000.0
SCALE = HD**-0.5
BF = jnp.bfloat16
F32 = jnp.float32
MASKED = -1e30
VMEM_LIMIT = 48 * 1024 * 1024
ATTN_LIMIT = 24 * 1024 * 1024
SMALL = pl.CostEstimate(flops=1000, bytes_accessed=1000, transcendentals=0)
TILE = 512


def cost(micros):
    return pl.CostEstimate(flops=int(1.1e9 * micros), bytes_accessed=1000, transcendentals=0)


def rope_tables(rows):
    half = HD // 2
    freq = np.power(ROPE_BASE, np.arange(half) * (-2.0 / HD))
    angles = np.arange(rows)[:, None] * freq[None, :]
    cos, sin = np.cos(angles), np.sin(angles)
    return (
        np.concatenate([cos, cos], axis=1).astype(np.float32),
        np.concatenate([-sin, sin], axis=1).astype(np.float32),
    )


def inv_rms(values):
    return lax.rsqrt(jnp.mean(values * values, axis=-1, keepdims=True) + EPSILON)


def nt_dot(a, b):
    return lax.dot_general(a, b, (((1,), (1,)), ((), ())), preferred_element_type=F32)


def tn_dot(a, b):
    return lax.dot_general(a, b, (((0,), (0,)), ((), ())), preferred_element_type=F32)


def mm(a, b):
    return jnp.dot(a, b, preferred_element_type=F32)


def spin(values, cos, sin):
    return values * cos + pltpu.roll(values, HD // 2, 1) * sin


def unspin(values, cos, sin):
    return values * cos - pltpu.roll(values, HD // 2, 1) * sin


def attn_forward_kernel(blocks, raw, kraw, vraw, cos_all, sin_all, cos, sin, qgain, kgain, out, keys, vals):
    head, block = pl.program_id(0), pl.program_id(1)

    @pl.when((head == 0) & (block == 0))
    def _():
        rows = kraw[...]
        keys[...] = spin(rows * inv_rms(rows) * kgain[...], cos_all[...], sin_all[...]).astype(BF)
        vals[...] = vraw[...].astype(BF)

    rows = raw[...]
    query = spin(rows * inv_rms(rows) * qgain[...], cos[...], sin[...]).astype(BF)
    for n in range(blocks):

        @pl.when(block == n)
        def _(n=n):
            span = (n + 1) * BLK
            weights = jnp.exp(nt_dot(query, keys[:span, :]) * SCALE)
            total = jnp.sum(weights, axis=-1, keepdims=True)
            probs = (weights * (1.0 / total)).astype(BF)
            out[...] = mm(probs, vals[:span, :]).astype(BF)


def attn_backward_kernel(
    blocks, raw, kraw, vraw, cos_all, sin_all, cos, sin, qgain, kgain, gout, *rest
):
    *start, gq, gk, gv, gqgain, keys, vals = rest
    head, block = pl.program_id(0), pl.program_id(1)

    @pl.when((head == 0) & (block == 0))
    def _():
        rows = kraw[...]
        keys[...] = spin(rows * inv_rms(rows) * kgain[...], cos_all[...], sin_all[...]).astype(BF)
        vals[...] = vraw[...].astype(BF)
        for ref, first in zip((gk, gv, gqgain), start or (None,) * 3):
            ref[...] = jnp.zeros_like(ref) if first is None else first[...]

    rows = raw[...]
    inverse = inv_rms(rows)
    normed = rows * inverse
    query = spin(normed * qgain[...], cos[...], sin[...]).astype(BF)
    grad_out = gout[...]

    def finish(grad_query):
        turned = unspin(grad_query, cos[...], sin[...])
        gqgain[...] += jnp.sum(turned * normed, axis=0, keepdims=True)
        scaled = turned * qgain[...]
        mean = jnp.mean(scaled * normed, axis=-1, keepdims=True)
        gq[...] = (inverse * (scaled - normed * mean)).astype(BF)

    for n in range(blocks):

        @pl.when(block == n)
        def _(n=n):
            span = (n + 1) * BLK
            seen, values = keys[:span, :], vals[:span, :]
            weights = jnp.exp(nt_dot(query, seen) * SCALE)
            total = jnp.sum(weights, axis=-1, keepdims=True)
            probs = weights * (1.0 / total)
            grad_probs = nt_dot(grad_out, values)
            delta = jnp.sum(probs * grad_probs, axis=-1, keepdims=True)
            grad_scores = (probs * (grad_probs - delta)).astype(BF)
            gv[:span, :] += tn_dot(probs.astype(BF), grad_out)
            gk[:span, :] += tn_dot(grad_scores, query) * SCALE
            finish(mm(grad_scores, seen) * SCALE)


def key_backward_kernel(count, kraw, cos, sin, kgain, *rest):
    gks, gvs, (gk_low, gv_low, gkgain) = rest[:count], rest[count : 2 * count], rest[2 * count :]
    grad_keys, grad_vals = gks[0][...], gvs[0][...]
    for n in range(1, count):
        grad_keys = grad_keys + gks[n][...]
        grad_vals = grad_vals + gvs[n][...]
    rows = kraw[...]
    inverse = inv_rms(rows)
    normed = rows * inverse
    turned = unspin(grad_keys, cos[...], sin[...])
    gkgain[...] = jnp.sum(turned * normed, axis=0, keepdims=True)
    scaled = turned * kgain[...]
    mean = jnp.mean(scaled * normed, axis=-1, keepdims=True)
    gk_low[...] = (inverse * (scaled - normed * mean)).astype(BF)
    gv_low[...] = grad_vals.astype(BF)


def attn_specs(rows, first=0):
    return [
        pl.BlockSpec((BLK, HD), lambda h, i: (i, h + first)),
        pl.BlockSpec((rows, HD), lambda h, i: (0, 0)),
        pl.BlockSpec((rows, HD), lambda h, i: (0, 0)),
        pl.BlockSpec((rows, HD), lambda h, i: (0, 0)),
        pl.BlockSpec((rows, HD), lambda h, i: (0, 0)),
        pl.BlockSpec((BLK, HD), lambda h, i: (i, 0)),
        pl.BlockSpec((BLK, HD), lambda h, i: (i, 0)),
        pl.BlockSpec((1, HD), lambda h, i: (0, 0)),
        pl.BlockSpec((1, HD), lambda h, i: (0, 0)),
    ]


def attn_forward(raw, kraw, vraw, cos, sin, qgain, kgain, first, heads):
    rows = raw.shape[0]
    blocks = rows // BLK
    return pl.pallas_call(
        lambda *refs: attn_forward_kernel(blocks, *refs),
        grid=(heads, blocks),
        in_specs=attn_specs(rows, first),
        out_specs=pl.BlockSpec((BLK, HD), lambda h, i: (i, h)),
        out_shape=jax.ShapeDtypeStruct((rows, heads * HD), BF),
        scratch_shapes=[pltpu.VMEM((rows, HD), BF), pltpu.VMEM((rows, HD), BF)],
        compiler_params=pltpu.CompilerParams(vmem_limit_bytes=ATTN_LIMIT),
        cost_estimate=cost(13),
        name="attn_fw",
    )(raw, kraw, vraw, cos, sin, cos, sin, qgain, kgain)


def attn_backward(raw, kraw, vraw, cos, sin, qgain, kgain, gout, first, heads, start):
    rows = raw.shape[0]
    blocks = rows // BLK
    return pl.pallas_call(
        lambda *refs: attn_backward_kernel(blocks, *refs),
        grid=(heads, blocks),
        in_specs=attn_specs(rows, first)
        + [pl.BlockSpec((BLK, HD), lambda h, i: (i, h + first))]
        + [pl.BlockSpec(v.shape, lambda h, i: (0, 0)) for v in start],
        out_specs=[
            pl.BlockSpec((BLK, HD), lambda h, i: (i, h)),
            pl.BlockSpec((rows, HD), lambda h, i: (0, 0)),
            pl.BlockSpec((rows, HD), lambda h, i: (0, 0)),
            pl.BlockSpec((1, HD), lambda h, i: (0, 0)),
        ],
        out_shape=[
            jax.ShapeDtypeStruct((rows, heads * HD), BF),
            jax.ShapeDtypeStruct((rows, HD), F32),
            jax.ShapeDtypeStruct((rows, HD), F32),
            jax.ShapeDtypeStruct((1, HD), F32),
        ],
        scratch_shapes=[pltpu.VMEM((rows, HD), BF), pltpu.VMEM((rows, HD), BF)],
        compiler_params=pltpu.CompilerParams(vmem_limit_bytes=ATTN_LIMIT),
        cost_estimate=cost(22),
        name="attn_bw",
    )(raw, kraw, vraw, cos, sin, cos, sin, qgain, kgain, gout, *start)


def key_backward(kraw, cos, sin, kgain, gks, gvs):
    rows = kraw.shape[0]
    return pl.pallas_call(
        lambda *refs: key_backward_kernel(len(gks), *refs),
        out_shape=[
            jax.ShapeDtypeStruct((rows, HD), BF),
            jax.ShapeDtypeStruct((rows, HD), BF),
            jax.ShapeDtypeStruct((1, HD), F32),
        ],
        compiler_params=pltpu.CompilerParams(vmem_limit_bytes=ATTN_LIMIT),
        cost_estimate=cost(2),
        name="key_bw",
    )(kraw, cos, sin, kgain, *gks, *gvs)


def call(kernel, name, out_shape, micros=0, **kw):
    return pl.pallas_call(
        kernel,
        out_shape=out_shape,
        compiler_params=pltpu.CompilerParams(vmem_limit_bytes=VMEM_LIMIT),
        cost_estimate=cost(micros) if micros else SMALL,
        name=name,
        **kw,
    )


def whole(values):
    return pl.BlockSpec(values.shape, lambda *_: (0,) * values.ndim)


def column_tile(height):
    return pl.BlockSpec((height, TILE), lambda j: (0, j))


def routing(ids, place, ne, experts, cap):
    nc, _, rows = ids.shape
    nchip = nc // 2
    block = 2 * cap

    def kernel(at, ids_ref, send, direct, chosen, spots, named):
        chip, core, ci, ei = at[0], at[1], at[2], at[3]
        number = lax.broadcasted_iota(jnp.int32, (experts, rows), 0)
        slot = lax.broadcasted_iota(jnp.int32, (cap, rows), 0).astype(F32)
        lower = (
            lax.broadcasted_iota(jnp.int32, (rows, rows), 0)
            < lax.broadcasted_iota(jnp.int32, (rows, rows), 1)
        ).astype(BF)
        for dev in range(nc):
            got = ids_ref[dev]
            hits = jnp.zeros((experts, rows), F32)
            for k in range(TOP):
                hits = hits + (got[k : k + 1, :] == number).astype(F32)
            named[dev] = hits.astype(BF)
            spots[dev] = jnp.where(hits > 0.5, mm(hits.astype(BF), lower), -1.0)

        def slots_of(dev, expert):
            line = jnp.sum(jnp.where(number == expert, spots[dev], 0.0), axis=0, keepdims=True)
            return (line == slot).astype(BF)

        for m in range(nchip):
            expert = ((chip ^ m) * 2 + core) * ne + ei
            send[m] = jnp.zeros((block, 2 * rows), BF)
            send[m, :cap, :rows] = slots_of(ci, expert)
            send[m, cap:, rows:] = slots_of(ci ^ 1, expert)
            for src in range(2):
                dev = (chip ^ m) * 2 + (core ^ src)
                taken = slots_of(dev, ci * ne + ei)
                first = (m * 2 + src) * cap
                chosen[first : first + cap, :] = nt_dot(taken, named[dev])
        for dev in range(nc):
            direct[dev] = slots_of(ci, dev * ne + ei)

    return pl.pallas_call(
        kernel,
        out_shape=[
            jax.ShapeDtypeStruct((nchip, block, 2 * rows), BF),
            jax.ShapeDtypeStruct((nc, cap, rows), BF),
            jax.ShapeDtypeStruct((nc * cap, experts), F32),
        ],
        in_specs=[pl.BlockSpec(memory_space=pltpu.SMEM), pl.BlockSpec(memory_space=pltpu.VMEM)],
        scratch_shapes=[
            pltpu.VMEM((nc, experts, rows), F32),
            pltpu.VMEM((nc, experts, rows), BF),
        ],
        compiler_params=pltpu.CompilerParams(vmem_limit_bytes=ATTN_LIMIT),
        cost_estimate=SMALL,
        name="routing",
    )(place, ids)


def select_direct(direct, planes, values):
    steps, (nc, cap, rows) = len(direct), direct[0].shape

    def kernel(at, *refs):
        tokens, out = refs[steps], refs[steps + 1]
        for n in range(steps):
            part = tokens[at[n]]
            for dev in range(nc):
                out[dev, n * cap : (n + 1) * cap, :] = mm(refs[n][dev], part).astype(BF)

    return call(
        kernel,
        "select_direct",
        micros=3,
        out_shape=jax.ShapeDtypeStruct((nc, steps * cap, D), BF),
        grid=(D // TILE,),
        in_specs=[pl.BlockSpec(memory_space=pltpu.SMEM)]
        + [whole(v) for v in direct]
        + [pl.BlockSpec((values.shape[0], rows, TILE), lambda j: (0, 0, j))],
        out_specs=pl.BlockSpec((nc, steps * cap, TILE), lambda j: (0, 0, j)),
    )(planes, *direct, values)


def select_rows(send, values, mates):
    nchip, block, _ = send.shape
    rows, count = values[0].shape[0], len(values)

    def kernel(picks, *refs):
        outs = refs[2 * count :]
        for n in range(count):
            pair = jnp.concatenate([refs[n][...], refs[count + n][...]], axis=0)
            for m in range(nchip):
                outs[m][n] = mm(picks[m], pair).astype(BF)

    return call(
        kernel,
        "select_rows",
        out_shape=[jax.ShapeDtypeStruct((count, block, D), BF)] * nchip,
        grid=(D // TILE,),
        in_specs=[whole(send)] + [column_tile(rows)] * (2 * count),
        out_specs=[pl.BlockSpec((count, block, TILE), lambda j: (0, 0, j))] * nchip,
    )(send, *values, *mates)


def combine_rows(send, home):
    nchip, block, _ = send.shape
    rows, wide = send.shape[2] // 2, home[0].shape[1]

    def kernel(picks, *refs):
        blocks, mine, theirs = refs[:nchip], refs[nchip], refs[nchip + 1]
        got = jnp.concatenate([b[...] for b in blocks], axis=0)
        chosen = jnp.concatenate([picks[m] for m in range(nchip)], axis=0)
        both = tn_dot(chosen, got)
        mine[...] = both[:rows]
        theirs[...] = both[rows:].astype(BF)

    return call(
        kernel,
        "combine_rows",
        micros=3,
        out_shape=[jax.ShapeDtypeStruct((rows, wide), F32), jax.ShapeDtypeStruct((rows, wide), BF)],
    )(send, *home)


def combine_all(send, planes, home):
    ne, (nchip, block, wide) = len(send), send[0].shape
    rows = wide // 2

    def kernel(at, *refs):
        mine, theirs = refs[-2:]
        for step in range(ne):
            blocks = refs[ne + step * nchip : ne + (step + 1) * nchip]
            got = jnp.concatenate([b[...] for b in blocks], axis=0)
            chosen = jnp.concatenate([refs[step][m] for m in range(nchip)], axis=0)
            both = tn_dot(chosen, got).astype(BF)
            mine[at[step]] = both[:rows]
            theirs[at[step]] = both[rows:]

    return call(
        kernel,
        "combine_all",
        micros=6,
        out_shape=[jax.ShapeDtypeStruct((ne, rows, D), BF)] * 2,
        grid=(D // TILE,),
        in_specs=[pl.BlockSpec(memory_space=pltpu.SMEM)]
        + [whole(v) for v in send]
        + [column_tile(block)] * (ne * nchip),
        out_specs=[pl.BlockSpec((ne, rows, TILE), lambda j: (0, 0, j))] * 2,
    )(planes, *send, *(v for blocks in home for v in blocks))


def expert_rows(rows_in, cot_in, devices, row_chosen, router, column, lane, weights):
    nchip, (both, block, _) = len(rows_in), rows_in[0].shape
    nc, cap = 2 * nchip, block // 2
    cots = 0 if both > 1 else nc
    slots, lanes, hidden_size = nchip * block, lane.shape[1], weights[0].shape[1]

    def kernel(_, *refs):
        ffn_in, cot_refs = refs[:nchip], refs[nchip : nchip + cots]
        chosen_ref, router_ref, column_ref, lane_ref, w_gate, w_up, w_down = refs[
            nchip + cots : nchip + cots + 7
        ]
        outs = refs[nchip + cots + 7 :]
        backs, mixes, kept = outs[:nchip], outs[nchip : 2 * nchip], outs[2 * nchip :]
        all_out, hidden_out, gate_out, up_out = kept
        rows = jnp.concatenate([r[0] for r in ffn_in], axis=0)
        cot = jnp.concatenate([r[0] for r in cot_refs] or [r[1] for r in ffn_in], axis=0)
        all_out[...] = rows
        gates = gates_of(mm(rows, router_ref[...]), chosen_ref[...] > 0.5, True)
        gate_vec = jnp.sum(gates * column_ref[...], axis=-1, keepdims=True)
        gate_act = mm(rows, w_gate[...])
        up_act = mm(rows, w_up[...])
        upstream = nt_dot(cot, w_down[...])
        sig = 1.0 / (1.0 + jnp.exp(-gate_act))
        silu = gate_act * sig
        hidden = (silu * up_act).astype(BF).astype(F32)
        score = jnp.sum(upstream * hidden, axis=-1, keepdims=True)
        gated = (hidden * gate_vec).astype(BF)
        hidden_out[...] = gated
        grad_hidden = upstream * gate_vec
        grad_gate = (grad_hidden * up_act * sig * (1.0 + gate_act * (1.0 - sig))).astype(BF)
        grad_up = (grad_hidden * silu).astype(BF)
        gate_out[...] = grad_gate
        up_out[...] = grad_up
        back = (nt_dot(grad_gate, w_gate[...]) + nt_dot(grad_up, w_up[...])).astype(BF)
        scores = (score * lane_ref[...]).astype(BF)
        for m in range(nchip):
            part = slice(m * block, (m + 1) * block)
            backs[m][:, :D] = back[part]
            backs[m][:, D:] = scores[part]
            mixes[m][...] = mm(gated[part], w_down[...]).astype(BF)

    narrow = jax.ShapeDtypeStruct((slots, hidden_size), BF)
    out_shape = [jax.ShapeDtypeStruct((block, D + lanes), BF)] * nchip
    out_shape += [jax.ShapeDtypeStruct((block, D), BF)] * nchip + [
        jax.ShapeDtypeStruct((slots, D), BF),
        narrow,
        narrow,
        narrow,
    ]
    fixed = [row_chosen, router, column, lane, *weights]
    outs = call(
        kernel,
        "expert_rows",
        micros=2,
        out_shape=out_shape,
        grid_spec=pltpu.PrefetchScalarGridSpec(
            num_scalar_prefetch=1,
            grid=(1,),
            in_specs=[whole(r) for r in rows_in]
            + [
                pl.BlockSpec((1, cap, D), lambda i, at, n=n: (at[n], 0, 0))
                for n in range(cots)
            ]
            + [whole(v) for v in fixed],
            out_specs=[whole(v) for v in out_shape],
        ),
    )(devices, *rows_in, *([cot_in] * cots), *fixed)
    return outs[:nchip], outs[nchip : 2 * nchip], outs[2 * nchip :]


def grad_in_weight(rows, grads):
    chunks, slots, size = len(rows), rows[0].shape[0], grads[0].shape[1]

    def kernel(*refs):
        total = tn_dot(refs[0][...], refs[chunks][...])
        for n in range(1, chunks):
            total += tn_dot(refs[n][...], refs[chunks + n][...])
        refs[2 * chunks][...] = total

    return call(
        kernel,
        "grad_in_weight",
        micros=10,
        out_shape=jax.ShapeDtypeStruct((D, size), F32),
        grid=(D // TILE,),
        in_specs=[column_tile(slots)] * chunks + [whole(v) for v in grads],
        out_specs=pl.BlockSpec((TILE, size), lambda i: (i, 0)),
    )(*rows, *grads)


def grad_down_weight(hidden, devices, cot_first, later):
    chunks = len(hidden)
    (nc, cap, _), size = cot_first.shape, hidden[0].shape[1]
    nchip = nc // 2

    def kernel(at, *refs):
        hid, early, late, out = refs[:chunks], refs[chunks], refs[chunks + 1 : -1], refs[-1]
        total = None
        for n in range(chunks):
            if n:
                rows = [r[0] for r in late[(n - 1) * nchip : n * nchip]]
            else:
                rows = [early[at[i]] for i in range(nc)]
            part = tn_dot(hid[n][...], jnp.concatenate(rows, axis=0))
            total = part if total is None else total + part
        out[...] = total

    late = [v for blocks in later for v in blocks]
    return call(
        kernel,
        "grad_down_weight",
        micros=10,
        out_shape=jax.ShapeDtypeStruct((size, D), F32),
        grid=(D // TILE,),
        in_specs=[pl.BlockSpec(memory_space=pltpu.SMEM)]
        + [whole(v) for v in hidden]
        + [pl.BlockSpec((nc, cap, TILE), lambda j: (0, 0, j))]
        + [pl.BlockSpec((1, 2 * cap, TILE), lambda j: (1, 0, j))] * len(late),
        out_specs=column_tile(size),
    )(devices, *hidden, cot_first, *late)


def project(x_all, gain, weight, wrows):
    rows, size = x_all.shape[0], weight.shape[3]

    def kernel(x, gain_ref, w, normed, raw):
        values = x[...].astype(F32)
        low = (values * inv_rms(values) * gain_ref[...]).astype(BF)
        normed[...] = low
        raw[...] = mm(low, w[:, :, :wrows, :].reshape(D, size))

    band = pl.BlockSpec((BLK, D), lambda i: (i, 0))
    return call(
        kernel,
        "project",
        micros=6,
        out_shape=[jax.ShapeDtypeStruct((rows, D), BF), jax.ShapeDtypeStruct((rows, size), F32)],
        grid=(rows // BLK,),
        in_specs=[band, whole(gain), whole(weight)],
        out_specs=[band, pl.BlockSpec((BLK, size), lambda i: (i, 0))],
    )(x_all, gain, weight)


def part_product(values, index, rows, weight, wrows, theirs, dtype):
    size = values.shape[1]
    extra = [] if theirs is None else [theirs]

    def kernel(_, part, w, *refs):
        if wrows:
            out = nt_dot(part[...], w[:, :, :wrows, :].reshape(TILE, size))
        else:
            out = mm(part[...], w[...])
        if theirs is not None:
            out = out + refs[0][...].astype(F32)
        refs[-1][...] = out.astype(dtype)

    if wrows:
        shape = (TILE // (weight.shape[1] * wrows),) + weight.shape[1:]
        weight_spec = pl.BlockSpec(shape, lambda j, at: (j, 0, 0, 0))
    else:
        weight_spec = pl.BlockSpec((size, TILE), lambda j, at: (0, j))
    column = pl.BlockSpec((rows, TILE), lambda j, at: (0, j))
    return call(
        kernel,
        "part_product",
        micros=2,
        out_shape=jax.ShapeDtypeStruct((rows, D), dtype),
        grid_spec=pltpu.PrefetchScalarGridSpec(
            num_scalar_prefetch=1,
            grid=(D // TILE,),
            in_specs=[pl.BlockSpec((rows, size), lambda j, at: (at[0], 0)), weight_spec]
            + [column] * len(extra),
            out_specs=column,
        ),
    )(index.reshape(1), values, weight, *extra)


def branch_grads(attn, pieces, devices, weight):
    (rows, size), height = attn.shape, pieces[0].shape[0]

    def kernel(at, a, w, *refs):
        parts, (to_weight, to_attn, whole_g) = refs[: len(pieces)], refs[len(pieces) :]
        for n, part in enumerate(parts):
            first = pl.multiple_of(at[n] * height, height)
            whole_g[pl.ds(first, height), :] = part[...]
        for n in range(0, D, TILE):
            to_weight[:, n : n + TILE] = tn_dot(a[...], whole_g[:, n : n + TILE]).astype(BF)
        for n in range(0, rows, BLK):
            to_attn[n : n + BLK, :] = nt_dot(whole_g[n : n + BLK, :], w[...]).astype(BF)

    outs = [jax.ShapeDtypeStruct((size, D), BF), jax.ShapeDtypeStruct((rows, size), BF)]
    return call(
        kernel,
        "branch_grads",
        micros=12,
        out_shape=outs,
        grid=(1,),
        in_specs=[pl.BlockSpec(memory_space=pltpu.SMEM)]
        + [whole(v) for v in (attn, weight, *pieces)],
        out_specs=[whole(v) for v in outs],
        scratch_shapes=[pltpu.VMEM((rows, D), BF)],
    )(devices, attn, weight, *pieces)


def projection_grads(xa, grads, nc, ne, small=None):
    rows, wrows, size = xa.shape[0], D // (nc * ne), grads.shape[1]
    more = [] if small is None else list(small)
    high = wrows + sum(v.shape[2] for v in more)

    def kernel(x, g, *refs):
        out = refs[-1]
        out[:, :, :wrows, :] = tn_dot(x[...], g[...]).astype(BF).reshape(ne, 1, wrows, size)
        if small is not None:
            out[:, :, wrows:, :] = jnp.concatenate([refs[0][...], refs[1][...]], axis=2)

    return call(
        kernel,
        "projection_grads",
        micros=8,
        out_shape=jax.ShapeDtypeStruct((ne, nc, high, size), BF),
        grid=(nc,),
        in_specs=[pl.BlockSpec((rows, ne * wrows), lambda i: (0, i)), whole(grads)]
        + [pl.BlockSpec((ne, 1) + v.shape[2:], lambda i: (0, i, 0, 0)) for v in more],
        out_specs=pl.BlockSpec((ne, 1, high, size), lambda i: (0, i, 0, 0)),
    )(xa, grads, *more)


def gates_of(logits, chosen, empty):
    top = jnp.max(jnp.where(chosen, logits, MASKED), axis=-1, keepdims=True)
    raised = jnp.where(chosen, jnp.exp(jnp.where(chosen, logits - top, 0.0)), 0.0)
    total = jnp.sum(raised, axis=-1, keepdims=True)
    return raised / (jnp.where(total > 0.0, total, 1.0) if empty else total)


def on_device(
    tokens,
    expert_ids,
    cotangent,
    attn_gain,
    ffn_gain,
    query_gain,
    key_gain,
    query_weight,
    key_weight,
    value_weight,
    output_weight,
    router_weight,
    gate_weight,
    up_weight,
    down_weight,
):
    both = ("ctx", "exp")
    nc, ne = lax.axis_size("ctx"), lax.axis_size("exp")
    ci, ei = lax.axis_index("ctx"), lax.axis_index("exp")
    chip, core = ci // 2, ci % 2
    nchip = nc // 2
    count = nc * ne
    rows = tokens.shape[1]
    seq = rows * nc
    heads = H // nc
    width = heads * HD
    share = nc // KVH
    piece = 2 * HD // share
    member = ci % share
    experts = router_weight.shape[1]
    lanes = -(-experts // 128) * 128
    cap = -(-max(2, rows * TOP * 3 // (2 * experts)) // 8) * 8
    block = 2 * cap
    slots = nchip * block
    wrows = query_weight.shape[0]
    gain_rows, head_rows = attn_gain.shape[0], query_gain.shape[0]

    def mate(values, bit=1):
        return lax.ppermute(values, "ctx", [(i, i ^ bit) for i in range(nc)])

    def peer(values, step):
        return mate(values, 2 * step) if step else values

    def along(values):
        return lax.ppermute(values, "exp", [(i, (i + 1) % ne) for i in range(ne)])

    def after(values, *others):
        return lax.optimization_barrier((values,) + others)[0]

    def place(step, other):
        return (chip ^ step) * 2 + (1 - core if other else core)

    def gather_ctx(values):
        got = [values] + [None] * (nchip - 1)
        for step in range(nchip - 1, 0, -1):
            got[step] = peer(values, step)
        return [v for part in got for v in (part, mate(part))]

    def scatter_ctx(values, weight, height, *late):
        def part(step, other, theirs, dtype):
            return part_product(values, place(step, other), rows, weight, height, theirs, dtype)

        arrived, sent = [], []
        for step in list(range(nchip - 1, 0, -1)) + [0]:
            theirs = after(mate(part(step, True, None, BF)), *late)
            mine = part(step, False, theirs, BF if step else F32)
            sent.append(mine)
            if step:
                arrived.append(peer(mine, step))
        total = mine
        for values in arrived:
            total = total + values.astype(F32)
        return total, sent

    own_tokens = tokens[0]
    x_all = lax.all_gather(own_tokens, "ctx", axis=0, tiled=True)
    w_out = lax.all_gather(after(output_weight, x_all), "exp", axis=0, tiled=True)
    total_width = width + piece
    packed = jnp.concatenate(
        [
            expert_ids[0].T.astype(BF).reshape(-1),
            attn_gain,
            ffn_gain,
            query_gain,
            key_gain,
            router_weight.reshape(-1),
        ]
    )
    more = -(-packed.shape[0] // (8 * total_width)) * 8
    packed = jnp.pad(packed, (0, more * total_width - packed.shape[0]))
    kv = jnp.concatenate(
        [key_weight.reshape(wrows, KVH, HD), value_weight.reshape(wrows, KVH, HD)], axis=2
    ).reshape(wrows, nc, piece)
    part = jnp.concatenate([query_weight.reshape(wrows, nc, width), kv], axis=2)
    part = jnp.concatenate(
        [
            part.transpose(1, 0, 2),
            jnp.broadcast_to(packed.reshape(1, more, total_width), (nc, more, total_width)),
        ],
        axis=1,
    )
    part = lax.all_to_all(part, "ctx", split_axis=0, concat_axis=0, tiled=True)

    spot = jnp.stack([chip, core, ci, ei]).astype(jnp.int32)
    index = lax.iota(jnp.int32, nc)
    devices = (chip ^ (index // 2)) * 2 + (core ^ (index % 2))
    planes = (ei - lax.iota(jnp.int32, ne)) % ne
    moving, send, direct, row_chosen = part, [], [], []
    w_in = jnp.zeros((nc, ne, wrows + more, total_width), BF)
    for step in range(ne):
        if step:
            moving = along(moving)
        w_in = lax.dynamic_update_slice(w_in, moving[:, None], (0, (ei - step) % ne, 0, 0))
        ids = moving[:, wrows:].reshape(nc, more * total_width)[:, : TOP * rows]
        ids = ids.reshape(nc, TOP, rows).astype(jnp.int32)
        if step:
            ids = after(ids, row_chosen[-1])
        else:
            own_ids = ids
        for into, values in zip(
            (send, direct, row_chosen), routing(ids, spot, ne, experts, cap)
        ):
            into.append(values)
        if step == 0:
            cot_first = select_direct(direct, jnp.zeros((1,), jnp.int32), cotangent)
            cot_first = lax.all_to_all(
                cot_first, "ctx", split_axis=0, concat_axis=0, tiled=True
            )
    table = w_in[:, :, wrows:].reshape(count, more * total_width)
    cuts = np.cumsum(
        [TOP * rows, gain_rows, gain_rows, head_rows, head_rows, wrows * experts]
    ).tolist()
    gain_attn = table[:, cuts[0] : cuts[1]].reshape(1, D).astype(F32)
    gain_ffn = table[:, cuts[1] : cuts[2]].reshape(1, D).astype(F32)
    gain_query = table[:, cuts[2] : cuts[3]].reshape(1, HD).astype(F32)
    gain_key = table[:, cuts[3] : cuts[4]].reshape(1, HD).astype(F32)
    router = table[:, cuts[4] : cuts[5]].reshape(D, experts)
    own_ids = lax.dynamic_index_in_dim(own_ids, ci, 0, keepdims=False)
    chosen_home = jnp.any(
        own_ids.T[:, :, None] == lax.iota(jnp.int32, experts)[None, None, :], axis=1
    )
    cot_all = lax.all_gather(
        after(cotangent[0], moving, w_out), "exp", axis=0, tiled=False
    )

    def to_experts(picked):
        return [peer(picked[m], m) for m in range(nchip - 1, -1, -1)][::-1]

    cos, sin = (jnp.asarray(v) for v in rope_tables(seq))
    x_all = after(x_all, cot_first, send[max(0, ne - 2)], row_chosen[max(0, ne - 2)])
    xa, raw = project(x_all, gain_attn, w_in, wrows)
    q_raw = raw[:, :width]
    kv_own = raw[:, width:]
    kv_parts = [kv_own] + [mate(kv_own, bit) for bit in range(1, share)]
    ordered = []
    for spot in range(share):
        chosen = kv_parts[spot]
        for m in range(1, share):
            chosen = jnp.where(member == m, kv_parts[spot ^ m], chosen)
        ordered.append(chosen)
    kv_raw = jnp.concatenate(ordered, axis=1) if share > 1 else ordered[0]
    k_raw, v_raw = kv_raw[:, :HD], kv_raw[:, HD:]
    attn = attn_forward(q_raw, k_raw, v_raw, cos, sin, gain_query, gain_key, 0, heads)
    w_gate, w_up, w_down = gate_weight[0], up_weight[0], down_weight[0]
    cot_all = after(cot_all, attn)
    cot_moving = [
        lax.dynamic_index_in_dim(cot_all, (ei - step) % ne, 0, keepdims=False)
        for step in range(ne)
    ]
    cot_mates = [mate(v) for v in cot_moving]
    inputs = own_tokens.astype(F32)
    residual = inputs + scatter_ctx(attn, w_out, 0)[0]
    inv_res = inv_rms(residual)
    normed_res = residual * inv_res
    ffn_in = (normed_res * gain_ffn).astype(BF)

    lane = (lax.iota(jnp.int32, lanes)[None, :] == ci * ne + ei).astype(F32)
    column = lane[:, :experts]
    ffn_moving = [ffn_in]
    for _ in range(1, min(ne, 2)):
        ffn_moving.append(along(ffn_moving[-1]))
    arrived, done, mixed, back_home = [None] * ne, [], [], {}

    def pick_chunk(step, *others):
        values = [after(ffn_moving[step], *others)]
        mates = [mate(values[0])]
        if step:
            values.append(cot_moving[step])
            mates.append(cot_mates[step])
        return select_rows(send[step], values, mates)

    def run_chunk(step, *others):
        rows_in = [after(v, *others) for v in arrived[step]]
        backs, mixes, kept = expert_rows(
            rows_in, cot_first, devices, row_chosen[step], router, column, lane,
            (w_gate, w_up, w_down),
        )
        done.append((backs, kept))
        mixed.append(mixes)
        return kept[0]

    def give_back(step, *others):
        backs = [after(v, *others) for v in done[step][0]] if others else done[step][0]
        back_home[step] = to_experts(backs)

    order = list(range(1, ne)) + [0]
    picked = {0: pick_chunk(0)}
    arrived[0] = to_experts(picked[0])
    if ne > 1:
        picked[1] = pick_chunk(1, picked[0][0])
    for _ in range(2, ne):
        ffn_moving.append(along(after(ffn_moving[-1], *arrived[0])))
    tick, outs = picked[0][0], []
    for step in range(ne):
        if step + 1 < ne:
            ready = picked[step + 1]
            arrived[step + 1] = to_experts([after(v, tick, *arrived[step]) for v in ready])
            tick = ready[0]
        if step + 2 < ne:
            picked[step + 2] = pick_chunk(step + 2, tick, *arrived[step])
            tick = picked[step + 2][0]
        tick = run_chunk(step, tick)
        outs.append(tick)
    waits = arrived[-1] + outs[-2:-1]
    for step in order:
        give_back(step, *waits)
        waits = back_home[step]

    all_rows, hidden_g, act_gate, act_up = ([d[1][n] for d in done] for n in range(4))
    work = [
        lambda t: grad_in_weight(all_rows, [after(v, t) for v in act_gate]),
        lambda t: grad_in_weight(all_rows, [after(v, t) for v in act_up]),
        lambda t: grad_down_weight(
            [after(v, t) for v in hidden_g], devices, cot_first, arrived[1:]
        ),
    ]
    grads, travelling = [], None
    for at, step in enumerate(order):
        waits = (tick,) if travelling is None else (tick, travelling)
        mine, theirs = combine_rows(send[step], [after(v, *waits) for v in back_home[step]])
        back_total = mine + mate(theirs).astype(F32)
        if travelling is not None:
            back_total = back_total + travelling.astype(F32)
        if at < ne - 1:
            tick = back_total.astype(BF)
            travelling = along(tick)
            if work:
                tick = work.pop(0)(tick)
                grads.append(tick)
    grad_gate, grad_up, grad_down = grads

    gates_home = gates_of(mm(ffn_in, router), chosen_home, False)
    grad_gates = back_total[:, D : D + experts]
    grad_logits = gates_home * (
        grad_gates - jnp.sum(gates_home * grad_gates, axis=-1, keepdims=True)
    )
    grad_logits_low = grad_logits.astype(BF)
    grad_ffn_in = back_total[:, :D] + nt_dot(grad_logits_low, router)
    scaled = grad_ffn_in * gain_ffn
    grad_residual = cotangent[0].astype(F32) + inv_res * (
        scaled - normed_res * jnp.mean(scaled * normed_res, axis=-1, keepdims=True)
    )
    grad_router = tn_dot(ffn_in, grad_logits_low)
    grad_gain_ffn = jnp.sum(grad_ffn_in * normed_res, axis=0)

    pieces = gather_ctx(grad_residual.astype(BF))
    small = jnp.concatenate(
        [grad_router.reshape(nc, ne, wrows * experts), grad_gain_ffn.reshape(nc, ne, gain_rows)],
        axis=2,
    )
    ends = small.shape[2]
    extra = -(-(-(-ends // total_width) + 1) // 8) * 8
    small = jnp.pad(small, ((0, 0), (0, 0), (0, (extra - 1) * total_width - ends)))
    small = small.transpose(1, 0, 2).astype(BF).reshape(ne, nc, extra - 1, total_width)
    pieces[0] = after(pieces[0], small)
    grad_output, grad_attn = branch_grads(attn, pieces, devices, w_out)
    orows = output_weight.shape[0]

    def output_part(step):
        return lax.dynamic_slice_in_dim(grad_output, ((ei - step) % ne) * orows, orows, 0)

    output_ring = [output_part(1 % ne)]
    for step in range(2, ne):
        output_ring.append(output_part(step) + along(output_ring[-1]))
    output_sum = output_part(0).astype(F32)
    if ne > 1:
        output_sum = output_sum + along(output_ring[-1]).astype(F32)

    mix_home, waits = [], pieces[1:]
    for blocks in mixed[:2]:
        waits = to_experts([after(v, *waits) for v in blocks])
        mix_home.append(waits)

    grad_q_low, grad_k, grad_v, grad_gain_query = attn_backward(
        q_raw, k_raw, v_raw, cos, sin, gain_query, gain_key, grad_attn, 0, heads, ()
    )
    grad_q_low, grad_k, grad_v, grad_gain_query, *_ = lax.optimization_barrier(
        (grad_q_low, grad_k, grad_v, grad_gain_query) + tuple(mix_home[0])
    )
    gks = [grad_k] + [mate(grad_k, bit) for bit in range(1, share)]
    gvs = [grad_v] + [mate(grad_v, bit) for bit in range(1, share)]
    grad_k_low, grad_v_low, grad_gain_key = key_backward(k_raw, cos, sin, gain_key, gks, gvs)
    grad_gain_key = jnp.where(member == 0, grad_gain_key, 0.0)
    grad_kv = jnp.concatenate([grad_k_low, grad_v_low], axis=1)
    if share > 1:
        grad_kv = lax.dynamic_slice_in_dim(grad_kv, member * piece, piece, 1)
    grad_in = jnp.concatenate([grad_q_low, grad_kv], axis=1)
    gains = jnp.concatenate(
        [
            grad_gain_query.reshape(nc, ne, head_rows),
            grad_gain_key.reshape(nc, ne, head_rows),
        ],
        axis=2,
    )
    gains = jnp.pad(gains, ((0, 0), (0, 0), (0, total_width - 2 * head_rows)))
    gains = gains.transpose(1, 0, 2).astype(BF).reshape(ne, nc, 1, total_width)
    local = projection_grads(xa, grad_in, nc, ne, (small, gains))
    grad_in = after(grad_in, local, output_ring[-1], *mix_home[1 % ne])
    waits = [grad_in]
    for blocks in mixed[2:]:
        waits = to_experts([after(v, *waits) for v in blocks])
        mix_home.append(waits)
    grad_w_sum = lax.psum_scatter(local, "exp", scatter_dimension=0, tiled=True)[0]
    grad_w = lax.all_to_all(
        grad_w_sum, "ctx", split_axis=0, concat_axis=0, tiled=True
    ).astype(F32)
    small = jnp.sum(grad_w[:, wrows:], axis=0)
    gains, small = small[-1], small[:-1].reshape(-1)
    grad_w = grad_w[:, :wrows]
    sum_query = grad_w[:, :, :width].transpose(1, 0, 2).reshape(wrows, H * HD)
    sum_kv = grad_w[:, :, width:].transpose(1, 0, 2).reshape(wrows, KVH, 2 * HD)
    sum_key = sum_kv[:, :, :HD].reshape(wrows, KVH * HD)
    sum_value = sum_kv[:, :, HD:].reshape(wrows, KVH * HD)
    sum_attn_gain = (
        jnp.sum(sum_query * query_weight.astype(F32), axis=1)
        + jnp.sum(sum_key * key_weight.astype(F32), axis=1)
        + jnp.sum(sum_value * value_weight.astype(F32), axis=1)
    ) / attn_gain.astype(F32)

    grad_xa, sent = scatter_ctx(grad_in, w_in, wrows, *mix_home[2 % ne], output_sum)
    mix_home[0][0] = after(mix_home[0][0], *sent)
    mine, theirs = combine_all(send, planes, mix_home)
    mixture = (mine.astype(F32) + mate(theirs).astype(F32)).astype(BF)
    mixture = after(mixture, grad_w_sum)
    mixture = lax.psum_scatter(mixture, "exp", scatter_dimension=0, tiled=True)[0].astype(F32)
    inv_in = inv_rms(inputs)
    normed_in = inputs * inv_in
    scaled_in = grad_xa * gain_attn
    grad_tokens = (
        grad_residual
        + inv_in
        * (scaled_in - normed_in * jnp.mean(scaled_in * normed_in, axis=-1, keepdims=True))
    )[None]

    layer_out = (residual + mixture).astype(BF)[None]

    router_size = wrows * experts
    return (
        layer_out,
        grad_tokens,
        sum_attn_gain,
        small[router_size : router_size + gain_rows],
        gains[:head_rows],
        gains[head_rows : 2 * head_rows],
        sum_query,
        sum_key,
        sum_value,
        output_sum,
        small[:router_size].reshape(wrows, experts),
        grad_gate[None],
        grad_up[None],
        grad_down[None],
    )


def solution(mesh):
    shard = ("ctx", "exp")
    rows = P("exp", "ctx", None)
    vector, matrix, stack = P(shard), P(shard, None), P(shard, None, None)
    return jax.shard_map(
        on_device,
        mesh=mesh,
        in_specs=(rows,) * 3 + (vector,) * 4 + (matrix,) * 5 + (stack,) * 3,
        out_specs=(rows,) * 2 + (vector,) * 4 + (matrix,) * 5 + (stack,) * 3,
        check_vma=False,
    )
```

```python
import jax
import jax.numpy as jnp
import numpy as np
from jax import lax
from jax.experimental import pallas as pl
from jax.experimental.pallas import tpu as pltpu
from jax.sharding import PartitionSpec as P

D = 2048
H = 32
KVH = 4
HD = 128
TOP = 8
BLK = 256

EPSILON = 1e-06
ROPE_BASE = 1000000.0
SCALE = HD**-0.5
BF = jnp.bfloat16
F32 = jnp.float32
MASKED = -1e30
VMEM_LIMIT = 48 * 1024 * 1024
ATTN_LIMIT = 24 * 1024 * 1024
SMALL = pl.CostEstimate(flops=1000, bytes_accessed=1000, transcendentals=0)
TILE = 512


def cost(micros):
    return pl.CostEstimate(flops=int(1.1e9 * micros), bytes_accessed=1000, transcendentals=0)


def rope_tables(rows):
    half = HD // 2
    freq = np.power(ROPE_BASE, np.arange(half) * (-2.0 / HD))
    angles = np.arange(rows)[:, None] * freq[None, :]
    cos, sin = np.cos(angles), np.sin(angles)
    return (
        np.concatenate([cos, cos], axis=1).astype(np.float32),
        np.concatenate([-sin, sin], axis=1).astype(np.float32),
    )


def inv_rms(values):
    return lax.rsqrt(jnp.mean(values * values, axis=-1, keepdims=True) + EPSILON)


def nt_dot(a, b):
    return lax.dot_general(a, b, (((1,), (1,)), ((), ())), preferred_element_type=F32)


def tn_dot(a, b):
    return lax.dot_general(a, b, (((0,), (0,)), ((), ())), preferred_element_type=F32)


def mm(a, b):
    return jnp.dot(a, b, preferred_element_type=F32)


def spin(values, cos, sin):
    return values * cos + pltpu.roll(values, HD // 2, 1) * sin


def unspin(values, cos, sin):
    return values * cos - pltpu.roll(values, HD // 2, 1) * sin


def attn_forward_kernel(blocks, raw, kraw, vraw, cos_all, sin_all, cos, sin, qgain, kgain, out, keys, vals):
    head, block = pl.program_id(0), pl.program_id(1)

    @pl.when((head == 0) & (block == 0))
    def _():
        rows = kraw[...]
        keys[...] = spin(rows * inv_rms(rows) * kgain[...], cos_all[...], sin_all[...]).astype(BF)
        vals[...] = vraw[...].astype(BF)

    rows = raw[...]
    query = spin(rows * inv_rms(rows) * qgain[...], cos[...], sin[...]).astype(BF)
    for n in range(blocks):

        @pl.when(block == n)
        def _(n=n):
            span = (n + 1) * BLK
            weights = jnp.exp(nt_dot(query, keys[:span, :]) * SCALE)
            total = jnp.sum(weights, axis=-1, keepdims=True)
            probs = (weights * (1.0 / total)).astype(BF)
            out[...] = mm(probs, vals[:span, :]).astype(BF)


def attn_backward_kernel(
    blocks, raw, kraw, vraw, cos_all, sin_all, cos, sin, qgain, kgain, gout, *rest
):
    *start, gq, gk, gv, gqgain, keys, vals = rest
    head, block = pl.program_id(0), pl.program_id(1)

    @pl.when((head == 0) & (block == 0))
    def _():
        rows = kraw[...]
        keys[...] = spin(rows * inv_rms(rows) * kgain[...], cos_all[...], sin_all[...]).astype(BF)
        vals[...] = vraw[...].astype(BF)
        for ref, first in zip((gk, gv, gqgain), start or (None,) * 3):
            ref[...] = jnp.zeros_like(ref) if first is None else first[...]

    rows = raw[...]
    inverse = inv_rms(rows)
    normed = rows * inverse
    query = spin(normed * qgain[...], cos[...], sin[...]).astype(BF)
    grad_out = gout[...]

    def finish(grad_query):
        turned = unspin(grad_query, cos[...], sin[...])
        gqgain[...] += jnp.sum(turned * normed, axis=0, keepdims=True)
        scaled = turned * qgain[...]
        mean = jnp.mean(scaled * normed, axis=-1, keepdims=True)
        gq[...] = (inverse * (scaled - normed * mean)).astype(BF)

    for n in range(blocks):

        @pl.when(block == n)
        def _(n=n):
            span = (n + 1) * BLK
            seen, values = keys[:span, :], vals[:span, :]
            weights = jnp.exp(nt_dot(query, seen) * SCALE)
            total = jnp.sum(weights, axis=-1, keepdims=True)
            probs = weights * (1.0 / total)
            grad_probs = nt_dot(grad_out, values)
            delta = jnp.sum(probs * grad_probs, axis=-1, keepdims=True)
            grad_scores = (probs * (grad_probs - delta)).astype(BF)
            gv[:span, :] += tn_dot(probs.astype(BF), grad_out)
            gk[:span, :] += tn_dot(grad_scores, query) * SCALE
            finish(mm(grad_scores, seen) * SCALE)


def key_backward_kernel(count, kraw, cos, sin, kgain, *rest):
    gks, gvs, (gk_low, gv_low, gkgain) = rest[:count], rest[count : 2 * count], rest[2 * count :]
    grad_keys, grad_vals = gks[0][...], gvs[0][...]
    for n in range(1, count):
        grad_keys = grad_keys + gks[n][...]
        grad_vals = grad_vals + gvs[n][...]
    rows = kraw[...]
    inverse = inv_rms(rows)
    normed = rows * inverse
    turned = unspin(grad_keys, cos[...], sin[...])
    gkgain[...] = jnp.sum(turned * normed, axis=0, keepdims=True)
    scaled = turned * kgain[...]
    mean = jnp.mean(scaled * normed, axis=-1, keepdims=True)
    gk_low[...] = (inverse * (scaled - normed * mean)).astype(BF)
    gv_low[...] = grad_vals.astype(BF)


def attn_specs(rows, first=0):
    return [
        pl.BlockSpec((BLK, HD), lambda h, i: (i, h + first)),
        pl.BlockSpec((rows, HD), lambda h, i: (0, 0)),
        pl.BlockSpec((rows, HD), lambda h, i: (0, 0)),
        pl.BlockSpec((rows, HD), lambda h, i: (0, 0)),
        pl.BlockSpec((rows, HD), lambda h, i: (0, 0)),
        pl.BlockSpec((BLK, HD), lambda h, i: (i, 0)),
        pl.BlockSpec((BLK, HD), lambda h, i: (i, 0)),
        pl.BlockSpec((1, HD), lambda h, i: (0, 0)),
        pl.BlockSpec((1, HD), lambda h, i: (0, 0)),
    ]


def attn_forward(raw, kraw, vraw, cos, sin, qgain, kgain, first, heads):
    rows = raw.shape[0]
    blocks = rows // BLK
    return pl.pallas_call(
        lambda *refs: attn_forward_kernel(blocks, *refs),
        grid=(heads, blocks),
        in_specs=attn_specs(rows, first),
        out_specs=pl.BlockSpec((BLK, HD), lambda h, i: (i, h)),
        out_shape=jax.ShapeDtypeStruct((rows, heads * HD), BF),
        scratch_shapes=[pltpu.VMEM((rows, HD), BF), pltpu.VMEM((rows, HD), BF)],
        compiler_params=pltpu.CompilerParams(vmem_limit_bytes=ATTN_LIMIT),
        cost_estimate=cost(13),
        name="attn_fw",
    )(raw, kraw, vraw, cos, sin, cos, sin, qgain, kgain)


def attn_backward(raw, kraw, vraw, cos, sin, qgain, kgain, gout, first, heads, start):
    rows = raw.shape[0]
    blocks = rows // BLK
    return pl.pallas_call(
        lambda *refs: attn_backward_kernel(blocks, *refs),
        grid=(heads, blocks),
        in_specs=attn_specs(rows, first)
        + [pl.BlockSpec((BLK, HD), lambda h, i: (i, h + first))]
        + [pl.BlockSpec(v.shape, lambda h, i: (0, 0)) for v in start],
        out_specs=[
            pl.BlockSpec((BLK, HD), lambda h, i: (i, h)),
            pl.BlockSpec((rows, HD), lambda h, i: (0, 0)),
            pl.BlockSpec((rows, HD), lambda h, i: (0, 0)),
            pl.BlockSpec((1, HD), lambda h, i: (0, 0)),
        ],
        out_shape=[
            jax.ShapeDtypeStruct((rows, heads * HD), BF),
            jax.ShapeDtypeStruct((rows, HD), F32),
            jax.ShapeDtypeStruct((rows, HD), F32),
            jax.ShapeDtypeStruct((1, HD), F32),
        ],
        scratch_shapes=[pltpu.VMEM((rows, HD), BF), pltpu.VMEM((rows, HD), BF)],
        compiler_params=pltpu.CompilerParams(vmem_limit_bytes=ATTN_LIMIT),
        cost_estimate=cost(22),
        name="attn_bw",
    )(raw, kraw, vraw, cos, sin, cos, sin, qgain, kgain, gout, *start)


def key_backward(kraw, cos, sin, kgain, gks, gvs):
    rows = kraw.shape[0]
    return pl.pallas_call(
        lambda *refs: key_backward_kernel(len(gks), *refs),
        out_shape=[
            jax.ShapeDtypeStruct((rows, HD), BF),
            jax.ShapeDtypeStruct((rows, HD), BF),
            jax.ShapeDtypeStruct((1, HD), F32),
        ],
        compiler_params=pltpu.CompilerParams(vmem_limit_bytes=ATTN_LIMIT),
        cost_estimate=cost(2),
        name="key_bw",
    )(kraw, cos, sin, kgain, *gks, *gvs)


def call(kernel, name, out_shape, micros=0, **kw):
    return pl.pallas_call(
        kernel,
        out_shape=out_shape,
        compiler_params=pltpu.CompilerParams(vmem_limit_bytes=VMEM_LIMIT),
        cost_estimate=cost(micros) if micros else SMALL,
        name=name,
        **kw,
    )


def whole(values):
    return pl.BlockSpec(values.shape, lambda *_: (0,) * values.ndim)


def column_tile(height):
    return pl.BlockSpec((height, TILE), lambda j: (0, j))


def routing(ids, place, ne, experts, cap):
    nc, _, rows = ids.shape
    nchip = nc // 2
    block = 2 * cap

    def kernel(at, ids_ref, send, direct, chosen, spots, named):
        chip, core, ci, ei = at[0], at[1], at[2], at[3]
        number = lax.broadcasted_iota(jnp.int32, (experts, rows), 0)
        slot = lax.broadcasted_iota(jnp.int32, (cap, rows), 0).astype(F32)
        lower = (
            lax.broadcasted_iota(jnp.int32, (rows, rows), 0)
            < lax.broadcasted_iota(jnp.int32, (rows, rows), 1)
        ).astype(BF)
        for dev in range(nc):
            got = ids_ref[dev]
            hits = jnp.zeros((experts, rows), F32)
            for k in range(TOP):
                hits = hits + (got[k : k + 1, :] == number).astype(F32)
            named[dev] = hits.astype(BF)
            spots[dev] = jnp.where(hits > 0.5, mm(hits.astype(BF), lower), -1.0)

        def slots_of(dev, expert):
            line = jnp.sum(jnp.where(number == expert, spots[dev], 0.0), axis=0, keepdims=True)
            return (line == slot).astype(BF)

        for m in range(nchip):
            expert = ((chip ^ m) * 2 + core) * ne + ei
            send[m] = jnp.zeros((block, 2 * rows), BF)
            send[m, :cap, :rows] = slots_of(ci, expert)
            send[m, cap:, rows:] = slots_of(ci ^ 1, expert)
            for src in range(2):
                dev = (chip ^ m) * 2 + (core ^ src)
                taken = slots_of(dev, ci * ne + ei)
                first = (m * 2 + src) * cap
                chosen[first : first + cap, :] = nt_dot(taken, named[dev])
        for dev in range(nc):
            direct[dev] = slots_of(ci, dev * ne + ei)

    return pl.pallas_call(
        kernel,
        out_shape=[
            jax.ShapeDtypeStruct((nchip, block, 2 * rows), BF),
            jax.ShapeDtypeStruct((nc, cap, rows), BF),
            jax.ShapeDtypeStruct((nc * cap, experts), F32),
        ],
        in_specs=[pl.BlockSpec(memory_space=pltpu.SMEM), pl.BlockSpec(memory_space=pltpu.VMEM)],
        scratch_shapes=[
            pltpu.VMEM((nc, experts, rows), F32),
            pltpu.VMEM((nc, experts, rows), BF),
        ],
        compiler_params=pltpu.CompilerParams(vmem_limit_bytes=ATTN_LIMIT),
        cost_estimate=SMALL,
        name="routing",
    )(place, ids)


def select_direct(direct, planes, values):
    steps, (nc, cap, rows) = len(direct), direct[0].shape

    def kernel(at, *refs):
        tokens, out = refs[steps], refs[steps + 1]
        for n in range(steps):
            part = tokens[at[n]]
            for dev in range(nc):
                out[dev, n * cap : (n + 1) * cap, :] = mm(refs[n][dev], part).astype(BF)

    return call(
        kernel,
        "select_direct",
        micros=3,
        out_shape=jax.ShapeDtypeStruct((nc, steps * cap, D), BF),
        grid=(D // TILE,),
        in_specs=[pl.BlockSpec(memory_space=pltpu.SMEM)]
        + [whole(v) for v in direct]
        + [pl.BlockSpec((values.shape[0], rows, TILE), lambda j: (0, 0, j))],
        out_specs=pl.BlockSpec((nc, steps * cap, TILE), lambda j: (0, 0, j)),
    )(planes, *direct, values)


def select_rows(send, values, mates):
    nchip, block, _ = send.shape
    rows, count = values[0].shape[0], len(values)

    def kernel(picks, *refs):
        outs = refs[2 * count :]
        for n in range(count):
            pair = jnp.concatenate([refs[n][...], refs[count + n][...]], axis=0)
            for m in range(nchip):
                outs[m][n] = mm(picks[m], pair).astype(BF)

    return call(
        kernel,
        "select_rows",
        out_shape=[jax.ShapeDtypeStruct((count, block, D), BF)] * nchip,
        grid=(D // TILE,),
        in_specs=[whole(send)] + [column_tile(rows)] * (2 * count),
        out_specs=[pl.BlockSpec((count, block, TILE), lambda j: (0, 0, j))] * nchip,
    )(send, *values, *mates)


def combine_rows(send, home):
    nchip, block, _ = send.shape
    rows, wide = send.shape[2] // 2, home[0].shape[1]

    def kernel(picks, *refs):
        blocks, mine, theirs = refs[:nchip], refs[nchip], refs[nchip + 1]
        got = jnp.concatenate([b[...] for b in blocks], axis=0)
        chosen = jnp.concatenate([picks[m] for m in range(nchip)], axis=0)
        both = tn_dot(chosen, got)
        mine[...] = both[:rows]
        theirs[...] = both[rows:].astype(BF)

    return call(
        kernel,
        "combine_rows",
        micros=3,
        out_shape=[jax.ShapeDtypeStruct((rows, wide), F32), jax.ShapeDtypeStruct((rows, wide), BF)],
    )(send, *home)


def combine_all(send, planes, home):
    ne, (nchip, block, wide) = len(send), send[0].shape
    rows = wide // 2

    def kernel(at, *refs):
        mine, theirs = refs[-2:]
        for step in range(ne):
            blocks = refs[ne + step * nchip : ne + (step + 1) * nchip]
            got = jnp.concatenate([b[...] for b in blocks], axis=0)
            chosen = jnp.concatenate([refs[step][m] for m in range(nchip)], axis=0)
            both = tn_dot(chosen, got).astype(BF)
            mine[at[step]] = both[:rows]
            theirs[at[step]] = both[rows:]

    return call(
        kernel,
        "combine_all",
        micros=6,
        out_shape=[jax.ShapeDtypeStruct((ne, rows, D), BF)] * 2,
        grid=(D // TILE,),
        in_specs=[pl.BlockSpec(memory_space=pltpu.SMEM)]
        + [whole(v) for v in send]
        + [column_tile(block)] * (ne * nchip),
        out_specs=[pl.BlockSpec((ne, rows, TILE), lambda j: (0, 0, j))] * 2,
    )(planes, *send, *(v for blocks in home for v in blocks))


def expert_rows(rows_in, cot_in, devices, row_chosen, router, column, lane, weights):
    nchip, (both, block, _) = len(rows_in), rows_in[0].shape
    nc, cap = 2 * nchip, block // 2
    cots = 0 if both > 1 else nc
    slots, lanes, hidden_size = nchip * block, lane.shape[1], weights[0].shape[1]

    def kernel(_, *refs):
        ffn_in, cot_refs = refs[:nchip], refs[nchip : nchip + cots]
        chosen_ref, router_ref, column_ref, lane_ref, w_gate, w_up, w_down = refs[
            nchip + cots : nchip + cots + 7
        ]
        outs = refs[nchip + cots + 7 :]
        backs, mixes, kept = outs[:nchip], outs[nchip : 2 * nchip], outs[2 * nchip :]
        all_out, hidden_out, gate_out, up_out = kept
        rows = jnp.concatenate([r[0] for r in ffn_in], axis=0)
        cot = jnp.concatenate([r[0] for r in cot_refs] or [r[1] for r in ffn_in], axis=0)
        all_out[...] = rows
        gates = gates_of(mm(rows, router_ref[...]), chosen_ref[...] > 0.5, True)
        gate_vec = jnp.sum(gates * column_ref[...], axis=-1, keepdims=True)
        gate_act = mm(rows, w_gate[...])
        up_act = mm(rows, w_up[...])
        upstream = nt_dot(cot, w_down[...])
        sig = 1.0 / (1.0 + jnp.exp(-gate_act))
        silu = gate_act * sig
        hidden = (silu * up_act).astype(BF).astype(F32)
        score = jnp.sum(upstream * hidden, axis=-1, keepdims=True)
        gated = (hidden * gate_vec).astype(BF)
        hidden_out[...] = gated
        grad_hidden = upstream * gate_vec
        grad_gate = (grad_hidden * up_act * sig * (1.0 + gate_act * (1.0 - sig))).astype(BF)
        grad_up = (grad_hidden * silu).astype(BF)
        gate_out[...] = grad_gate
        up_out[...] = grad_up
        back = (nt_dot(grad_gate, w_gate[...]) + nt_dot(grad_up, w_up[...])).astype(BF)
        scores = (score * lane_ref[...]).astype(BF)
        for m in range(nchip):
            part = slice(m * block, (m + 1) * block)
            backs[m][:, :D] = back[part]
            backs[m][:, D:] = scores[part]
            mixes[m][...] = mm(gated[part], w_down[...]).astype(BF)

    narrow = jax.ShapeDtypeStruct((slots, hidden_size), BF)
    out_shape = [jax.ShapeDtypeStruct((block, D + lanes), BF)] * nchip
    out_shape += [jax.ShapeDtypeStruct((block, D), BF)] * nchip + [
        jax.ShapeDtypeStruct((slots, D), BF),
        narrow,
        narrow,
        narrow,
    ]
    fixed = [row_chosen, router, column, lane, *weights]
    outs = call(
        kernel,
        "expert_rows",
        micros=2,
        out_shape=out_shape,
        grid_spec=pltpu.PrefetchScalarGridSpec(
            num_scalar_prefetch=1,
            grid=(1,),
            in_specs=[whole(r) for r in rows_in]
            + [
                pl.BlockSpec((1, cap, D), lambda i, at, n=n: (at[n], 0, 0))
                for n in range(cots)
            ]
            + [whole(v) for v in fixed],
            out_specs=[whole(v) for v in out_shape],
        ),
    )(devices, *rows_in, *([cot_in] * cots), *fixed)
    return outs[:nchip], outs[nchip : 2 * nchip], outs[2 * nchip :]


def grad_in_weight(rows, grads):
    chunks, slots, size = len(rows), rows[0].shape[0], grads[0].shape[1]

    def kernel(*refs):
        total = tn_dot(refs[0][...], refs[chunks][...])
        for n in range(1, chunks):
            total += tn_dot(refs[n][...], refs[chunks + n][...])
        refs[2 * chunks][...] = total

    return call(
        kernel,
        "grad_in_weight",
        micros=10,
        out_shape=jax.ShapeDtypeStruct((D, size), F32),
        grid=(D // TILE,),
        in_specs=[column_tile(slots)] * chunks + [whole(v) for v in grads],
        out_specs=pl.BlockSpec((TILE, size), lambda i: (i, 0)),
    )(*rows, *grads)


def grad_down_weight(hidden, devices, cot_first, later):
    chunks = len(hidden)
    (nc, cap, _), size = cot_first.shape, hidden[0].shape[1]
    nchip = nc // 2

    def kernel(at, *refs):
        hid, early, late, out = refs[:chunks], refs[chunks], refs[chunks + 1 : -1], refs[-1]
        total = None
        for n in range(chunks):
            if n:
                rows = [r[0] for r in late[(n - 1) * nchip : n * nchip]]
            else:
                rows = [early[at[i]] for i in range(nc)]
            part = tn_dot(hid[n][...], jnp.concatenate(rows, axis=0))
            total = part if total is None else total + part
        out[...] = total

    late = [v for blocks in later for v in blocks]
    return call(
        kernel,
        "grad_down_weight",
        micros=10,
        out_shape=jax.ShapeDtypeStruct((size, D), F32),
        grid=(D // TILE,),
        in_specs=[pl.BlockSpec(memory_space=pltpu.SMEM)]
        + [whole(v) for v in hidden]
        + [pl.BlockSpec((nc, cap, TILE), lambda j: (0, 0, j))]
        + [pl.BlockSpec((1, 2 * cap, TILE), lambda j: (1, 0, j))] * len(late),
        out_specs=column_tile(size),
    )(devices, *hidden, cot_first, *late)


def project(x_all, gain, weight, wrows):
    rows, size = x_all.shape[0], weight.shape[3]

    def kernel(x, gain_ref, w, normed, raw):
        values = x[...].astype(F32)
        low = (values * inv_rms(values) * gain_ref[...]).astype(BF)
        normed[...] = low
        raw[...] = mm(low, w[:, :, :wrows, :].reshape(D, size))

    band = pl.BlockSpec((BLK, D), lambda i: (i, 0))
    return call(
        kernel,
        "project",
        micros=6,
        out_shape=[jax.ShapeDtypeStruct((rows, D), BF), jax.ShapeDtypeStruct((rows, size), F32)],
        grid=(rows // BLK,),
        in_specs=[band, whole(gain), whole(weight)],
        out_specs=[band, pl.BlockSpec((BLK, size), lambda i: (i, 0))],
    )(x_all, gain, weight)


def part_product(values, index, rows, weight, wrows, theirs, dtype):
    size = values.shape[1]
    extra = [] if theirs is None else [theirs]

    def kernel(_, part, w, *refs):
        if wrows:
            out = nt_dot(part[...], w[:, :, :wrows, :].reshape(TILE, size))
        else:
            out = mm(part[...], w[...])
        if theirs is not None:
            out = out + refs[0][...].astype(F32)
        refs[-1][...] = out.astype(dtype)

    if wrows:
        shape = (TILE // (weight.shape[1] * wrows),) + weight.shape[1:]
        weight_spec = pl.BlockSpec(shape, lambda j, at: (j, 0, 0, 0))
    else:
        weight_spec = pl.BlockSpec((size, TILE), lambda j, at: (0, j))
    column = pl.BlockSpec((rows, TILE), lambda j, at: (0, j))
    return call(
        kernel,
        "part_product",
        micros=2,
        out_shape=jax.ShapeDtypeStruct((rows, D), dtype),
        grid_spec=pltpu.PrefetchScalarGridSpec(
            num_scalar_prefetch=1,
            grid=(D // TILE,),
            in_specs=[pl.BlockSpec((rows, size), lambda j, at: (at[0], 0)), weight_spec]
            + [column] * len(extra),
            out_specs=column,
        ),
    )(index.reshape(1), values, weight, *extra)


def branch_grads(attn, pieces, devices, weight):
    (rows, size), height = attn.shape, pieces[0].shape[0]

    def kernel(at, a, w, *refs):
        parts, (to_weight, to_attn, whole_g) = refs[: len(pieces)], refs[len(pieces) :]
        for n, part in enumerate(parts):
            first = pl.multiple_of(at[n] * height, height)
            whole_g[pl.ds(first, height), :] = part[...]
        for n in range(0, D, TILE):
            to_weight[:, n : n + TILE] = tn_dot(a[...], whole_g[:, n : n + TILE]).astype(BF)
        for n in range(0, rows, BLK):
            to_attn[n : n + BLK, :] = nt_dot(whole_g[n : n + BLK, :], w[...]).astype(BF)

    outs = [jax.ShapeDtypeStruct((size, D), BF), jax.ShapeDtypeStruct((rows, size), BF)]
    return call(
        kernel,
        "branch_grads",
        micros=12,
        out_shape=outs,
        grid=(1,),
        in_specs=[pl.BlockSpec(memory_space=pltpu.SMEM)]
        + [whole(v) for v in (attn, weight, *pieces)],
        out_specs=[whole(v) for v in outs],
        scratch_shapes=[pltpu.VMEM((rows, D), BF)],
    )(devices, attn, weight, *pieces)


def projection_grads(xa, grads, nc, ne, small=None):
    rows, wrows, size = xa.shape[0], D // (nc * ne), grads.shape[1]
    more = [] if small is None else list(small)
    high = wrows + sum(v.shape[2] for v in more)

    def kernel(x, g, *refs):
        out = refs[-1]
        out[:, :, :wrows, :] = tn_dot(x[...], g[...]).astype(BF).reshape(ne, 1, wrows, size)
        if small is not None:
            out[:, :, wrows:, :] = jnp.concatenate([refs[0][...], refs[1][...]], axis=2)

    return call(
        kernel,
        "projection_grads",
        micros=2,
        out_shape=jax.ShapeDtypeStruct((ne, nc, high, size), BF),
        grid=(nc,),
        in_specs=[pl.BlockSpec((rows, ne * wrows), lambda i: (0, i)), whole(grads)]
        + [pl.BlockSpec((ne, 1) + v.shape[2:], lambda i: (0, i, 0, 0)) for v in more],
        out_specs=pl.BlockSpec((ne, 1, high, size), lambda i: (0, i, 0, 0)),
    )(xa, grads, *more)


def gates_of(logits, chosen, empty):
    top = jnp.max(jnp.where(chosen, logits, MASKED), axis=-1, keepdims=True)
    raised = jnp.where(chosen, jnp.exp(jnp.where(chosen, logits - top, 0.0)), 0.0)
    total = jnp.sum(raised, axis=-1, keepdims=True)
    return raised / (jnp.where(total > 0.0, total, 1.0) if empty else total)


def on_device(
    tokens,
    expert_ids,
    cotangent,
    attn_gain,
    ffn_gain,
    query_gain,
    key_gain,
    query_weight,
    key_weight,
    value_weight,
    output_weight,
    router_weight,
    gate_weight,
    up_weight,
    down_weight,
):
    both = ("ctx", "exp")
    nc, ne = lax.axis_size("ctx"), lax.axis_size("exp")
    ci, ei = lax.axis_index("ctx"), lax.axis_index("exp")
    chip, core = ci // 2, ci % 2
    nchip = nc // 2
    count = nc * ne
    rows = tokens.shape[1]
    seq = rows * nc
    heads = H // nc
    width = heads * HD
    share = nc // KVH
    piece = 2 * HD // share
    member = ci % share
    experts = router_weight.shape[1]
    lanes = -(-experts // 128) * 128
    cap = -(-max(2, rows * TOP * 3 // (2 * experts)) // 8) * 8
    block = 2 * cap
    slots = nchip * block
    wrows = query_weight.shape[0]
    gain_rows, head_rows = attn_gain.shape[0], query_gain.shape[0]

    def mate(values, bit=1):
        return lax.ppermute(values, "ctx", [(i, i ^ bit) for i in range(nc)])

    def peer(values, step):
        return mate(values, 2 * step) if step else values

    def along(values):
        return lax.ppermute(values, "exp", [(i, (i + 1) % ne) for i in range(ne)])

    def after(values, *others):
        return lax.optimization_barrier((values,) + others)[0]

    def place(step, other):
        return (chip ^ step) * 2 + (1 - core if other else core)

    def gather_ctx(values):
        got = [values] + [None] * (nchip - 1)
        for step in range(nchip - 1, 0, -1):
            got[step] = peer(values, step)
        return [v for part in got for v in (part, mate(part))]

    def scatter_ctx(values, weight, height, *late):
        def part(step, other, theirs, dtype):
            return part_product(values, place(step, other), rows, weight, height, theirs, dtype)

        arrived, sent = [], []
        for step in list(range(nchip - 1, 0, -1)) + [0]:
            theirs = after(mate(part(step, True, None, BF)), *late)
            mine = part(step, False, theirs, BF if step else F32)
            sent.append(mine)
            if step:
                arrived.append(peer(mine, step))
        total = mine
        for values in arrived:
            total = total + values.astype(F32)
        return total, sent

    own_tokens = tokens[0]
    x_all = lax.all_gather(own_tokens, "ctx", axis=0, tiled=True)
    w_out = lax.all_gather(after(output_weight, x_all), "exp", axis=0, tiled=True)
    total_width = width + piece
    packed = jnp.concatenate(
        [
            expert_ids[0].T.astype(BF).reshape(-1),
            attn_gain,
            ffn_gain,
            query_gain,
            key_gain,
            router_weight.reshape(-1),
        ]
    )
    more = -(-packed.shape[0] // (8 * total_width)) * 8
    packed = jnp.pad(packed, (0, more * total_width - packed.shape[0]))
    kv = jnp.concatenate(
        [key_weight.reshape(wrows, KVH, HD), value_weight.reshape(wrows, KVH, HD)], axis=2
    ).reshape(wrows, nc, piece)
    part = jnp.concatenate([query_weight.reshape(wrows, nc, width), kv], axis=2)
    part = jnp.concatenate(
        [
            part.transpose(1, 0, 2),
            jnp.broadcast_to(packed.reshape(1, more, total_width), (nc, more, total_width)),
        ],
        axis=1,
    )
    part = lax.all_to_all(part, "ctx", split_axis=0, concat_axis=0, tiled=True)

    spot = jnp.stack([chip, core, ci, ei]).astype(jnp.int32)
    index = lax.iota(jnp.int32, nc)
    devices = (chip ^ (index // 2)) * 2 + (core ^ (index % 2))
    planes = (ei - lax.iota(jnp.int32, ne)) % ne
    moving, send, direct, row_chosen = part, [], [], []
    w_in = jnp.zeros((nc, ne, wrows + more, total_width), BF)
    for step in range(ne):
        if step:
            moving = along(moving)
        w_in = lax.dynamic_update_slice(w_in, moving[:, None], (0, (ei - step) % ne, 0, 0))
        ids = moving[:, wrows:].reshape(nc, more * total_width)[:, : TOP * rows]
        ids = ids.reshape(nc, TOP, rows).astype(jnp.int32)
        if step:
            ids = after(ids, row_chosen[-1])
        else:
            own_ids = ids
        for into, values in zip(
            (send, direct, row_chosen), routing(ids, spot, ne, experts, cap)
        ):
            into.append(values)
        if step == 0:
            cot_first = select_direct(direct, jnp.zeros((1,), jnp.int32), cotangent)
            cot_first = lax.all_to_all(
                cot_first, "ctx", split_axis=0, concat_axis=0, tiled=True
            )
    table = w_in[:, :, wrows:].reshape(count, more * total_width)
    cuts = np.cumsum(
        [TOP * rows, gain_rows, gain_rows, head_rows, head_rows, wrows * experts]
    ).tolist()
    gain_attn = table[:, cuts[0] : cuts[1]].reshape(1, D).astype(F32)
    gain_ffn = table[:, cuts[1] : cuts[2]].reshape(1, D).astype(F32)
    gain_query = table[:, cuts[2] : cuts[3]].reshape(1, HD).astype(F32)
    gain_key = table[:, cuts[3] : cuts[4]].reshape(1, HD).astype(F32)
    router = table[:, cuts[4] : cuts[5]].reshape(D, experts)
    own_ids = lax.dynamic_index_in_dim(own_ids, ci, 0, keepdims=False)
    chosen_home = jnp.any(
        own_ids.T[:, :, None] == lax.iota(jnp.int32, experts)[None, None, :], axis=1
    )
    cot_all = lax.all_gather(
        after(cotangent[0], moving, w_out), "exp", axis=0, tiled=False
    )

    def to_experts(picked):
        return [peer(picked[m], m) for m in range(nchip - 1, -1, -1)][::-1]

    cos, sin = (jnp.asarray(v) for v in rope_tables(seq))
    x_all = after(x_all, cot_first, send[max(0, ne - 2)], row_chosen[max(0, ne - 2)])
    xa, raw = project(x_all, gain_attn, w_in, wrows)
    q_raw = raw[:, :width]
    kv_own = raw[:, width:]
    kv_parts = [kv_own] + [mate(kv_own, bit) for bit in range(1, share)]
    ordered = []
    for spot in range(share):
        chosen = kv_parts[spot]
        for m in range(1, share):
            chosen = jnp.where(member == m, kv_parts[spot ^ m], chosen)
        ordered.append(chosen)
    kv_raw = jnp.concatenate(ordered, axis=1) if share > 1 else ordered[0]
    k_raw, v_raw = kv_raw[:, :HD], kv_raw[:, HD:]
    attn = attn_forward(q_raw, k_raw, v_raw, cos, sin, gain_query, gain_key, 0, heads)
    w_gate, w_up, w_down = gate_weight[0], up_weight[0], down_weight[0]
    cot_all = after(cot_all, attn)
    cot_moving = [
        lax.dynamic_index_in_dim(cot_all, (ei - step) % ne, 0, keepdims=False)
        for step in range(ne)
    ]
    cot_mates = [mate(v) for v in cot_moving]
    inputs = own_tokens.astype(F32)
    residual = inputs + scatter_ctx(attn, w_out, 0)[0]
    inv_res = inv_rms(residual)
    normed_res = residual * inv_res
    ffn_in = (normed_res * gain_ffn).astype(BF)

    lane = (lax.iota(jnp.int32, lanes)[None, :] == ci * ne + ei).astype(F32)
    column = lane[:, :experts]
    ffn_moving = [ffn_in]
    for _ in range(1, min(ne, 2)):
        ffn_moving.append(along(ffn_moving[-1]))
    arrived, done, mixed, back_home = [None] * ne, [], [], {}

    def pick_chunk(step, *others):
        values = [after(ffn_moving[step], *others)]
        mates = [mate(values[0])]
        if step:
            values.append(cot_moving[step])
            mates.append(cot_mates[step])
        return select_rows(send[step], values, mates)

    def run_chunk(step, *others):
        rows_in = [after(v, *others) for v in arrived[step]]
        backs, mixes, kept = expert_rows(
            rows_in, cot_first, devices, row_chosen[step], router, column, lane,
            (w_gate, w_up, w_down),
        )
        done.append((backs, kept))
        mixed.append(mixes)
        return kept[0]

    def give_back(step, *others):
        backs = [after(v, *others) for v in done[step][0]] if others else done[step][0]
        back_home[step] = to_experts(backs)

    order = list(range(1, ne)) + [0]
    picked = {0: pick_chunk(0)}
    arrived[0] = to_experts(picked[0])
    if ne > 1:
        picked[1] = pick_chunk(1, picked[0][0])
    for _ in range(2, ne):
        ffn_moving.append(along(after(ffn_moving[-1], *arrived[0])))
    tick, outs = picked[0][0], []
    for step in range(ne):
        if step + 1 < ne:
            ready = picked[step + 1]
            arrived[step + 1] = to_experts([after(v, tick, *arrived[step]) for v in ready])
            tick = ready[0]
        if step + 2 < ne:
            picked[step + 2] = pick_chunk(step + 2, tick, *arrived[step])
            tick = picked[step + 2][0]
        tick = run_chunk(step, tick)
        outs.append(tick)
    waits = arrived[-1] + outs[-2:-1]
    for step in order:
        give_back(step, *waits)
        waits = back_home[step]

    all_rows, hidden_g, act_gate, act_up = ([d[1][n] for d in done] for n in range(4))
    work = [
        lambda t: grad_in_weight(all_rows, [after(v, t) for v in act_gate]),
        lambda t: grad_in_weight(all_rows, [after(v, t) for v in act_up]),
        lambda t: grad_down_weight(
            [after(v, t) for v in hidden_g], devices, cot_first, arrived[1:]
        ),
    ]
    grads, travelling = [], None
    for at, step in enumerate(order):
        waits = (tick,) if travelling is None else (tick, travelling)
        mine, theirs = combine_rows(send[step], [after(v, *waits) for v in back_home[step]])
        back_total = mine + mate(theirs).astype(F32)
        if travelling is not None:
            back_total = back_total + travelling.astype(F32)
        if at < ne - 1:
            tick = back_total.astype(BF)
            travelling = along(tick)
            if work:
                tick = work.pop(0)(tick)
                grads.append(tick)
    grad_gate, grad_up, grad_down = grads

    gates_home = gates_of(mm(ffn_in, router), chosen_home, False)
    grad_gates = back_total[:, D : D + experts]
    grad_logits = gates_home * (
        grad_gates - jnp.sum(gates_home * grad_gates, axis=-1, keepdims=True)
    )
    grad_logits_low = grad_logits.astype(BF)
    grad_ffn_in = back_total[:, :D] + nt_dot(grad_logits_low, router)
    scaled = grad_ffn_in * gain_ffn
    grad_residual = cotangent[0].astype(F32) + inv_res * (
        scaled - normed_res * jnp.mean(scaled * normed_res, axis=-1, keepdims=True)
    )
    grad_router = tn_dot(ffn_in, grad_logits_low)
    grad_gain_ffn = jnp.sum(grad_ffn_in * normed_res, axis=0)

    pieces = gather_ctx(grad_residual.astype(BF))
    small = jnp.concatenate(
        [grad_router.reshape(nc, ne, wrows * experts), grad_gain_ffn.reshape(nc, ne, gain_rows)],
        axis=2,
    )
    ends = small.shape[2]
    extra = -(-(-(-ends // total_width) + 1) // 8) * 8
    small = jnp.pad(small, ((0, 0), (0, 0), (0, (extra - 1) * total_width - ends)))
    small = small.transpose(1, 0, 2).astype(BF).reshape(ne, nc, extra - 1, total_width)
    pieces[0] = after(pieces[0], small)
    grad_output, grad_attn = branch_grads(attn, pieces, devices, w_out)
    output_sum = lax.psum_scatter(grad_output, "exp", scatter_dimension=0, tiled=True)

    mix_home, waits = [], pieces[1:]
    for blocks in mixed[:2]:
        waits = to_experts([after(v, *waits) for v in blocks])
        mix_home.append(waits)

    grad_q_low, grad_k, grad_v, grad_gain_query = attn_backward(
        q_raw, k_raw, v_raw, cos, sin, gain_query, gain_key, grad_attn, 0, heads, ()
    )
    grad_q_low, grad_k, grad_v, grad_gain_query, *_ = lax.optimization_barrier(
        (grad_q_low, grad_k, grad_v, grad_gain_query) + tuple(mix_home[0])
    )
    gks = [grad_k] + [mate(grad_k, bit) for bit in range(1, share)]
    gvs = [grad_v] + [mate(grad_v, bit) for bit in range(1, share)]
    grad_k_low, grad_v_low, grad_gain_key = key_backward(k_raw, cos, sin, gain_key, gks, gvs)
    grad_gain_key = jnp.where(member == 0, grad_gain_key, 0.0)
    grad_kv = jnp.concatenate([grad_k_low, grad_v_low], axis=1)
    if share > 1:
        grad_kv = lax.dynamic_slice_in_dim(grad_kv, member * piece, piece, 1)
    grad_in = jnp.concatenate([grad_q_low, grad_kv], axis=1)
    gains = jnp.concatenate(
        [
            grad_gain_query.reshape(nc, ne, head_rows),
            grad_gain_key.reshape(nc, ne, head_rows),
        ],
        axis=2,
    )
    gains = jnp.pad(gains, ((0, 0), (0, 0), (0, total_width - 2 * head_rows)))
    gains = gains.transpose(1, 0, 2).astype(BF).reshape(ne, nc, 1, total_width)
    local = projection_grads(xa, grad_in, nc, ne, (small, gains))
    grad_in = after(grad_in, local, *mix_home[1 % ne])
    waits = [grad_in]
    for blocks in mixed[2:]:
        waits = to_experts([after(v, *waits) for v in blocks])
        mix_home.append(waits)
    local = after(local, output_sum, *mix_home[1 % ne])
    grad_w_sum = lax.psum_scatter(local, "exp", scatter_dimension=0, tiled=True)[0]
    grad_w = lax.all_to_all(
        grad_w_sum, "ctx", split_axis=0, concat_axis=0, tiled=True
    ).astype(F32)
    small = jnp.sum(grad_w[:, wrows:], axis=0)
    gains, small = small[-1], small[:-1].reshape(-1)
    grad_w = grad_w[:, :wrows]
    sum_query = grad_w[:, :, :width].transpose(1, 0, 2).reshape(wrows, H * HD)
    sum_kv = grad_w[:, :, width:].transpose(1, 0, 2).reshape(wrows, KVH, 2 * HD)
    sum_key = sum_kv[:, :, :HD].reshape(wrows, KVH * HD)
    sum_value = sum_kv[:, :, HD:].reshape(wrows, KVH * HD)
    sum_attn_gain = (
        jnp.sum(sum_query * query_weight.astype(F32), axis=1)
        + jnp.sum(sum_key * key_weight.astype(F32), axis=1)
        + jnp.sum(sum_value * value_weight.astype(F32), axis=1)
    ) / attn_gain.astype(F32)

    grad_xa, sent = scatter_ctx(grad_in, w_in, wrows, *mix_home[2 % ne])
    mix_home[0][0] = after(mix_home[0][0], *sent)
    mine, theirs = combine_all(send, planes, mix_home)
    mixture = (mine.astype(F32) + mate(theirs).astype(F32)).astype(BF)
    mixture = after(mixture, grad_w_sum)
    mixture = lax.psum_scatter(mixture, "exp", scatter_dimension=0, tiled=True)[0].astype(F32)
    inv_in = inv_rms(inputs)
    normed_in = inputs * inv_in
    scaled_in = grad_xa * gain_attn
    grad_tokens = (
        grad_residual
        + inv_in
        * (scaled_in - normed_in * jnp.mean(scaled_in * normed_in, axis=-1, keepdims=True))
    )[None]

    layer_out = (residual + mixture).astype(BF)[None]

    router_size = wrows * experts
    return (
        layer_out,
        grad_tokens,
        sum_attn_gain,
        small[router_size : router_size + gain_rows],
        gains[:head_rows],
        gains[head_rows : 2 * head_rows],
        sum_query,
        sum_key,
        sum_value,
        output_sum.astype(F32),
        small[:router_size].reshape(wrows, experts),
        grad_gate[None],
        grad_up[None],
        grad_down[None],
    )


def solution(mesh):
    shard = ("ctx", "exp")
    rows = P("exp", "ctx", None)
    vector, matrix, stack = P(shard), P(shard, None), P(shard, None, None)
    return jax.shard_map(
        on_device,
        mesh=mesh,
        in_specs=(rows,) * 3 + (vector,) * 4 + (matrix,) * 5 + (stack,) * 3,
        out_specs=(rows,) * 2 + (vector,) * 4 + (matrix,) * 5 + (stack,) * 3,
        check_vma=False,
    )
```

```python
import jax
import jax.numpy as jnp
import numpy as np
from jax import lax
from jax.experimental import pallas as pl
from jax.experimental.pallas import tpu as pltpu
from jax.sharding import PartitionSpec as P

D = 2048
H = 32
KVH = 4
HD = 128
TOP = 8
BLK = 256

EPSILON = 1e-06
ROPE_BASE = 1000000.0
SCALE = HD**-0.5
BF = jnp.bfloat16
F32 = jnp.float32
MASKED = -1e30
VMEM_LIMIT = 48 * 1024 * 1024
ATTN_LIMIT = 24 * 1024 * 1024
SMALL = pl.CostEstimate(flops=1000, bytes_accessed=1000, transcendentals=0)
TILE = 512


def cost(micros):
    return pl.CostEstimate(flops=int(1.1e9 * micros), bytes_accessed=1000, transcendentals=0)


def rope_tables(rows):
    half = HD // 2
    freq = np.power(ROPE_BASE, np.arange(half) * (-2.0 / HD))
    angles = np.arange(rows)[:, None] * freq[None, :]
    cos, sin = np.cos(angles), np.sin(angles)
    return (
        np.concatenate([cos, cos], axis=1).astype(np.float32),
        np.concatenate([-sin, sin], axis=1).astype(np.float32),
    )


def inv_rms(values):
    return lax.rsqrt(jnp.mean(values * values, axis=-1, keepdims=True) + EPSILON)


def nt_dot(a, b):
    return lax.dot_general(a, b, (((1,), (1,)), ((), ())), preferred_element_type=F32)


def tn_dot(a, b):
    return lax.dot_general(a, b, (((0,), (0,)), ((), ())), preferred_element_type=F32)


def mm(a, b):
    return jnp.dot(a, b, preferred_element_type=F32)


def spin(values, cos, sin):
    return values * cos + pltpu.roll(values, HD // 2, 1) * sin


def unspin(values, cos, sin):
    return values * cos - pltpu.roll(values, HD // 2, 1) * sin


def attn_forward_kernel(blocks, raw, kraw, vraw, cos_all, sin_all, cos, sin, qgain, kgain, out, keys, vals):
    head, block = pl.program_id(0), pl.program_id(1)

    @pl.when((head == 0) & (block == 0))
    def _():
        rows = kraw[...]
        keys[...] = spin(rows * inv_rms(rows) * kgain[...], cos_all[...], sin_all[...]).astype(BF)
        vals[...] = vraw[...].astype(BF)

    rows = raw[...]
    query = spin(rows * inv_rms(rows) * qgain[...], cos[...], sin[...]).astype(BF)
    for n in range(blocks):

        @pl.when(block == n)
        def _(n=n):
            span = (n + 1) * BLK
            weights = jnp.exp(nt_dot(query, keys[:span, :]) * SCALE)
            total = jnp.sum(weights, axis=-1, keepdims=True)
            probs = (weights * (1.0 / total)).astype(BF)
            out[...] = mm(probs, vals[:span, :]).astype(BF)


def attn_backward_kernel(
    blocks, raw, kraw, vraw, cos_all, sin_all, cos, sin, qgain, kgain, gout, *rest
):
    *start, gq, gk, gv, gqgain, keys, vals = rest
    head, block = pl.program_id(0), pl.program_id(1)

    @pl.when((head == 0) & (block == 0))
    def _():
        rows = kraw[...]
        keys[...] = spin(rows * inv_rms(rows) * kgain[...], cos_all[...], sin_all[...]).astype(BF)
        vals[...] = vraw[...].astype(BF)
        for ref, first in zip((gk, gv, gqgain), start or (None,) * 3):
            ref[...] = jnp.zeros_like(ref) if first is None else first[...]

    rows = raw[...]
    inverse = inv_rms(rows)
    normed = rows * inverse
    query = spin(normed * qgain[...], cos[...], sin[...]).astype(BF)
    grad_out = gout[...]

    def finish(grad_query):
        turned = unspin(grad_query, cos[...], sin[...])
        gqgain[...] += jnp.sum(turned * normed, axis=0, keepdims=True)
        scaled = turned * qgain[...]
        mean = jnp.mean(scaled * normed, axis=-1, keepdims=True)
        gq[...] = (inverse * (scaled - normed * mean)).astype(BF)

    for n in range(blocks):

        @pl.when(block == n)
        def _(n=n):
            span = (n + 1) * BLK
            seen, values = keys[:span, :], vals[:span, :]
            weights = jnp.exp(nt_dot(query, seen) * SCALE)
            total = jnp.sum(weights, axis=-1, keepdims=True)
            probs = weights * (1.0 / total)
            grad_probs = nt_dot(grad_out, values)
            delta = jnp.sum(probs * grad_probs, axis=-1, keepdims=True)
            grad_scores = (probs * (grad_probs - delta)).astype(BF)
            gv[:span, :] += tn_dot(probs.astype(BF), grad_out)
            gk[:span, :] += tn_dot(grad_scores, query) * SCALE
            finish(mm(grad_scores, seen) * SCALE)


def key_backward_kernel(count, kraw, cos, sin, kgain, *rest):
    gks, gvs, (gk_low, gv_low, gkgain) = rest[:count], rest[count : 2 * count], rest[2 * count :]
    grad_keys, grad_vals = gks[0][...], gvs[0][...]
    for n in range(1, count):
        grad_keys = grad_keys + gks[n][...]
        grad_vals = grad_vals + gvs[n][...]
    rows = kraw[...]
    inverse = inv_rms(rows)
    normed = rows * inverse
    turned = unspin(grad_keys, cos[...], sin[...])
    gkgain[...] = jnp.sum(turned * normed, axis=0, keepdims=True)
    scaled = turned * kgain[...]
    mean = jnp.mean(scaled * normed, axis=-1, keepdims=True)
    gk_low[...] = (inverse * (scaled - normed * mean)).astype(BF)
    gv_low[...] = grad_vals.astype(BF)


def attn_specs(rows, first=0):
    return [
        pl.BlockSpec((BLK, HD), lambda h, i: (i, h + first)),
        pl.BlockSpec((rows, HD), lambda h, i: (0, 0)),
        pl.BlockSpec((rows, HD), lambda h, i: (0, 0)),
        pl.BlockSpec((rows, HD), lambda h, i: (0, 0)),
        pl.BlockSpec((rows, HD), lambda h, i: (0, 0)),
        pl.BlockSpec((BLK, HD), lambda h, i: (i, 0)),
        pl.BlockSpec((BLK, HD), lambda h, i: (i, 0)),
        pl.BlockSpec((1, HD), lambda h, i: (0, 0)),
        pl.BlockSpec((1, HD), lambda h, i: (0, 0)),
    ]


def attn_forward(raw, kraw, vraw, cos, sin, qgain, kgain, first, heads):
    rows = raw.shape[0]
    blocks = rows // BLK
    return pl.pallas_call(
        lambda *refs: attn_forward_kernel(blocks, *refs),
        grid=(heads, blocks),
        in_specs=attn_specs(rows, first),
        out_specs=pl.BlockSpec((BLK, HD), lambda h, i: (i, h)),
        out_shape=jax.ShapeDtypeStruct((rows, heads * HD), BF),
        scratch_shapes=[pltpu.VMEM((rows, HD), BF), pltpu.VMEM((rows, HD), BF)],
        compiler_params=pltpu.CompilerParams(vmem_limit_bytes=ATTN_LIMIT),
        cost_estimate=cost(13),
        name="attn_fw",
    )(raw, kraw, vraw, cos, sin, cos, sin, qgain, kgain)


def attn_backward(raw, kraw, vraw, cos, sin, qgain, kgain, gout, first, heads, start):
    rows = raw.shape[0]
    blocks = rows // BLK
    return pl.pallas_call(
        lambda *refs: attn_backward_kernel(blocks, *refs),
        grid=(heads, blocks),
        in_specs=attn_specs(rows, first)
        + [pl.BlockSpec((BLK, HD), lambda h, i: (i, h + first))]
        + [pl.BlockSpec(v.shape, lambda h, i: (0, 0)) for v in start],
        out_specs=[
            pl.BlockSpec((BLK, HD), lambda h, i: (i, h)),
            pl.BlockSpec((rows, HD), lambda h, i: (0, 0)),
            pl.BlockSpec((rows, HD), lambda h, i: (0, 0)),
            pl.BlockSpec((1, HD), lambda h, i: (0, 0)),
        ],
        out_shape=[
            jax.ShapeDtypeStruct((rows, heads * HD), BF),
            jax.ShapeDtypeStruct((rows, HD), F32),
            jax.ShapeDtypeStruct((rows, HD), F32),
            jax.ShapeDtypeStruct((1, HD), F32),
        ],
        scratch_shapes=[pltpu.VMEM((rows, HD), BF), pltpu.VMEM((rows, HD), BF)],
        compiler_params=pltpu.CompilerParams(vmem_limit_bytes=ATTN_LIMIT),
        cost_estimate=cost(22),
        name="attn_bw",
    )(raw, kraw, vraw, cos, sin, cos, sin, qgain, kgain, gout, *start)


def key_backward(kraw, cos, sin, kgain, gks, gvs):
    rows = kraw.shape[0]
    return pl.pallas_call(
        lambda *refs: key_backward_kernel(len(gks), *refs),
        out_shape=[
            jax.ShapeDtypeStruct((rows, HD), BF),
            jax.ShapeDtypeStruct((rows, HD), BF),
            jax.ShapeDtypeStruct((1, HD), F32),
        ],
        compiler_params=pltpu.CompilerParams(vmem_limit_bytes=ATTN_LIMIT),
        cost_estimate=cost(2),
        name="key_bw",
    )(kraw, cos, sin, kgain, *gks, *gvs)


def call(kernel, name, out_shape, micros=0, **kw):
    return pl.pallas_call(
        kernel,
        out_shape=out_shape,
        compiler_params=pltpu.CompilerParams(vmem_limit_bytes=VMEM_LIMIT),
        cost_estimate=cost(micros) if micros else SMALL,
        name=name,
        **kw,
    )


def whole(values):
    return pl.BlockSpec(values.shape, lambda *_: (0,) * values.ndim)


def column_tile(height):
    return pl.BlockSpec((height, TILE), lambda j: (0, j))


def routing(ids, place, ne, experts, cap):
    nc, _, rows = ids.shape
    nchip = nc // 2
    block = 2 * cap

    def kernel(at, ids_ref, send, direct, chosen, spots, named):
        chip, core, ci, ei = at[0], at[1], at[2], at[3]
        number = lax.broadcasted_iota(jnp.int32, (experts, rows), 0)
        slot = lax.broadcasted_iota(jnp.int32, (cap, rows), 0).astype(F32)
        lower = (
            lax.broadcasted_iota(jnp.int32, (rows, rows), 0)
            < lax.broadcasted_iota(jnp.int32, (rows, rows), 1)
        ).astype(BF)
        for dev in range(nc):
            got = ids_ref[dev]
            hits = jnp.zeros((experts, rows), F32)
            for k in range(TOP):
                hits = hits + (got[k : k + 1, :] == number).astype(F32)
            named[dev] = hits.astype(BF)
            spots[dev] = jnp.where(hits > 0.5, mm(hits.astype(BF), lower), -1.0)

        def slots_of(dev, expert):
            line = jnp.sum(jnp.where(number == expert, spots[dev], 0.0), axis=0, keepdims=True)
            return (line == slot).astype(BF)

        for m in range(nchip):
            expert = ((chip ^ m) * 2 + core) * ne + ei
            send[m] = jnp.zeros((block, 2 * rows), BF)
            send[m, :cap, :rows] = slots_of(ci, expert)
            send[m, cap:, rows:] = slots_of(ci ^ 1, expert)
            for src in range(2):
                dev = (chip ^ m) * 2 + (core ^ src)
                taken = slots_of(dev, ci * ne + ei)
                first = (m * 2 + src) * cap
                chosen[first : first + cap, :] = nt_dot(taken, named[dev])
        for dev in range(nc):
            direct[dev] = slots_of(ci, dev * ne + ei)

    return pl.pallas_call(
        kernel,
        out_shape=[
            jax.ShapeDtypeStruct((nchip, block, 2 * rows), BF),
            jax.ShapeDtypeStruct((nc, cap, rows), BF),
            jax.ShapeDtypeStruct((nc * cap, experts), F32),
        ],
        in_specs=[pl.BlockSpec(memory_space=pltpu.SMEM), pl.BlockSpec(memory_space=pltpu.VMEM)],
        scratch_shapes=[
            pltpu.VMEM((nc, experts, rows), F32),
            pltpu.VMEM((nc, experts, rows), BF),
        ],
        compiler_params=pltpu.CompilerParams(vmem_limit_bytes=ATTN_LIMIT),
        cost_estimate=SMALL,
        name="routing",
    )(place, ids)


def select_direct(direct, planes, values):
    steps, (nc, cap, rows) = len(direct), direct[0].shape

    def kernel(at, *refs):
        tokens, out = refs[steps], refs[steps + 1]
        for n in range(steps):
            part = tokens[at[n]]
            for dev in range(nc):
                out[dev, n * cap : (n + 1) * cap, :] = mm(refs[n][dev], part).astype(BF)

    return call(
        kernel,
        "select_direct",
        micros=3,
        out_shape=jax.ShapeDtypeStruct((nc, steps * cap, D), BF),
        grid=(D // TILE,),
        in_specs=[pl.BlockSpec(memory_space=pltpu.SMEM)]
        + [whole(v) for v in direct]
        + [pl.BlockSpec((values.shape[0], rows, TILE), lambda j: (0, 0, j))],
        out_specs=pl.BlockSpec((nc, steps * cap, TILE), lambda j: (0, 0, j)),
    )(planes, *direct, values)


def select_rows(send, values, mates):
    nchip, block, _ = send.shape
    rows, count = values[0].shape[0], len(values)

    def kernel(picks, *refs):
        outs = refs[2 * count :]
        for n in range(count):
            pair = jnp.concatenate([refs[n][...], refs[count + n][...]], axis=0)
            for m in range(nchip):
                outs[m][n] = mm(picks[m], pair).astype(BF)

    return call(
        kernel,
        "select_rows",
        out_shape=[jax.ShapeDtypeStruct((count, block, D), BF)] * nchip,
        grid=(D // TILE,),
        in_specs=[whole(send)] + [column_tile(rows)] * (2 * count),
        out_specs=[pl.BlockSpec((count, block, TILE), lambda j: (0, 0, j))] * nchip,
    )(send, *values, *mates)


def combine_rows(send, home):
    nchip, block, _ = send.shape
    rows, wide = send.shape[2] // 2, home[0].shape[1]

    def kernel(picks, *refs):
        blocks, mine, theirs = refs[:nchip], refs[nchip], refs[nchip + 1]
        got = jnp.concatenate([b[...] for b in blocks], axis=0)
        chosen = jnp.concatenate([picks[m] for m in range(nchip)], axis=0)
        both = tn_dot(chosen, got)
        mine[...] = both[:rows]
        theirs[...] = both[rows:].astype(BF)

    return call(
        kernel,
        "combine_rows",
        micros=3,
        out_shape=[jax.ShapeDtypeStruct((rows, wide), F32), jax.ShapeDtypeStruct((rows, wide), BF)],
    )(send, *home)


def combine_all(send, planes, home):
    ne, (nchip, block, wide) = len(send), send[0].shape
    rows = wide // 2

    def kernel(at, *refs):
        mine, theirs = refs[-2:]
        for step in range(ne):
            blocks = refs[ne + step * nchip : ne + (step + 1) * nchip]
            got = jnp.concatenate([b[...] for b in blocks], axis=0)
            chosen = jnp.concatenate([refs[step][m] for m in range(nchip)], axis=0)
            both = tn_dot(chosen, got).astype(BF)
            mine[at[step]] = both[:rows]
            theirs[at[step]] = both[rows:]

    return call(
        kernel,
        "combine_all",
        micros=6,
        out_shape=[jax.ShapeDtypeStruct((ne, rows, D), BF)] * 2,
        grid=(D // TILE,),
        in_specs=[pl.BlockSpec(memory_space=pltpu.SMEM)]
        + [whole(v) for v in send]
        + [column_tile(block)] * (ne * nchip),
        out_specs=[pl.BlockSpec((ne, rows, TILE), lambda j: (0, 0, j))] * 2,
    )(planes, *send, *(v for blocks in home for v in blocks))


def expert_rows(rows_in, cot_in, devices, row_chosen, router, column, lane, weights):
    nchip, (both, block, _) = len(rows_in), rows_in[0].shape
    nc, cap = 2 * nchip, block // 2
    cots = 0 if both > 1 else nc
    slots, lanes, hidden_size = nchip * block, lane.shape[1], weights[0].shape[1]

    def kernel(_, *refs):
        ffn_in, cot_refs = refs[:nchip], refs[nchip : nchip + cots]
        chosen_ref, router_ref, column_ref, lane_ref, w_gate, w_up, w_down = refs[
            nchip + cots : nchip + cots + 7
        ]
        outs = refs[nchip + cots + 7 :]
        backs, mixes, kept = outs[:nchip], outs[nchip : 2 * nchip], outs[2 * nchip :]
        all_out, hidden_out, gate_out, up_out = kept
        rows = jnp.concatenate([r[0] for r in ffn_in], axis=0)
        cot = jnp.concatenate([r[0] for r in cot_refs] or [r[1] for r in ffn_in], axis=0)
        all_out[...] = rows
        gates = gates_of(mm(rows, router_ref[...]), chosen_ref[...] > 0.5, True)
        gate_vec = jnp.sum(gates * column_ref[...], axis=-1, keepdims=True)
        gate_act = mm(rows, w_gate[...])
        up_act = mm(rows, w_up[...])
        upstream = nt_dot(cot, w_down[...])
        sig = 1.0 / (1.0 + jnp.exp(-gate_act))
        silu = gate_act * sig
        hidden = (silu * up_act).astype(BF).astype(F32)
        score = jnp.sum(upstream * hidden, axis=-1, keepdims=True)
        gated = (hidden * gate_vec).astype(BF)
        hidden_out[...] = gated
        grad_hidden = upstream * gate_vec
        grad_gate = (grad_hidden * up_act * sig * (1.0 + gate_act * (1.0 - sig))).astype(BF)
        grad_up = (grad_hidden * silu).astype(BF)
        gate_out[...] = grad_gate
        up_out[...] = grad_up
        back = (nt_dot(grad_gate, w_gate[...]) + nt_dot(grad_up, w_up[...])).astype(BF)
        scores = (score * lane_ref[...]).astype(BF)
        for m in range(nchip):
            part = slice(m * block, (m + 1) * block)
            backs[m][:, :D] = back[part]
            backs[m][:, D:] = scores[part]
            mixes[m][...] = mm(gated[part], w_down[...]).astype(BF)

    narrow = jax.ShapeDtypeStruct((slots, hidden_size), BF)
    out_shape = [jax.ShapeDtypeStruct((block, D + lanes), BF)] * nchip
    out_shape += [jax.ShapeDtypeStruct((block, D), BF)] * nchip + [
        jax.ShapeDtypeStruct((slots, D), BF),
        narrow,
        narrow,
        narrow,
    ]
    fixed = [row_chosen, router, column, lane, *weights]
    outs = call(
        kernel,
        "expert_rows",
        micros=2,
        out_shape=out_shape,
        grid_spec=pltpu.PrefetchScalarGridSpec(
            num_scalar_prefetch=1,
            grid=(1,),
            in_specs=[whole(r) for r in rows_in]
            + [
                pl.BlockSpec((1, cap, D), lambda i, at, n=n: (at[n], 0, 0))
                for n in range(cots)
            ]
            + [whole(v) for v in fixed],
            out_specs=[whole(v) for v in out_shape],
        ),
    )(devices, *rows_in, *([cot_in] * cots), *fixed)
    return outs[:nchip], outs[nchip : 2 * nchip], outs[2 * nchip :]


def grad_in_weight(rows, grads):
    chunks, slots, size = len(rows), rows[0].shape[0], grads[0].shape[1]

    def kernel(*refs):
        total = tn_dot(refs[0][...], refs[chunks][...])
        for n in range(1, chunks):
            total += tn_dot(refs[n][...], refs[chunks + n][...])
        refs[2 * chunks][...] = total

    return call(
        kernel,
        "grad_in_weight",
        micros=10,
        out_shape=jax.ShapeDtypeStruct((D, size), F32),
        grid=(D // TILE,),
        in_specs=[column_tile(slots)] * chunks + [whole(v) for v in grads],
        out_specs=pl.BlockSpec((TILE, size), lambda i: (i, 0)),
    )(*rows, *grads)


def grad_down_weight(hidden, devices, cot_first, later):
    chunks = len(hidden)
    (nc, cap, _), size = cot_first.shape, hidden[0].shape[1]
    nchip = nc // 2

    def kernel(at, *refs):
        hid, early, late, out = refs[:chunks], refs[chunks], refs[chunks + 1 : -1], refs[-1]
        total = None
        for n in range(chunks):
            if n:
                rows = [r[0] for r in late[(n - 1) * nchip : n * nchip]]
            else:
                rows = [early[at[i]] for i in range(nc)]
            part = tn_dot(hid[n][...], jnp.concatenate(rows, axis=0))
            total = part if total is None else total + part
        out[...] = total

    late = [v for blocks in later for v in blocks]
    return call(
        kernel,
        "grad_down_weight",
        micros=10,
        out_shape=jax.ShapeDtypeStruct((size, D), F32),
        grid=(D // TILE,),
        in_specs=[pl.BlockSpec(memory_space=pltpu.SMEM)]
        + [whole(v) for v in hidden]
        + [pl.BlockSpec((nc, cap, TILE), lambda j: (0, 0, j))]
        + [pl.BlockSpec((1, 2 * cap, TILE), lambda j: (1, 0, j))] * len(late),
        out_specs=column_tile(size),
    )(devices, *hidden, cot_first, *late)


def project(x_all, gain, weight, wrows):
    rows, size = x_all.shape[0], weight.shape[3]

    def kernel(x, gain_ref, w, normed, raw):
        values = x[...].astype(F32)
        low = (values * inv_rms(values) * gain_ref[...]).astype(BF)
        normed[...] = low
        raw[...] = mm(low, w[:, :, :wrows, :].reshape(D, size))

    band = pl.BlockSpec((BLK, D), lambda i: (i, 0))
    return call(
        kernel,
        "project",
        micros=6,
        out_shape=[jax.ShapeDtypeStruct((rows, D), BF), jax.ShapeDtypeStruct((rows, size), F32)],
        grid=(rows // BLK,),
        in_specs=[band, whole(gain), whole(weight)],
        out_specs=[band, pl.BlockSpec((BLK, size), lambda i: (i, 0))],
    )(x_all, gain, weight)


def part_product(values, index, rows, weight, wrows, theirs, dtype):
    size = values.shape[1]
    extra = [] if theirs is None else [theirs]

    def kernel(_, part, w, *refs):
        if wrows:
            out = nt_dot(part[...], w[:, :, :wrows, :].reshape(TILE, size))
        else:
            out = mm(part[...], w[...])
        if theirs is not None:
            out = out + refs[0][...].astype(F32)
        refs[-1][...] = out.astype(dtype)

    if wrows:
        shape = (TILE // (weight.shape[1] * wrows),) + weight.shape[1:]
        weight_spec = pl.BlockSpec(shape, lambda j, at: (j, 0, 0, 0))
    else:
        weight_spec = pl.BlockSpec((size, TILE), lambda j, at: (0, j))
    column = pl.BlockSpec((rows, TILE), lambda j, at: (0, j))
    return call(
        kernel,
        "part_product",
        micros=2,
        out_shape=jax.ShapeDtypeStruct((rows, D), dtype),
        grid_spec=pltpu.PrefetchScalarGridSpec(
            num_scalar_prefetch=1,
            grid=(D // TILE,),
            in_specs=[pl.BlockSpec((rows, size), lambda j, at: (at[0], 0)), weight_spec]
            + [column] * len(extra),
            out_specs=column,
        ),
    )(index.reshape(1), values, weight, *extra)


def branch_grads(attn, pieces, devices, weight):
    (rows, size), height = attn.shape, pieces[0].shape[0]

    def kernel(at, a, w, *refs):
        parts, (to_weight, to_attn, whole_g) = refs[: len(pieces)], refs[len(pieces) :]
        for n, part in enumerate(parts):
            first = pl.multiple_of(at[n] * height, height)
            whole_g[pl.ds(first, height), :] = part[...]
        for n in range(0, D, TILE):
            to_weight[:, n : n + TILE] = tn_dot(a[...], whole_g[:, n : n + TILE]).astype(BF)
        for n in range(0, rows, BLK):
            to_attn[n : n + BLK, :] = nt_dot(whole_g[n : n + BLK, :], w[...]).astype(BF)

    outs = [jax.ShapeDtypeStruct((size, D), BF), jax.ShapeDtypeStruct((rows, size), BF)]
    return call(
        kernel,
        "branch_grads",
        micros=12,
        out_shape=outs,
        grid=(1,),
        in_specs=[pl.BlockSpec(memory_space=pltpu.SMEM)]
        + [whole(v) for v in (attn, weight, *pieces)],
        out_specs=[whole(v) for v in outs],
        scratch_shapes=[pltpu.VMEM((rows, D), BF)],
    )(devices, attn, weight, *pieces)


def projection_grads(xa, grads, nc, ne, small=None):
    rows, wrows, size = xa.shape[0], D // (nc * ne), grads.shape[1]
    more = [] if small is None else list(small)
    high = wrows + sum(v.shape[2] for v in more)

    def kernel(x, g, *refs):
        out = refs[-1]
        out[:, :, :wrows, :] = tn_dot(x[...], g[...]).astype(BF).reshape(ne, 1, wrows, size)
        if small is not None:
            out[:, :, wrows:, :] = jnp.concatenate([refs[0][...], refs[1][...]], axis=2)

    return call(
        kernel,
        "projection_grads",
        micros=2,
        out_shape=jax.ShapeDtypeStruct((ne, nc, high, size), BF),
        grid=(nc,),
        in_specs=[pl.BlockSpec((rows, ne * wrows), lambda i: (0, i)), whole(grads)]
        + [pl.BlockSpec((ne, 1) + v.shape[2:], lambda i: (0, i, 0, 0)) for v in more],
        out_specs=pl.BlockSpec((ne, 1, high, size), lambda i: (0, i, 0, 0)),
    )(xa, grads, *more)


def gates_of(logits, chosen, empty):
    top = jnp.max(jnp.where(chosen, logits, MASKED), axis=-1, keepdims=True)
    raised = jnp.where(chosen, jnp.exp(jnp.where(chosen, logits - top, 0.0)), 0.0)
    total = jnp.sum(raised, axis=-1, keepdims=True)
    return raised / (jnp.where(total > 0.0, total, 1.0) if empty else total)


def on_device(
    tokens,
    expert_ids,
    cotangent,
    attn_gain,
    ffn_gain,
    query_gain,
    key_gain,
    query_weight,
    key_weight,
    value_weight,
    output_weight,
    router_weight,
    gate_weight,
    up_weight,
    down_weight,
):
    both = ("ctx", "exp")
    nc, ne = lax.axis_size("ctx"), lax.axis_size("exp")
    ci, ei = lax.axis_index("ctx"), lax.axis_index("exp")
    chip, core = ci // 2, ci % 2
    nchip = nc // 2
    count = nc * ne
    rows = tokens.shape[1]
    seq = rows * nc
    heads = H // nc
    width = heads * HD
    share = nc // KVH
    piece = 2 * HD // share
    member = ci % share
    experts = router_weight.shape[1]
    lanes = -(-experts // 128) * 128
    cap = -(-max(2, rows * TOP * 3 // (2 * experts)) // 8) * 8
    block = 2 * cap
    slots = nchip * block
    wrows = query_weight.shape[0]
    gain_rows, head_rows = attn_gain.shape[0], query_gain.shape[0]

    def mate(values, bit=1):
        return lax.ppermute(values, "ctx", [(i, i ^ bit) for i in range(nc)])

    def peer(values, step):
        return mate(values, 2 * step) if step else values

    def along(values):
        return lax.ppermute(values, "exp", [(i, (i + 1) % ne) for i in range(ne)])

    def after(values, *others):
        return lax.optimization_barrier((values,) + others)[0]

    def place(step, other):
        return (chip ^ step) * 2 + (1 - core if other else core)

    def gather_ctx(values):
        got = [values] + [None] * (nchip - 1)
        for step in range(nchip - 1, 0, -1):
            got[step] = peer(values, step)
        return [v for part in got for v in (part, mate(part))]

    def scatter_ctx(values, weight, height, *late):
        def part(step, other, theirs, dtype):
            return part_product(values, place(step, other), rows, weight, height, theirs, dtype)

        arrived, sent = [], []
        for step in list(range(nchip - 1, 0, -1)) + [0]:
            theirs = after(mate(part(step, True, None, BF)), *late)
            mine = part(step, False, theirs, BF if step else F32)
            sent.append(mine)
            if step:
                arrived.append(peer(mine, step))
        total = mine
        for values in arrived:
            total = total + values.astype(F32)
        return total, sent

    own_tokens = tokens[0]
    x_all = lax.all_gather(own_tokens, "ctx", axis=0, tiled=True)
    w_out = lax.all_gather(after(output_weight, x_all), "exp", axis=0, tiled=True)
    total_width = width + piece
    packed = jnp.concatenate(
        [
            expert_ids[0].T.astype(BF).reshape(-1),
            attn_gain,
            ffn_gain,
            query_gain,
            key_gain,
            router_weight.reshape(-1),
        ]
    )
    more = -(-packed.shape[0] // (8 * total_width)) * 8
    packed = jnp.pad(packed, (0, more * total_width - packed.shape[0]))
    kv = jnp.concatenate(
        [key_weight.reshape(wrows, KVH, HD), value_weight.reshape(wrows, KVH, HD)], axis=2
    ).reshape(wrows, nc, piece)
    part = jnp.concatenate([query_weight.reshape(wrows, nc, width), kv], axis=2)
    part = jnp.concatenate(
        [
            part.transpose(1, 0, 2),
            jnp.broadcast_to(packed.reshape(1, more, total_width), (nc, more, total_width)),
        ],
        axis=1,
    )
    part = lax.all_to_all(part, "ctx", split_axis=0, concat_axis=0, tiled=True)

    spot = jnp.stack([chip, core, ci, ei]).astype(jnp.int32)
    index = lax.iota(jnp.int32, nc)
    devices = (chip ^ (index // 2)) * 2 + (core ^ (index % 2))
    planes = (ei - lax.iota(jnp.int32, ne)) % ne
    moving, send, direct, row_chosen = part, [], [], []
    w_in = jnp.zeros((nc, ne, wrows + more, total_width), BF)
    for step in range(ne):
        if step:
            moving = along(moving)
        w_in = lax.dynamic_update_slice(w_in, moving[:, None], (0, (ei - step) % ne, 0, 0))
        ids = moving[:, wrows:].reshape(nc, more * total_width)[:, : TOP * rows]
        ids = ids.reshape(nc, TOP, rows).astype(jnp.int32)
        if step:
            ids = after(ids, row_chosen[-1])
        else:
            own_ids = ids
        for into, values in zip(
            (send, direct, row_chosen), routing(ids, spot, ne, experts, cap)
        ):
            into.append(values)
        if step == 0:
            cot_first = select_direct(direct, jnp.zeros((1,), jnp.int32), cotangent)
            cot_first = lax.all_to_all(
                cot_first, "ctx", split_axis=0, concat_axis=0, tiled=True
            )
    table = w_in[:, :, wrows:].reshape(count, more * total_width)
    cuts = np.cumsum(
        [TOP * rows, gain_rows, gain_rows, head_rows, head_rows, wrows * experts]
    ).tolist()
    gain_attn = table[:, cuts[0] : cuts[1]].reshape(1, D).astype(F32)
    gain_ffn = table[:, cuts[1] : cuts[2]].reshape(1, D).astype(F32)
    gain_query = table[:, cuts[2] : cuts[3]].reshape(1, HD).astype(F32)
    gain_key = table[:, cuts[3] : cuts[4]].reshape(1, HD).astype(F32)
    router = table[:, cuts[4] : cuts[5]].reshape(D, experts)
    own_ids = lax.dynamic_index_in_dim(own_ids, ci, 0, keepdims=False)
    chosen_home = jnp.any(
        own_ids.T[:, :, None] == lax.iota(jnp.int32, experts)[None, None, :], axis=1
    )
    cot_all = lax.all_gather(
        after(cotangent[0], moving, w_out), "exp", axis=0, tiled=False
    )

    def to_experts(picked):
        return [peer(picked[m], m) for m in range(nchip - 1, -1, -1)][::-1]

    cos, sin = (jnp.asarray(v) for v in rope_tables(seq))
    x_all = after(x_all, cot_first, send[max(0, ne - 2)], row_chosen[max(0, ne - 2)])
    xa, raw = project(x_all, gain_attn, w_in, wrows)
    kv_own = raw[:, width:]
    kv_parts = [kv_own] + [mate(kv_own, bit) for bit in range(1, share)]
    ordered = []
    for spot in range(share):
        chosen = kv_parts[spot]
        for m in range(1, share):
            chosen = jnp.where(member == m, kv_parts[spot ^ m], chosen)
        ordered.append(chosen)
    kv_raw = jnp.concatenate(ordered, axis=1) if share > 1 else ordered[0]
    k_raw, v_raw = kv_raw[:, :HD], kv_raw[:, HD:]
    attn = attn_forward(raw, k_raw, v_raw, cos, sin, gain_query, gain_key, 0, heads)
    w_gate, w_up, w_down = gate_weight[0], up_weight[0], down_weight[0]
    cot_all = after(cot_all, attn)
    cot_moving = [
        lax.dynamic_index_in_dim(cot_all, (ei - step) % ne, 0, keepdims=False)
        for step in range(ne)
    ]
    cot_mates = [mate(v) for v in cot_moving]
    inputs = own_tokens.astype(F32)
    residual = inputs + scatter_ctx(attn, w_out, 0)[0]
    inv_res = inv_rms(residual)
    normed_res = residual * inv_res
    ffn_in = (normed_res * gain_ffn).astype(BF)

    lane = (lax.iota(jnp.int32, lanes)[None, :] == ci * ne + ei).astype(F32)
    column = lane[:, :experts]
    ffn_moving = [ffn_in]
    for _ in range(1, min(ne, 2)):
        ffn_moving.append(along(ffn_moving[-1]))
    arrived, done, mixed, back_home = [None] * ne, [], [], {}

    def pick_chunk(step, *others):
        values = [after(ffn_moving[step], *others)]
        mates = [mate(values[0])]
        if step:
            values.append(cot_moving[step])
            mates.append(cot_mates[step])
        return select_rows(send[step], values, mates)

    def run_chunk(step, *others):
        rows_in = [after(v, *others) for v in arrived[step]]
        backs, mixes, kept = expert_rows(
            rows_in, cot_first, devices, row_chosen[step], router, column, lane,
            (w_gate, w_up, w_down),
        )
        done.append((backs, kept))
        mixed.append(mixes)
        return kept[0]

    def give_back(step, *others):
        backs = [after(v, *others) for v in done[step][0]] if others else done[step][0]
        back_home[step] = to_experts(backs)

    order = list(range(1, ne)) + [0]
    picked = {0: pick_chunk(0)}
    arrived[0] = to_experts(picked[0])
    if ne > 1:
        picked[1] = pick_chunk(1, picked[0][0])
    for _ in range(2, ne):
        ffn_moving.append(along(after(ffn_moving[-1], *arrived[0])))
    tick, outs = picked[0][0], []
    for step in range(ne):
        if step + 1 < ne:
            ready = picked[step + 1]
            arrived[step + 1] = to_experts([after(v, tick, *arrived[step]) for v in ready])
            tick = ready[0]
        if step + 2 < ne:
            picked[step + 2] = pick_chunk(step + 2, tick, *arrived[step])
            tick = picked[step + 2][0]
        tick = run_chunk(step, tick)
        outs.append(tick)
    waits = arrived[-1] + outs[-2:-1]
    for step in order:
        give_back(step, *waits)
        waits = back_home[step]

    all_rows, hidden_g, act_gate, act_up = ([d[1][n] for d in done] for n in range(4))
    work = [
        lambda t: grad_in_weight(all_rows, [after(v, t) for v in act_gate]),
        lambda t: grad_in_weight(all_rows, [after(v, t) for v in act_up]),
        lambda t: grad_down_weight(
            [after(v, t) for v in hidden_g], devices, cot_first, arrived[1:]
        ),
    ]
    grads, travelling = [], None
    for at, step in enumerate(order):
        waits = (tick,) if travelling is None else (tick, travelling)
        mine, theirs = combine_rows(send[step], [after(v, *waits) for v in back_home[step]])
        back_total = mine + mate(theirs).astype(F32)
        if travelling is not None:
            back_total = back_total + travelling.astype(F32)
        if at < ne - 1:
            tick = back_total.astype(BF)
            travelling = along(tick)
            if work:
                tick = work.pop(0)(tick)
                grads.append(tick)
    grad_gate, grad_up, grad_down = grads

    gates_home = gates_of(mm(ffn_in, router), chosen_home, False)
    grad_gates = back_total[:, D : D + experts]
    grad_logits = gates_home * (
        grad_gates - jnp.sum(gates_home * grad_gates, axis=-1, keepdims=True)
    )
    grad_logits_low = grad_logits.astype(BF)
    grad_ffn_in = back_total[:, :D] + nt_dot(grad_logits_low, router)
    scaled = grad_ffn_in * gain_ffn
    grad_residual = cotangent[0].astype(F32) + inv_res * (
        scaled - normed_res * jnp.mean(scaled * normed_res, axis=-1, keepdims=True)
    )
    grad_router = tn_dot(ffn_in, grad_logits_low)
    grad_gain_ffn = jnp.sum(grad_ffn_in * normed_res, axis=0)

    pieces = gather_ctx(grad_residual.astype(BF))
    small = jnp.concatenate(
        [grad_router.reshape(nc, ne, wrows * experts), grad_gain_ffn.reshape(nc, ne, gain_rows)],
        axis=2,
    )
    ends = small.shape[2]
    extra = -(-(-(-ends // total_width) + 1) // 8) * 8
    small = jnp.pad(small, ((0, 0), (0, 0), (0, (extra - 1) * total_width - ends)))
    small = small.transpose(1, 0, 2).astype(BF).reshape(ne, nc, extra - 1, total_width)
    pieces[0] = after(pieces[0], small)
    grad_output, grad_attn = branch_grads(attn, pieces, devices, w_out)
    output_sum = lax.psum_scatter(grad_output, "exp", scatter_dimension=0, tiled=True)

    mix_home, waits = [], pieces[1:]
    for blocks in mixed[:2]:
        waits = to_experts([after(v, *waits) for v in blocks])
        mix_home.append(waits)

    grad_q_low, grad_k, grad_v, grad_gain_query = attn_backward(
        raw, k_raw, v_raw, cos, sin, gain_query, gain_key, grad_attn, 0, heads, ()
    )
    grad_q_low, grad_k, grad_v, grad_gain_query, *_ = lax.optimization_barrier(
        (grad_q_low, grad_k, grad_v, grad_gain_query) + tuple(mix_home[0])
    )
    gks = [grad_k] + [mate(grad_k, bit) for bit in range(1, share)]
    gvs = [grad_v] + [mate(grad_v, bit) for bit in range(1, share)]
    grad_k_low, grad_v_low, grad_gain_key = key_backward(k_raw, cos, sin, gain_key, gks, gvs)
    grad_gain_key = jnp.where(member == 0, grad_gain_key, 0.0)
    grad_kv = jnp.concatenate([grad_k_low, grad_v_low], axis=1)
    if share > 1:
        grad_kv = lax.dynamic_slice_in_dim(grad_kv, member * piece, piece, 1)
    grad_in = jnp.concatenate([grad_q_low, grad_kv], axis=1)
    gains = jnp.concatenate(
        [
            grad_gain_query.reshape(nc, ne, head_rows),
            grad_gain_key.reshape(nc, ne, head_rows),
        ],
        axis=2,
    )
    gains = jnp.pad(gains, ((0, 0), (0, 0), (0, total_width - 2 * head_rows)))
    gains = gains.transpose(1, 0, 2).astype(BF).reshape(ne, nc, 1, total_width)
    local = projection_grads(xa, grad_in, nc, ne, (small, gains))
    grad_in = after(grad_in, local, *mix_home[1 % ne])
    waits = [grad_in]
    for blocks in mixed[2:]:
        waits = to_experts([after(v, *waits) for v in blocks])
        mix_home.append(waits)
    local = after(local, output_sum, *mix_home[1 % ne])
    grad_w_sum = lax.psum_scatter(local, "exp", scatter_dimension=0, tiled=True)[0]
    grad_w = lax.all_to_all(
        grad_w_sum, "ctx", split_axis=0, concat_axis=0, tiled=True
    ).astype(F32)
    small = jnp.sum(grad_w[:, wrows:], axis=0)
    gains, small = small[-1], small[:-1].reshape(-1)
    grad_w = grad_w[:, :wrows]
    sum_query = grad_w[:, :, :width].transpose(1, 0, 2).reshape(wrows, H * HD)
    sum_kv = grad_w[:, :, width:].transpose(1, 0, 2).reshape(wrows, KVH, 2 * HD)
    sum_key = sum_kv[:, :, :HD].reshape(wrows, KVH * HD)
    sum_value = sum_kv[:, :, HD:].reshape(wrows, KVH * HD)
    sum_attn_gain = (
        jnp.sum(sum_query * query_weight.astype(F32), axis=1)
        + jnp.sum(sum_key * key_weight.astype(F32), axis=1)
        + jnp.sum(sum_value * value_weight.astype(F32), axis=1)
    ) / attn_gain.astype(F32)

    grad_xa, sent = scatter_ctx(grad_in, w_in, wrows, *mix_home[2 % ne])
    mix_home[0][0] = after(mix_home[0][0], *sent)
    mine, theirs = combine_all(send, planes, mix_home)
    mixture = (mine.astype(F32) + mate(theirs).astype(F32)).astype(BF)
    mixture = after(mixture, grad_w_sum)
    mixture = lax.psum_scatter(mixture, "exp", scatter_dimension=0, tiled=True)[0].astype(F32)
    inv_in = inv_rms(inputs)
    normed_in = inputs * inv_in
    scaled_in = grad_xa * gain_attn
    grad_tokens = (
        grad_residual
        + inv_in
        * (scaled_in - normed_in * jnp.mean(scaled_in * normed_in, axis=-1, keepdims=True))
    )[None]

    layer_out = (residual + mixture).astype(BF)[None]

    router_size = wrows * experts
    return (
        layer_out,
        grad_tokens,
        sum_attn_gain,
        small[router_size : router_size + gain_rows],
        gains[:head_rows],
        gains[head_rows : 2 * head_rows],
        sum_query,
        sum_key,
        sum_value,
        output_sum.astype(F32),
        small[:router_size].reshape(wrows, experts),
        grad_gate[None],
        grad_up[None],
        grad_down[None],
    )


def solution(mesh):
    shard = ("ctx", "exp")
    rows = P("exp", "ctx", None)
    vector, matrix, stack = P(shard), P(shard, None), P(shard, None, None)
    return jax.shard_map(
        on_device,
        mesh=mesh,
        in_specs=(rows,) * 3 + (vector,) * 4 + (matrix,) * 5 + (stack,) * 3,
        out_specs=(rows,) * 2 + (vector,) * 4 + (matrix,) * 5 + (stack,) * 3,
        check_vma=False,
    )
```
